32 devices in a mesh: grp: 2 (over y), tile: 4 (over z), sub: 2 (over x), lev: 2 (over core).
Axes of the slice: x: 2, y: 2, z: 4, core: 2. Of those that a mesh axis runs over, the one named last changes fastest.
Arguments:
- model_error: bfloat16 [2, 64, 2, 24, 128], P('sub', 'grp', 'lev', 'tile'), parts along dimension 1, may hold values from -6 to 6
- start_state: float32 [64, 2, 24, 128], P('grp', 'lev', 'tile'), parts along dimension 0, may hold values from -6 to 6
- covariance: bfloat16 [12, 5, 512, 512], P('tile', None, 'lev'), may hold values from -0.125 to 0.125
- offsets: int32 [12, 5], P('tile'), may hold values from 0 to 4, each once within a row
- diffusion: float32 [2, 2, 24, 128], P('sub', 'lev', 'tile'), may hold values from 0.05 to 0.24
- observed_cell: int32 [2, 4, 512], P('sub', 'tile', 'grp'), parts along dimension 2, may hold values from 0 to 1535
- observed_count: int32 [2, 4, 2], P('sub', 'tile', 'grp'), parts along dimension 2, may hold values from 128 to 256, as said below
- observed_value: float32 [2, 4, 256, 64], P('sub', 'tile', None, 'grp'), parts along dimension 3, may hold values from -6 to 6
- observed_weight: float32 [2, 4, 512], P('sub', 'tile', 'grp'), parts along dimension 2, may hold values from 0.5 to 4
Outputs:
- gradient: float32 [2, 64, 2, 24, 128], P('sub', 'grp', 'lev', 'tile'), parts along dimension 1
The draws below stay inside these ranges and needn't reach their ends.
There are 2 independent parts, one for each index of `grp`. The reference program is written for one: setup_inputs(seed, part) draws one part's arguments, and reference() takes and returns one part's arrays. A program takes and returns all parts, laid end to end along the dimension named above; an argument that names none is the same for every part. Nothing has to cross between parts.
Inputs may be any that keep to these rules, and one draw needn't show every extreme that they name: `offsets`: each row holds every number of 0 to 4 once. `observed_count`: some tile of some section has all 256 slots live.
All inputs are finite; a program needn't handle non-finite values.
Results may differ from the reference program's by a relative error of at most 0.0013.
Values may be sent and summed in bfloat16 or wider, within the bound.
No kernel may reach another device: no remote copies, remote signals or barrier semaphores. Data moves between devices by JAX's collectives and lax.ppermute only.
A program may use at most 64 MiB of HBM per device.

```python
import math
import jax
import jax.numpy as jnp
from jax import lax

COLS = 128
LEVS = 2
BROWS = 2
ORDER = 512
BAND = 5
STEPS = 4
MEMB = 32
OBS_MAX = 256
TILES = 4
NSEC = 2
NBLK = 12
ROWS_DEV = 6
NROWS = 24


def draw_observed_count(key, part):
    counts = jax.random.randint(key, (NSEC * TILES,), OBS_MAX // 2, OBS_MAX + 1)
    chosen = jax.random.randint(jax.random.fold_in(key, 7), (), 0, NSEC * TILES)
    counts = counts.at[chosen].set(OBS_MAX)
    return counts.reshape(NSEC, TILES, 1).astype(jnp.int32)


def place_ends(result, stream_key, smallest, top_value):
    longest = result.shape.index(max(result.shape))
    spots = []
    for shift in (0, 1):
        where = [jax.random.randint(jax.random.fold_in(stream_key, axis), (), 0, length) for axis, length in enumerate(result.shape)]
        where[longest] = (where[longest] + shift) % result.shape[longest]
        spots.append(tuple(where))
    return result.at[spots[0]].set(smallest).at[spots[1]].set(top_value)


def block_scale(key, extent, cuts, low, largest):
    level, own = 1.0, jax.random.fold_in(key, 6)
    for axis_at, blocks in cuts:
        heights = jnp.exp(jax.random.uniform(jax.random.fold_in(own, axis_at), (blocks,), jnp.float32, low / len(cuts), largest / len(cuts)))
        level = level * jnp.repeat(heights, extent[axis_at] // blocks).reshape([-1 if axis == axis_at else 1 for axis in range(len(extent))])
    return level


def noise(own_key, dims, width, most, pieces=(), held_as=jnp.bfloat16):
    values = width * jax.random.normal(own_key, dims, jnp.float32)
    if pieces:
        values = values * block_scale(own_key, dims, pieces, -0.22, 0.18)
    return jnp.clip(values, -most, most).astype(held_as)


def setup_inputs(seed: int = 0, part: int = 0) -> dict:
    streams_of = jax.random.split(jax.random.key(seed), 10)
    part_splits = jax.random.split(jax.random.fold_in(streams_of[9], part), 10)
    model_error = noise(part_splits[0], (NSEC, MEMB, LEVS, NROWS, COLS), 1.0, 6.0, ((0, 2), (2, 2), (3, 4)))
    start_state = noise(part_splits[1], (MEMB, LEVS, NROWS, COLS), 1.0, 6.0, ((1, 2), (2, 4)), jnp.float32)
    covariance = noise(streams_of[2], (NBLK, BAND, ORDER, ORDER), (BAND * ORDER) ** -0.5, 0.125, ((0, 4), (2, 2)))
    offsets = jax.vmap(lambda own: jax.random.permutation(own, BAND))(jax.random.split(streams_of[3], NBLK)).reshape((NBLK, BAND)).astype(jnp.int32)
    diffusion = jnp.clip(0.05 + 0.19 * jax.random.uniform(streams_of[4], (NSEC, LEVS, NROWS, COLS), jnp.float32) ** block_scale(streams_of[4], (NSEC, LEVS, NROWS, COLS), ((0, 2), (1, 2), (2, 4)), -0.2, 0.2), 0.05, 0.24)
    observed_cell = place_ends(jax.random.randint(part_splits[5], (NSEC, TILES, OBS_MAX), 0, LEVS * ROWS_DEV * COLS), jax.random.fold_in(part_splits[5], 1), 0, (LEVS * ROWS_DEV * COLS) - 1).astype(jnp.int32)
    observed_count = draw_observed_count(jax.random.fold_in(jax.random.fold_in(streams_of[9], part), 71), part)
    observed_value = noise(part_splits[7], (NSEC, TILES, OBS_MAX, MEMB), 1.0, 6.0, ((0, 2), (1, 4)), jnp.float32)
    observed_weight = jnp.clip(jnp.exp(math.log(4.0) - 2.0794415 * jax.random.uniform(part_splits[8], (NSEC, TILES, OBS_MAX), jnp.float32) ** block_scale(part_splits[8], (NSEC, TILES, OBS_MAX), ((0, 2), (1, 4)), -0.2, 0.2)), 0.5, 4.0)
    return dict(model_error=model_error, start_state=start_state, covariance=covariance, offsets=offsets, diffusion=diffusion, observed_cell=observed_cell, observed_count=observed_count, observed_value=observed_value, observed_weight=observed_weight)


def laplace_sum(value):
    widths = [(0, 0)] * (value.ndim - 2) + [(1, 1), (0, 0)]
    padded = jnp.pad(value, widths)
    return padded[..., :-2, :] + padded[..., 2:, :] + jnp.roll(value, 1, -1) + jnp.roll(value, -1, -1) - 4.0 * value


def reference(model_error, start_state, covariance, offsets, diffusion, observed_cell, observed_count, observed_value, observed_weight):
    member_count = model_error.shape[1]
    cells = LEVS * ROWS_DEV * COLS

    def to_blocks(field):
        return field.reshape(member_count, LEVS, NBLK, BROWS, COLS).transpose(0, 2, 1, 3, 4).reshape(member_count, NBLK, ORDER)

    def from_blocks(blocks):
        return blocks.reshape(member_count, NBLK, LEVS, BROWS, COLS).transpose(0, 2, 1, 3, 4).reshape(member_count, LEVS, NROWS, COLS)

    source = jnp.arange(NBLK, dtype=jnp.int32)[:, None] + offsets
    cov_wide = covariance.astype(jnp.float32)

    def forcing_of(control):
        blocks = to_blocks(control.astype(jnp.float32))
        extended = jnp.pad(blocks, ((0, 0), (2, 2), (0, 0)))
        picked = extended[:, source]
        return from_blocks(jnp.einsum('mikc,iknc->min', picked, cov_wide))

    forcing = lax.map(forcing_of, model_error)

    def to_tiles(field):
        return field.reshape(member_count, LEVS, TILES, ROWS_DEV, COLS).transpose(2, 0, 1, 3, 4).reshape(TILES, member_count, cells)

    def from_tiles(tiled):
        return tiled.reshape(TILES, member_count, LEVS, ROWS_DEV, COLS).transpose(1, 2, 0, 3, 4).reshape(member_count, LEVS, NROWS, COLS)

    field = start_state
    misfits = []
    for section in range(NSEC):
        pushed = field + forcing[section]
        for step_index in range(STEPS):
            pushed = pushed + diffusion[section] * laplace_sum(pushed)
        field = pushed
        tiled = to_tiles(field)
        observed_model = jax.vmap(lambda flat, where_at: flat[:, where_at])(tiled, observed_cell[section])
        live = jnp.arange(OBS_MAX, dtype=jnp.int32)[None, :] < observed_count[section]
        weight = jnp.where(live, observed_weight[section], 0.0)
        resid = weight[:, None, :] * (observed_model - observed_value[section].transpose(0, 2, 1))
        back = jax.vmap(lambda share, where_at: jnp.zeros((member_count, cells), jnp.float32).at[:, where_at].add(share))(resid, observed_cell[section])
        misfits.append(from_tiles(back))

    adjoint = jnp.zeros_like(start_state)
    adjoints = [None] * NSEC
    for section in range(NSEC - 1, -1, -1):
        moving = adjoint + misfits[section]
        for step_index in range(STEPS):
            moving = moving + laplace_sum(diffusion[section] * moving)
        adjoints[section] = moving
        adjoint = moving
    stacked = jnp.stack(adjoints)

    def transpose_apply(adjoint_field):
        rounded = lax.optimization_barrier(adjoint_field.astype(jnp.bfloat16))
        blocks = to_blocks(rounded.astype(jnp.float32))
        terms = jnp.einsum('min,iknc->mikc', blocks, cov_wide)
        extended = jnp.zeros((member_count, NBLK + 4, ORDER), jnp.float32).at[:, source].add(terms)
        return from_blocks(extended[:, 2:NBLK + 2])

    return model_error.astype(jnp.float32) + lax.map(transpose_apply, stacked)
```

```python
import functools

import jax
import jax.numpy as jnp
from jax import lax
from jax.experimental import pallas as pl
from jax.experimental.pallas import tpu as pltpu
from jax.sharding import PartitionSpec as P

STEPS = 4
LANES = 128
BF = jnp.bfloat16
F32 = jnp.float32
NT = (((1,), (1,)), ((), ()))


def xor_moves(block, axis, mask):
    count = lax.axis_size(axis)
    return lax.ppermute(block, axis, [(i, i ^ mask) for i in range(count)])


def shifted(block, axis, distance):
    count = lax.axis_size(axis)
    route = [(i, i + distance) for i in range(count) if 0 <= i + distance < count]
    return lax.ppermute(block, axis, route)


def loop(count, step, carry):
    if count <= 4:
        for i in range(count):
            carry = step(i, carry)
        return carry
    return lax.fori_loop(0, count, step, carry)


def halves(value):
    high = value.astype(BF).astype(F32)
    return high, value - high


def forcing_kernel(
    place, offsets, count, own, other, start, diffusion, cells, weights, values, cov_hbm,
    message, cov, control, meta, sems,
):
    blocks, band, half, order = cov.shape
    members = own.shape[1]
    rows = message_rows = diffusion.shape[0]
    copies = [pltpu.make_async_copy(cov_hbm.at[i], cov.at[i], sems.at[i]) for i in range(blocks)]
    for copy in copies:
        copy.start()
    section, level = place[1], place[2]

    def place_control(low, high):
        for b in range(control.shape[0]):
            for part, source in ((0, low), (1, high)):
                for r in range(2):
                    lane = (part * 2 + r) * LANES
                    control[b, :, lane : lane + LANES] = source[2 * b + r]

    @pl.when(level == 0)
    def _():
        place_control(own, other)

    @pl.when(level != 0)
    def _():
        place_control(other, own)

    base = rows * members
    slots = cells.shape[0] * LANES
    chunks = slots // LANES
    slot = lax.broadcasted_iota(jnp.int32, cells.shape, 0) * LANES + lax.broadcasted_iota(
        jnp.int32, cells.shape, 1
    )
    live = jnp.where(slot < count[0], weights[...], 0.0)
    weight_high, weight_low = halves(live)
    coef_high, coef_low = halves(diffusion[...])
    meta[...] = jnp.zeros_like(meta)
    cell = cells[...]
    meta[0:chunks] = (cell >> 5).astype(F32)
    meta[chunks : 2 * chunks] = (cell & 31).astype(F32)
    meta[2 * chunks : 3 * chunks] = weight_high
    meta[3 * chunks : 4 * chunks] = weight_low
    meta[4 * chunks : 4 * chunks + rows] = coef_high
    meta[4 * chunks + rows : 4 * chunks + 2 * rows] = coef_low
    for c in range(chunks):
        high, low = halves(values[:, c * LANES : (c + 1) * LANES])
        at = base + c * members
        message[at : at + members] = high.astype(BF)
        at = at + chunks * members
        message[at : at + members] = low.astype(BF)
    at = base + 2 * chunks * members
    message[at : at + meta.shape[0]] = meta[...].astype(BF)

    first = jnp.where(section == 0, 1.0, 0.0).astype(F32)
    for i in range(blocks):
        copies[i].wait()
        total = jnp.zeros((members, half), F32)
        for k in range(band):
            total += lax.dot_general(
                control[i + offsets[i, k]], cov[i, k], NT, preferred_element_type=F32
            )
        for r in range(2):
            row = 2 * i + r
            begin = start[pl.ds(row, members, stride=rows), :]
            value = total[:, r * LANES : (r + 1) * LANES] + first * begin
            message[row * members : (row + 1) * members] = value.astype(BF)


def chain_kernel(
    tiles, sections, members, rows, chunks, place, offsets, *refs
):
    pieces_count = 2 if sections > 1 else 1
    own, remote = refs[0], refs[1]
    swapped, swapped_remote = refs[2], refs[3]
    cov_hbm = refs[4]
    terms = refs[5]
    field, drive, seen, heavy, coef, result, cov, sems = refs[6:]
    blocks, band, half, order = cov.shape
    copies = [pltpu.make_async_copy(cov_hbm.at[i], cov.at[i], sems.at[i]) for i in range(blocks)]
    for copy in copies:
        copy.start()
    tile, section, level = place[0], place[1], place[2]
    per_piece = own.shape[0]
    cells = rows * LANES

    def unpack(read, sec, at_tile):
        for r in range(rows):
            drive[sec, at_tile * rows + r] = read(r * members, members).astype(F32)
        base = rows * members
        meta_at = base + 2 * chunks * members
        meta = read(meta_at, per_piece - meta_at).astype(F32)
        weight = meta[2 * chunks : 3 * chunks] + meta[3 * chunks : 4 * chunks]
        at = 4 * chunks
        spread = meta[at : at + rows] + meta[at + rows : at + 2 * rows]
        for r in range(rows):
            coef[sec, at_tile * rows + r] = jnp.broadcast_to(spread[r : r + 1], (8, LANES))
        cell = (meta[0:chunks] * 32.0 + meta[chunks : 2 * chunks]).astype(jnp.int32)
        local = cell - level * cells
        total = jnp.zeros((2 * members + 16, cells), F32)
        which = lax.broadcasted_iota(jnp.int32, (16, LANES), 0)
        for c in range(chunks):
            at = base + c * members
            value = read(at, members).astype(F32) + read(at + chunks * members, members).astype(F32)
            high, low = halves(value * weight[c : c + 1])
            weight_high = meta[2 * chunks + c : 2 * chunks + c + 1]
            weight_low = meta[3 * chunks + c : 3 * chunks + c + 1]
            tail = jnp.where(which == 0, weight_high, jnp.where(which == 1, weight_low, 0.0))
            left = jnp.concatenate([high, low, tail], axis=0).astype(BF)
            hit = lax.broadcasted_iota(jnp.int32, (cells, LANES), 0) == local[c : c + 1]
            total += lax.dot_general(
                left, jnp.where(hit, 1.0, 0.0).astype(BF), NT, preferred_element_type=F32
            )
        both = total[:members] + total[members : 2 * members]
        sums = total[2 * members : 2 * members + 1] + total[2 * members + 1 : 2 * members + 2]
        for r in range(rows):
            lanes = slice(r * LANES, (r + 1) * LANES)
            seen[sec, at_tile * rows + r] = both[:, lanes]
            heavy[sec, at_tile * rows + r] = jnp.broadcast_to(sums[:, lanes], (8, LANES))

    def reader(ref, at):
        return lambda start, size: ref[at + start : at + start + size]

    for ds in range(sections):
        for dt in range(tiles):
            if ds == 0:
                ref, at = (own, 0) if dt == 0 else (remote, (dt - 1) * per_piece)
            elif dt == 0:
                ref, at = swapped, (ds - 1) * per_piece
            else:
                ref, at = swapped_remote, ((ds - 1) * (tiles - 1) + dt - 1) * per_piece
            unpack(reader(ref, at), section ^ ds, tile ^ dt)

    all_rows = tiles * rows
    zero = jnp.zeros((members, LANES), F32)
    field[0] = zero
    field[all_rows + 1] = zero

    def times(row_value, value):
        return (row_value[None] * value.reshape(members // 8, 8, LANES)).reshape(members, LANES)

    def beside(value):
        return pltpu.roll(value, 1, 1) + pltpu.roll(value, LANES - 1, 1)

    def forward_step(sec):
        def on_tile(t, before):
            for r in range(rows):
                row = t * rows + r
                now = field[row + 1]
                around = before + field[row + 2] + beside(now) - 4.0 * now
                field[row + 1] = now + times(coef[sec, row], around)
                before = now
            return before

        loop(tiles, on_tile, zero)

    def adjoint_step(sec):
        def on_tile(t, carry):
            before, now = carry
            for r in range(rows):
                row = t * rows + r
                after_row = row + 1
                if isinstance(after_row, int):
                    after_row = min(after_row, all_rows - 1)
                else:
                    after_row = jnp.minimum(after_row, all_rows - 1)
                after = times(coef[sec, after_row], field[row + 2])
                field[row + 1] = field[row + 1] + (before + after + beside(now) - 4.0 * now)
                before, now = now, after
            return before, now

        loop(tiles, on_tile, (zero, times(coef[sec, 0], field[1])))

    def each_row(step):
        def on_tile(t, carry):
            for r in range(rows):
                step(t * rows + r)
            return carry

        loop(tiles, on_tile, 0)

    for sec in range(sections):
        def push(row):
            if sec == 0:
                field[row + 1] = drive[sec, row]
            else:
                field[row + 1] = field[row + 1] + drive[sec, row]

        each_row(push)
        for _ in range(STEPS):
            forward_step(sec)

        def observe(row):
            drive[sec, row] = times(heavy[sec, row], field[row + 1]) - seen[sec, row]

        each_row(observe)

    for sec in range(sections - 1, -1, -1):
        def pull(row):
            if sec == sections - 1:
                field[row + 1] = drive[sec, row]
            else:
                field[row + 1] = field[row + 1] + drive[sec, row]

        each_row(pull)
        for _ in range(STEPS):
            adjoint_step(sec)

        @pl.when(section == sec)
        def _():
            for r in range(rows):
                lane = (r % 2) * LANES
                result[r // 2, :, lane : lane + LANES] = field[tile * rows + r + 1].astype(BF)

    terms[...] = jnp.zeros_like(terms)
    for i in range(blocks):
        copies[i].wait()
        left = result[i]
        for k in range(band):
            part = jnp.dot(left, cov[i, k], preferred_element_type=F32)
            at = i + offsets[i, k]
            for h in range(2):
                terms[h, at] = terms[h, at] + part[:, h * half : (h + 1) * half]


def final_kernel(control, kept, got, below, above, out):
    blocks, members, half = kept.shape
    rows = control.shape[0]
    for b in range(blocks):
        total = kept[b] + got[b]
        if b < 2:
            total = total + below[b].astype(F32)
        if b >= blocks - 2:
            total = total + above[b - (blocks - 2)].astype(F32)
        for r in range(2):
            row = 2 * b + r
            value = control[row].astype(F32) + total[:, r * LANES : (r + 1) * LANES]
            out[pl.ds(row, members, stride=rows), :] = value


def body(
    model_error, start_state, covariance, offsets, diffusion, observed_cell, observed_count,
    observed_value, observed_weight,
):
    members, rows = model_error.shape[1], model_error.shape[3]
    blocks, band, half, order = covariance.shape
    tiles, sections = lax.axis_size("tile"), lax.axis_size("sub")
    slots = observed_cell.shape[2]
    chunks = slots // LANES
    level = lax.axis_index("lev")
    place = jnp.stack([lax.axis_index("tile"), lax.axis_index("sub"), level]).astype(jnp.int32)
    vmem, smem = pl.BlockSpec(memory_space=pltpu.VMEM), pl.BlockSpec(memory_space=pltpu.SMEM)
    anywhere = pl.BlockSpec(memory_space=pl.ANY)

    control = model_error[0, :, 0].transpose(1, 0, 2)
    low = shifted(control[rows - 4 :], "tile", 1)
    high = shifted(control[:4], "tile", -1)
    own = jnp.concatenate([low, control, high], axis=0)
    other = xor_moves(own, "lev", 1)

    meta_rows = -(-(4 * chunks + 2 * rows) // 16) * 16
    message_rows = rows * members + 2 * chunks * members + meta_rows
    message = pl.pallas_call(
        forcing_kernel,
        out_shape=jax.ShapeDtypeStruct((message_rows, LANES), BF),
        in_specs=[smem, smem, smem] + [vmem] * 7 + [anywhere],
        out_specs=vmem,
        scratch_shapes=[
            pltpu.VMEM(covariance.shape, BF),
            pltpu.VMEM((blocks + 4, members, order), BF),
            pltpu.VMEM((meta_rows, LANES), F32),
            pltpu.SemaphoreType.DMA((blocks,)),
        ],
        compiler_params=pltpu.CompilerParams(vmem_limit_bytes=32 * 2**20),
        name="forcing",
    )(
        place, offsets, observed_count.reshape(1), own, other,
        start_state.reshape(members * rows, LANES), diffusion[0, 0],
        observed_cell.reshape(chunks, LANES), observed_weight.reshape(chunks, LANES),
        observed_value[0, 0].T, covariance,
    )

    remote = jnp.concatenate([xor_moves(message, "tile", d) for d in range(1, tiles)], axis=0)
    swapped = jnp.concatenate([xor_moves(message, "sub", d) for d in range(1, sections)], axis=0)
    swapped_remote = jnp.concatenate(
        [xor_moves(remote, "sub", d) for d in range(1, sections)], axis=0
    )
    all_rows = tiles * rows
    terms = pl.pallas_call(
        functools.partial(chain_kernel, tiles, sections, members, rows, chunks),
        out_shape=jax.ShapeDtypeStruct((2, blocks + 4, members, half), F32),
        in_specs=[smem, smem] + [vmem] * 4 + [anywhere],
        out_specs=vmem,
        scratch_shapes=[
            pltpu.VMEM((all_rows + 2, members, LANES), F32),
            pltpu.VMEM((sections, all_rows, members, LANES), F32),
            pltpu.VMEM((sections, all_rows, members, LANES), F32),
            pltpu.VMEM((sections, all_rows, 8, LANES), F32),
            pltpu.VMEM((sections, all_rows, 8, LANES), F32),
            pltpu.VMEM((blocks, members, half), BF),
            pltpu.VMEM(covariance.shape, BF),
            pltpu.SemaphoreType.DMA((blocks,)),
        ],
        compiler_params=pltpu.CompilerParams(vmem_limit_bytes=56 * 2**20),
        name="chain",
    )(place, offsets, message, remote, swapped, swapped_remote, covariance)

    kept = lax.dynamic_index_in_dim(terms, level, 0, keepdims=False)
    given = lax.dynamic_index_in_dim(terms, 1 - level, 0, keepdims=False)
    got = xor_moves(given, "lev", 1)
    top = (kept[blocks + 2 :] + got[blocks + 2 :]).astype(BF)
    bottom = (kept[:2] + got[:2]).astype(BF)
    below = shifted(top, "tile", 1)
    above = shifted(bottom, "tile", -1)
    out = pl.pallas_call(
        final_kernel,
        out_shape=jax.ShapeDtypeStruct((members * rows, LANES), F32),
        in_specs=[vmem] * 5,
        out_specs=vmem,
        name="final",
    )(control, kept[2 : blocks + 2], got[2 : blocks + 2], below, above)
    return out.reshape(1, members, 1, rows, LANES)


def solution(mesh):
    in_specs = (
        P("sub", "grp", "lev", "tile", None),
        P("grp", "lev", "tile", None),
        P("tile", None, "lev", None),
        P("tile", None),
        P("sub", "lev", "tile", None),
        P("sub", "tile", "grp"),
        P("sub", "tile", "grp"),
        P("sub", "tile", None, "grp"),
        P("sub", "tile", "grp"),
    )
    out_specs = P("sub", "grp", "lev", "tile", None)
    return jax.shard_map(body, mesh=mesh, in_specs=in_specs, out_specs=out_specs, check_vma=False)
```

```python
import functools

import jax
import jax.numpy as jnp
from jax import lax
from jax.experimental import pallas as pl
from jax.experimental.pallas import tpu as pltpu
from jax.sharding import PartitionSpec as P

STEPS = 4
LANES = 128
BF = jnp.bfloat16
F32 = jnp.float32
NT = (((1,), (1,)), ((), ()))
MIB = 2**20


def swap(block, axis, mask=1):
    count = lax.axis_size(axis)
    return lax.ppermute(block, axis, [(i, i ^ mask) for i in range(count)])


def swap_facing(block):
    pairs = [(2 * t, 2 * (t + 1) + 1) for t in range(lax.axis_size("tile") - 1)]
    return lax.ppermute(block, ("tile", "lev"), pairs + [(b, a) for a, b in pairs])


def swap_split(block, masks):
    moves = [
        (2 * t + level, 2 * (t ^ mask) + level)
        for t in range(lax.axis_size("tile"))
        for level, mask in enumerate(masks)
    ]
    return lax.ppermute(block, ("tile", "lev"), moves)


def loop(count, step, carry):
    if count <= 4:
        for i in range(count):
            carry = step(i, carry)
        return carry
    return lax.fori_loop(0, count, step, carry)


def halves(value):
    high = value.astype(BF).astype(F32)
    return high, value - high


def stage_kernel(cov_hbm, start_hbm, diffusion_hbm, cov, start, diffusion, sems):
    copies = [
        pltpu.make_async_copy(source, target, sems.at[n])
        for n, (source, target) in enumerate(
            ((cov_hbm, cov), (start_hbm, start), (diffusion_hbm, diffusion))
        )
    ]
    for copy in copies:
        copy.start()
    for copy in copies:
        copy.wait()


def forcing_kernel(
    place, offsets, own, other, near, far, start, diffusion, cov, message, control, tail
):
    blocks, band, half, order = cov.shape
    rows, members = own.shape[0], own.shape[1]
    section, level = place[1], place[2]

    def fill(b, part, source, at):
        for r in range(2):
            lane = (part * 2 + r) * LANES
            control[b, :, lane : lane + LANES] = source[at + r]

    @pl.when(level == 0)
    def _():
        for b in range(blocks):
            fill(b + 2, 0, own, 2 * b)
            fill(b + 2, 1, other, 2 * b)
        for b in range(2):
            fill(b, 0, far, 2 * b)
            fill(b, 1, far, 4 + 2 * b)
            fill(blocks + 2 + b, 0, near, 4 + 2 * b)
            fill(blocks + 2 + b, 1, near, 2 * b)

    @pl.when(level != 0)
    def _():
        for b in range(blocks):
            fill(b + 2, 1, own, 2 * b)
            fill(b + 2, 0, other, 2 * b)
        for b in range(2):
            fill(b, 1, near, 4 + 2 * b)
            fill(b, 0, near, 2 * b)
            fill(blocks + 2 + b, 1, far, 2 * b)
            fill(blocks + 2 + b, 0, far, 4 + 2 * b)

    coef_high, coef_low = halves(diffusion[...])
    tail[...] = jnp.zeros_like(tail)
    tail[0:rows] = coef_high
    tail[rows : 2 * rows] = coef_low
    message[rows * members : rows * members + tail.shape[0]] = tail[...].astype(BF)

    first = jnp.where(section == 0, 1.0, 0.0).astype(F32)
    for i in range(blocks):
        total = jnp.zeros((members, half), F32)
        for k in range(band):
            total += lax.dot_general(
                control[i + offsets[i, k]], cov[i, k], NT, preferred_element_type=F32
            )
        for r in range(2):
            row = 2 * i + r
            begin = start[pl.ds(row, members, stride=rows), :]
            value = total[:, r * LANES : (r + 1) * LANES] + first * begin
            message[row * members : (row + 1) * members] = value.astype(BF)


def observe_kernel(tiles, sections, rows, place, local, *refs):
    split, last, split_far, last_far = refs[:4]
    seen, heavy = refs[4:]
    tile, section, level = place[0], place[1], place[2]
    height, slots = local.shape[1], local.shape[2]
    members = height - 8
    cells = rows * LANES

    def unpack(read, sec, at_tile):
        value = read[0:members, :]
        extra = read[members:height, :]
        weight = extra[1:2]
        high, low = halves(value * weight)
        weight_high, rest = halves(weight)
        weight_mid, weight_low = halves(rest)
        which = lax.broadcasted_iota(jnp.int32, (16, slots), 0)
        ends = jnp.where(
            which == 0, weight_high, jnp.where(which == 1, weight_mid, jnp.where(which == 2, weight_low, 0.0))
        )
        left = jnp.concatenate([high, low, ends], axis=0).astype(BF)
        where = extra[0:1].astype(jnp.int32) - level * cells
        hit = lax.broadcasted_iota(jnp.int32, (cells, slots), 0) == where
        total = lax.dot_general(
            left, jnp.where(hit, 1.0, 0.0).astype(BF), NT, preferred_element_type=F32
        )
        both = total[:members] + total[members : 2 * members]
        at = 2 * members
        sums = total[at : at + 1] + total[at + 1 : at + 2] + total[at + 2 : at + 3]
        for r in range(rows):
            lanes = slice(r * LANES, (r + 1) * LANES)
            seen[sec, at_tile * rows + r] = both[:, lanes]
            heavy[sec, at_tile * rows + r] = jnp.broadcast_to(sums[:, lanes], (8, LANES))

    half = sections // 2 if sections % 2 == 0 else sections
    for d in range(sections):
        unpack(local.at[d], section ^ d, tile)
        for j in range((tiles - 2) // 2):
            low_mask, high_mask = 2 * j + 1, 2 * j + 2
            mine = jnp.where(level == 0, low_mask, high_mask)
            unpack(split.at[j * sections + d], section ^ d, tile ^ mine)
            unpack(split_far.at[j * sections + d], section ^ d, tile ^ low_mask ^ high_mask ^ mine)
    for d in range(half):
        if half == sections:
            unpack(last.at[d], section ^ d, tile ^ (tiles - 1))
        else:
            unpack(last.at[d], section ^ (d + level * half), tile ^ (tiles - 1))
            unpack(last_far.at[d], section ^ (d + (1 - level) * half), tile ^ (tiles - 1))


def chain_kernel(
    tiles, sections, rows, place, offsets, own, remote, swapped, swapped_remote, seen, heavy, cov,
    keep, give, field, drive, coef, result, terms,
):
    blocks, band, half, order = cov.shape
    members = field.shape[1]
    tile, section, level = place[0], place[1], place[2]
    per_piece = own.shape[0]

    def unpack(ref, at, sec, at_tile):
        for r in range(rows):
            start = at + r * members
            drive[sec, at_tile * rows + r] = ref[start : start + members].astype(F32)
        start = at + rows * members
        tail = ref[start : start + per_piece - rows * members].astype(F32)
        spread = tail[0:rows] + tail[rows : 2 * rows]
        for r in range(rows):
            coef[sec, at_tile * rows + r] = jnp.broadcast_to(spread[r : r + 1], (8, LANES))

    for ds in range(sections):
        for dt in range(tiles):
            if ds == 0:
                ref, at = (own, 0) if dt == 0 else (remote, (dt - 1) * per_piece)
            elif dt == 0:
                ref, at = swapped, (ds - 1) * per_piece
            else:
                ref, at = swapped_remote, ((ds - 1) * (tiles - 1) + dt - 1) * per_piece
            unpack(ref, at, section ^ ds, tile ^ dt)

    all_rows = tiles * rows
    zero = jnp.zeros((members, LANES), F32)
    field[0] = zero
    field[all_rows + 1] = zero

    def times(row_value, value):
        return (row_value[None] * value.reshape(members // 8, 8, LANES)).reshape(members, LANES)

    def beside(value):
        return pltpu.roll(value, 1, 1) + pltpu.roll(value, LANES - 1, 1)

    def forward_step(sec):
        def on_tile(t, before):
            for r in range(rows):
                row = t * rows + r
                now = field[row + 1]
                around = before + field[row + 2] + beside(now) - 4.0 * now
                field[row + 1] = now + times(coef[sec, row], around)
                before = now
            return before

        loop(tiles, on_tile, zero)

    def adjoint_step(sec):
        def on_tile(t, carry):
            before, now = carry
            for r in range(rows):
                row = t * rows + r
                after_row = row + 1
                if isinstance(after_row, int):
                    after_row = min(after_row, all_rows - 1)
                else:
                    after_row = jnp.minimum(after_row, all_rows - 1)
                after = times(coef[sec, after_row], field[row + 2])
                field[row + 1] = field[row + 1] + (before + after + beside(now) - 4.0 * now)
                before, now = now, after
            return before, now

        loop(tiles, on_tile, (zero, times(coef[sec, 0], field[1])))

    def each_row(step):
        def on_tile(t, carry):
            for r in range(rows):
                step(t * rows + r)
            return carry

        loop(tiles, on_tile, 0)

    for sec in range(sections):
        def push(row):
            if sec == 0:
                field[row + 1] = drive[sec, row]
            else:
                field[row + 1] = field[row + 1] + drive[sec, row]

        each_row(push)
        for _ in range(STEPS):
            forward_step(sec)

        def observe(row):
            drive[sec, row] = times(heavy[sec, row], field[row + 1]) - seen[sec, row]

        each_row(observe)

    for sec in range(sections - 1, -1, -1):
        def pull(row):
            if sec == sections - 1:
                field[row + 1] = drive[sec, row]
            else:
                field[row + 1] = field[row + 1] + drive[sec, row]

        each_row(pull)
        for _ in range(STEPS):
            adjoint_step(sec)

        @pl.when(section == sec)
        def _():
            for r in range(rows):
                lane = (r % 2) * LANES
                result[r // 2, :, lane : lane + LANES] = field[tile * rows + r + 1].astype(BF)

    terms[...] = jnp.zeros_like(terms)
    for i in range(blocks):
        left = result[i]
        for k in range(band):
            at = i + offsets[i, k]
            terms[at] = terms[at] + jnp.dot(left, cov[i, k], preferred_element_type=F32)

    def hand_out(level_now):
        mine, theirs = level_now * half, (1 - level_now) * half
        for b in range(blocks):
            keep[b] = terms[b + 2, :, mine : mine + half]
            give[b] = terms[b + 2, :, theirs : theirs + half]
        top, bottom = blocks + 2, 0
        kept_at, given_at = (top, bottom) if level_now == 0 else (bottom, top)
        for h in range(2):
            for b in range(2):
                at = blocks + 2 * h + b
                keep[at] = terms[kept_at + b, :, h * half : (h + 1) * half]
                give[at] = terms[given_at + b, :, h * half : (h + 1) * half]

    @pl.when(level == 0)
    def _():
        hand_out(0)

    @pl.when(level != 0)
    def _():
        hand_out(1)


def final_kernel(place, control, kept, got, ghost, ghost_far, out, spare):
    rows, members = control.shape[0], control.shape[1]
    blocks, half = rows // 2, kept.shape[2]
    level = place[2]
    for b in range(blocks):
        spare[b] = kept[b] + got[b]

    def add_ghosts(level_now):
        for b in range(2):
            near = ghost[2 * level_now + b].astype(F32)
            far = ghost_far[b].astype(F32)
            below, above = (far, near) if level_now == 0 else (near, far)
            spare[b] = spare[b] + below
            spare[blocks - 2 + b] = spare[blocks - 2 + b] + above

    @pl.when(level == 0)
    def _():
        add_ghosts(0)

    @pl.when(level != 0)
    def _():
        add_ghosts(1)

    for b in range(blocks):
        for r in range(2):
            row = 2 * b + r
            value = control[row].astype(F32) + spare[b, :, r * LANES : (r + 1) * LANES]
            out[pl.ds(row, members, stride=rows), :] = value


def body(
    model_error, start_state, covariance, offsets, diffusion, observed_cell, observed_count,
    observed_value, observed_weight,
):
    members, rows = model_error.shape[1], model_error.shape[3]
    blocks, band, half, order = covariance.shape
    tiles, sections = lax.axis_size("tile"), lax.axis_size("sub")
    slots = observed_cell.shape[2]
    level = lax.axis_index("lev")
    place = jnp.stack([lax.axis_index("tile"), lax.axis_index("sub"), level]).astype(jnp.int32)
    vmem, smem = pl.BlockSpec(memory_space=pltpu.VMEM), pl.BlockSpec(memory_space=pltpu.SMEM)
    hbm = pl.BlockSpec(memory_space=pltpu.HBM)

    control = model_error[0, :, 0].transpose(1, 0, 2)
    other = swap(control, "lev")
    edge = jnp.where(level == 0, rows - 4, 0)
    near = swap_facing(
        jnp.concatenate(
            [lax.dynamic_slice_in_dim(control, edge, 4), lax.dynamic_slice_in_dim(other, edge, 4)]
        )
    )
    far = swap(near, "lev")

    live = jnp.arange(slots, dtype=jnp.int32)[None] < observed_count[0]
    local = jnp.concatenate(
        [
            observed_value[0, 0].T,
            observed_cell[0].astype(F32),
            jnp.where(live, observed_weight[0], 0.0),
            jnp.zeros((6, slots), F32),
        ]
    )[None]
    local = jnp.concatenate([local] + [swap(local, "sub", d) for d in range(1, sections)])
    split = jnp.concatenate(
        [swap_split(local, (2 * j + 1, 2 * j + 2)) for j in range((tiles - 2) // 2)]
    )
    if sections % 2 == 0:
        part = jnp.where(level == 0, local[: sections // 2], local[sections // 2 :])
    else:
        part = local
    last = swap(part, "tile", tiles - 1)
    split_far, last_far = swap(split, "lev"), swap(last, "lev")

    cov, start, spread = pl.pallas_call(
        stage_kernel,
        out_shape=[
            pltpu.VMEM(covariance.shape, BF),
            pltpu.VMEM((members * rows, LANES), F32),
            pltpu.VMEM((rows, LANES), F32),
        ],
        in_specs=[hbm] * 3,
        out_specs=[vmem] * 3,
        scratch_shapes=[pltpu.SemaphoreType.DMA((3,))],
        compiler_params=pltpu.CompilerParams(vmem_limit_bytes=8 * MIB),
        name="stage",
    )(covariance, start_state.reshape(members * rows, LANES), diffusion[0, 0])

    tail_rows = -(-2 * rows // 16) * 16
    message_rows = rows * members + tail_rows
    message = pl.pallas_call(
        forcing_kernel,
        out_shape=jax.ShapeDtypeStruct((message_rows, LANES), BF),
        in_specs=[smem, smem] + [vmem] * 7,
        out_specs=vmem,
        scratch_shapes=[
            pltpu.VMEM((blocks + 4, members, order), BF),
            pltpu.VMEM((tail_rows, LANES), F32),
        ],
        compiler_params=pltpu.CompilerParams(vmem_limit_bytes=8 * MIB),
        name="forcing",
    )(place, offsets, control, other, near, far, start, spread, cov)

    remote = jnp.concatenate([swap(message, "tile", d) for d in range(1, tiles)])
    swapped = jnp.concatenate([swap(message, "sub", d) for d in range(1, sections)])
    swapped_remote = jnp.concatenate([swap(remote, "sub", d) for d in range(1, sections)])

    all_rows = tiles * rows
    wide = (sections, all_rows, members, LANES)
    flat = (sections, all_rows, 8, LANES)
    room = 4 * (sections * all_rows * (members + 8) + all_rows * members) * LANES
    seen, heavy = pl.pallas_call(
        functools.partial(observe_kernel, tiles, sections, rows),
        out_shape=[jax.ShapeDtypeStruct(wide, F32), jax.ShapeDtypeStruct(flat, F32)],
        in_specs=[smem] + [vmem] * 5,
        out_specs=[vmem] * 2,
        compiler_params=pltpu.CompilerParams(vmem_limit_bytes=6 * MIB + 2 * room),
        cost_estimate=pl.CostEstimate(flops=10**9, bytes_accessed=4 * 10**6, transcendentals=0),
        name="observe",
    )(place, local, split, last, split_far, last_far)

    keep, give = pl.pallas_call(
        functools.partial(chain_kernel, tiles, sections, rows),
        out_shape=[jax.ShapeDtypeStruct((blocks + 4, members, half), F32)] * 2,
        in_specs=[smem, smem] + [vmem] * 7,
        out_specs=[vmem] * 2,
        scratch_shapes=[
            pltpu.VMEM((all_rows + 2, members, LANES), F32),
            pltpu.VMEM(wide, F32),
            pltpu.VMEM(flat, F32),
            pltpu.VMEM((blocks, members, half), BF),
            pltpu.VMEM((blocks + 4, members, order), F32),
        ],
        compiler_params=pltpu.CompilerParams(vmem_limit_bytes=6 * MIB + room),
        name="chain",
    )(place, offsets, message, remote, swapped, swapped_remote, seen, heavy, cov)

    got = swap(give, "lev")
    ghost = swap_facing((keep[blocks:] + got[blocks:]).astype(BF))
    ghost_far = swap(jnp.where(level == 0, ghost[2:], ghost[:2]), "lev")
    out = pl.pallas_call(
        final_kernel,
        out_shape=jax.ShapeDtypeStruct((members * rows, LANES), F32),
        in_specs=[smem] + [vmem] * 5,
        out_specs=vmem,
        scratch_shapes=[pltpu.VMEM((blocks, members, half), F32)],
        compiler_params=pltpu.CompilerParams(vmem_limit_bytes=4 * MIB),
        name="final",
    )(place, control, keep, got, ghost, ghost_far)
    return out.reshape(1, members, 1, rows, LANES)


def solution(mesh):
    in_specs = (
        P("sub", "grp", "lev", "tile", None),
        P("grp", "lev", "tile", None),
        P("tile", None, "lev", None),
        P("tile", None),
        P("sub", "lev", "tile", None),
        P("sub", "tile", "grp"),
        P("sub", "tile", "grp"),
        P("sub", "tile", None, "grp"),
        P("sub", "tile", "grp"),
    )
    out_specs = P("sub", "grp", "lev", "tile", None)
    return jax.shard_map(body, mesh=mesh, in_specs=in_specs, out_specs=out_specs, check_vma=False)
```

```python
import functools

import jax
import jax.numpy as jnp
from jax import lax
from jax.experimental import pallas as pl
from jax.experimental.pallas import tpu as pltpu
from jax.sharding import PartitionSpec as P

STEPS = 4
LANES = 128
BF = jnp.bfloat16
F32 = jnp.float32
NT = (((1,), (1,)), ((), ()))
MIB = 2**20
META = 16
WEIGHT_UNIT, COEF_UNIT, VALUE_UNIT = 8191.0, 131072.0, 5461.0
STAGE_ROOM = 56 * MIB


def swap(block, axis, mask=1):
    count = lax.axis_size(axis)
    return lax.ppermute(block, axis, [(i, i ^ mask) for i in range(count)])


def swap_facing(block):
    pairs = [(2 * t, 2 * (t + 1) + 1) for t in range(lax.axis_size("tile") - 1)]
    return lax.ppermute(block, ("tile", "lev"), pairs + [(b, a) for a, b in pairs])


def loop(count, step, carry):
    if count <= 4:
        for i in range(count):
            carry = step(i, carry)
        return carry
    return lax.fori_loop(0, count, step, carry)


def halves(value):
    high = value.astype(BF).astype(F32)
    return high, value - high


def to_i16(value):
    return jnp.round(value).astype(jnp.int32).astype(jnp.int16)


def from_i16(value):
    return value.astype(jnp.int32).astype(F32)


def stage_kernel(
    count, cov_hbm, start_hbm, diffusion_hbm, cells_hbm, weights_hbm, values_hbm,
    cov, start, packed, meta, diffusion, cells, weights, values, sems,
):
    targets = (diffusion, cells, weights, values, start, cov)
    sources = (diffusion_hbm, cells_hbm, weights_hbm, values_hbm, start_hbm, cov_hbm)
    copies = [
        pltpu.make_async_copy(source, target, sems.at[n])
        for n, (source, target) in enumerate(zip(sources, targets))
    ]
    for copy in copies:
        copy.start()
    for copy in copies[:4]:
        copy.wait()
    chunks, members, rows = cells.shape[0], values.shape[0], diffusion.shape[0]
    slot = lax.broadcasted_iota(jnp.int32, cells.shape, 0) * LANES + lax.broadcasted_iota(
        jnp.int32, cells.shape, 1
    )
    live = jnp.where(slot < count[0], weights[...], 0.0)
    meta[...] = jnp.zeros_like(meta)
    meta[0:chunks] = cells[...]
    meta[chunks : 2 * chunks] = jnp.round(live * WEIGHT_UNIT).astype(jnp.int32)
    meta[2 * chunks : 2 * chunks + rows] = jnp.round(diffusion[...] * COEF_UNIT).astype(jnp.int32)
    for c in range(chunks):
        value = values[:, c * LANES : (c + 1) * LANES]
        packed[c * members : (c + 1) * members] = to_i16(value * VALUE_UNIT)
    for copy in copies[4:]:
        copy.wait()


def forcing_kernel(
    place, offsets, own, other, near, far, start, packed, meta, cov, message, control, total
):
    blocks, band, half, order = cov.shape
    rows, members = own.shape[0], own.shape[1]
    section, level = place[1], place[2]

    def fill(b, part, source, at):
        for r in range(2):
            lane = (part * 2 + r) * LANES
            control[b, :, lane : lane + LANES] = source[at + r]

    @pl.when(level == 0)
    def _():
        for b in range(blocks):
            fill(b + 2, 0, own, 2 * b)
            fill(b + 2, 1, other, 2 * b)
        for b in range(2):
            fill(b, 0, far, 2 * b)
            fill(b, 1, far, 4 + 2 * b)
            fill(blocks + 2 + b, 0, near, 4 + 2 * b)
            fill(blocks + 2 + b, 1, near, 2 * b)

    @pl.when(level != 0)
    def _():
        for b in range(blocks):
            fill(b + 2, 1, own, 2 * b)
            fill(b + 2, 0, other, 2 * b)
        for b in range(2):
            fill(b, 1, near, 4 + 2 * b)
            fill(b, 0, near, 2 * b)
            fill(blocks + 2 + b, 1, far, 2 * b)
            fill(blocks + 2 + b, 0, far, 4 + 2 * b)

    first = jnp.where(section == 0, 1.0, 0.0).astype(F32)
    most = jnp.zeros((members, LANES), F32)
    for i in range(blocks):
        sums = jnp.zeros((members, half), F32)
        for k in range(band):
            sums += lax.dot_general(
                control[i + offsets[i, k]], cov[i, k], NT, preferred_element_type=F32
            )
        for r in range(2):
            row = 2 * i + r
            begin = start[pl.ds(row, members, stride=rows), :]
            value = sums[:, r * LANES : (r + 1) * LANES] + first * begin
            total[row] = value
            most = jnp.maximum(most, jnp.abs(value))
    peak = jnp.max(jnp.max(most, axis=0, keepdims=True), axis=1, keepdims=True)
    power = jnp.ceil(jnp.log2(jnp.maximum(peak, 1e-30) * (1.0 / 32000.0)))
    unit = jnp.broadcast_to(jnp.exp2(-power), (1, LANES))
    for row in range(rows):
        message[row * members : (row + 1) * members] = to_i16(total[row] * unit)
    at = rows * members
    message[at : at + packed.shape[0]] = packed[...]
    at = at + packed.shape[0]
    which = lax.broadcasted_iota(jnp.int32, meta.shape, 0)
    spot = meta.shape[0] - 1
    last = jnp.where(which == spot, jnp.broadcast_to(power, meta.shape).astype(jnp.int32), meta[...])
    message[at : at + meta.shape[0]] = last.astype(jnp.int16)


def unpack(ref, at, rows, members, chunks, level, drive, coef, seen, heavy):
    cells, base = rows * LANES, at + rows * members
    meta_at = base + chunks * members
    meta = from_i16(ref[meta_at : meta_at + META])
    unit = jnp.exp2(meta[META - 1 : META])
    for r in range(rows):
        start = at + r * members
        drive[r] = from_i16(ref[start : start + members]) * unit
        spread = meta[2 * chunks + r : 2 * chunks + r + 1] * (1.0 / COEF_UNIT)
        coef[r] = jnp.broadcast_to(spread, (8, LANES))
    weight = meta[chunks : 2 * chunks] * (1.0 / WEIGHT_UNIT)
    local = meta[0:chunks].astype(jnp.int32) - level * cells
    which = lax.broadcasted_iota(jnp.int32, (16, LANES), 0)
    total = jnp.zeros((2 * members + 16, cells), F32)
    for c in range(chunks):
        start = base + c * members
        value = from_i16(ref[start : start + members]) * (1.0 / VALUE_UNIT)
        high, low = halves(value * weight[c : c + 1])
        weight_high, weight_low = halves(weight[c : c + 1])
        ends = jnp.where(which == 0, weight_high, jnp.where(which == 1, weight_low, 0.0))
        left = jnp.concatenate([high, low, ends], axis=0).astype(BF)
        hit = lax.broadcasted_iota(jnp.int32, (cells, LANES), 0) == local[c : c + 1]
        total += lax.dot_general(
            left, jnp.where(hit, 1.0, 0.0).astype(BF), NT, preferred_element_type=F32
        )
    both = total[:members] + total[members : 2 * members]
    sums = total[2 * members : 2 * members + 1] + total[2 * members + 1 : 2 * members + 2]
    for r in range(rows):
        lanes = slice(r * LANES, (r + 1) * LANES)
        seen[r] = both[:, lanes]
        heavy[r] = jnp.broadcast_to(sums[:, lanes], (8, LANES))


def prepare_kernel(tiles, rows, members, chunks, place, own, remote, drive, coef, seen, heavy):
    tile, level = place[0], place[2]
    for d in range(tiles):
        ref, at = (own, 0) if d == 0 else (remote, (d - 1) * own.shape[0])
        spot = pl.ds((tile ^ d) * rows, rows)
        unpack(
            ref, at, rows, members, chunks, level,
            drive.at[spot], coef.at[spot], seen.at[spot], heavy.at[spot],
        )


def inverse(offsets, i, wanted):
    found = 0
    for k in range(offsets.shape[1]):
        found = found + jnp.where(offsets[i, k] == wanted, k, 0)
    return found


def target_sum(result, cov, offsets, target):
    blocks, band = cov.shape[0], cov.shape[1]
    total = None
    for i in range(max(0, target - band + 1), min(blocks - 1, target) + 1):
        part = jnp.dot(
            result[i], cov[i, inverse(offsets, i, target - i)], preferred_element_type=F32
        )
        total = part if total is None else total + part
    return total


def chain_kernel(
    tiles, sections, rows, chunks, place, offsets, drive_own, coef_own, seen_own, heavy_own,
    swapped, swapped_remote, cov, result, keep, give, field, drive, coef, seen, heavy,
):
    blocks, band, half, order = cov.shape
    members = field.shape[1]
    tile, section, level = place[0], place[1], place[2]
    per_piece = swapped.shape[0] // max(1, sections - 1)

    drive[section] = drive_own[...]
    coef[section] = coef_own[...]
    seen[section] = seen_own[...]
    heavy[section] = heavy_own[...]
    for ds in range(1, sections):
        for dt in range(tiles):
            if dt == 0:
                ref, at = swapped, (ds - 1) * per_piece
            else:
                ref, at = swapped_remote, ((ds - 1) * (tiles - 1) + dt - 1) * per_piece
            spot = pl.ds((tile ^ dt) * rows, rows)
            unpack(
                ref, at, rows, members, chunks, level,
                drive.at[section ^ ds, spot], coef.at[section ^ ds, spot],
                seen.at[section ^ ds, spot], heavy.at[section ^ ds, spot],
            )

    all_rows = tiles * rows
    zero = jnp.zeros((members, LANES), F32)
    field[0] = zero
    field[all_rows + 1] = zero

    def times(row_value, value):
        return (row_value[None] * value.reshape(members // 8, 8, LANES)).reshape(members, LANES)

    def beside(value):
        return pltpu.roll(value, 1, 1) + pltpu.roll(value, LANES - 1, 1)

    def forward_step(sec):
        def on_tile(t, before):
            for r in range(rows):
                row = t * rows + r
                now = field[row + 1]
                around = before + field[row + 2] + beside(now) - 4.0 * now
                field[row + 1] = now + times(coef[sec, row], around)
                before = now
            return before

        loop(tiles, on_tile, zero)

    def adjoint_step(sec):
        def on_tile(t, carry):
            before, now = carry
            for r in range(rows):
                row = t * rows + r
                after_row = row + 1
                if isinstance(after_row, int):
                    after_row = min(after_row, all_rows - 1)
                else:
                    after_row = jnp.minimum(after_row, all_rows - 1)
                after = times(coef[sec, after_row], field[row + 2])
                field[row + 1] = field[row + 1] + (before + after + beside(now) - 4.0 * now)
                before, now = now, after
            return before, now

        loop(tiles, on_tile, (zero, times(coef[sec, 0], field[1])))

    def each_row(step):
        def on_tile(t, carry):
            for r in range(rows):
                step(t * rows + r)
            return carry

        loop(tiles, on_tile, 0)

    for sec in range(sections):
        def push(row):
            if sec == 0:
                field[row + 1] = drive[sec, row]
            else:
                field[row + 1] = field[row + 1] + drive[sec, row]

        each_row(push)
        for _ in range(STEPS):
            forward_step(sec)

        def observe(row):
            drive[sec, row] = times(heavy[sec, row], field[row + 1]) - seen[sec, row]

        each_row(observe)

    for sec in range(sections - 1, -1, -1):
        def pull(row):
            if sec == sections - 1:
                field[row + 1] = drive[sec, row]
            else:
                field[row + 1] = field[row + 1] + drive[sec, row]

        each_row(pull)
        for _ in range(STEPS):
            adjoint_step(sec)

        @pl.when(section == sec)
        def _():
            for r in range(rows):
                lane = (r % 2) * LANES
                result[r // 2, :, lane : lane + LANES] = field[tile * rows + r + 1].astype(BF)

    def hand_out(kept_at, given_at):
        for target in (kept_at, kept_at + 1, given_at, given_at + 1):
            sums = target_sum(result, cov, offsets, target)
            out, first = (keep, kept_at) if target in (kept_at, kept_at + 1) else (give, given_at)
            for h in range(2):
                out[2 * h + target - first] = sums[:, h * half : (h + 1) * half]

    @pl.when(level == 0)
    def _():
        hand_out(blocks + 2, 0)

    @pl.when(level != 0)
    def _():
        hand_out(0, blocks + 2)


def core_kernel(place, offsets, result, cov, keep, give):
    blocks, band, half, order = cov.shape
    level = place[2]
    for b in range(blocks):
        sums = target_sum(result, cov, offsets, b + 2)
        low, high = sums[:, :half], sums[:, half:]
        keep[b] = jnp.where(level == 0, low, high)
        give[b] = jnp.where(level == 0, high, low)


def final_kernel(place, control, kept, got, ghost, ghost_far, out, spare):
    rows, members = control.shape[0], control.shape[1]
    blocks, half = rows // 2, kept.shape[2]
    level = place[2]
    for b in range(blocks):
        spare[b] = kept[b] + got[b]

    def add_ghosts(level_now):
        for b in range(2):
            near = ghost[2 * level_now + b].astype(F32)
            far = ghost_far[b].astype(F32)
            below, above = (far, near) if level_now == 0 else (near, far)
            spare[b] = spare[b] + below
            spare[blocks - 2 + b] = spare[blocks - 2 + b] + above

    @pl.when(level == 0)
    def _():
        add_ghosts(0)

    @pl.when(level != 0)
    def _():
        add_ghosts(1)

    for b in range(blocks):
        for r in range(2):
            row = 2 * b + r
            value = control[row].astype(F32) + spare[b, :, r * LANES : (r + 1) * LANES]
            out[pl.ds(row, members, stride=rows), :] = value


def body(
    model_error, start_state, covariance, offsets, diffusion, observed_cell, observed_count,
    observed_value, observed_weight,
):
    members, rows = model_error.shape[1], model_error.shape[3]
    blocks, band, half, order = covariance.shape
    tiles, sections = lax.axis_size("tile"), lax.axis_size("sub")
    slots = observed_cell.shape[2]
    level = lax.axis_index("lev")
    place = jnp.stack([lax.axis_index("tile"), lax.axis_index("sub"), level]).astype(jnp.int32)
    vmem, smem = pl.BlockSpec(memory_space=pltpu.VMEM), pl.BlockSpec(memory_space=pltpu.SMEM)
    hbm = pl.BlockSpec(memory_space=pltpu.HBM)

    control = model_error[0, :, 0].transpose(1, 0, 2)
    other = swap(control, "lev")
    edge = jnp.where(level == 0, rows - 4, 0)
    near = swap_facing(
        jnp.concatenate(
            [lax.dynamic_slice_in_dim(control, edge, 4), lax.dynamic_slice_in_dim(other, edge, 4)]
        )
    )
    far = swap(near, "lev")

    chunks = slots // LANES
    cov, start, packed, meta = pl.pallas_call(
        stage_kernel,
        out_shape=[
            pltpu.VMEM(covariance.shape, BF),
            pltpu.VMEM((members * rows, LANES), F32),
            pltpu.VMEM((chunks * members, LANES), jnp.int16),
            pltpu.VMEM((META, LANES), jnp.int32),
        ],
        in_specs=[smem] + [hbm] * 6,
        out_specs=[vmem] * 4,
        scratch_shapes=[
            pltpu.VMEM((rows, LANES), F32),
            pltpu.VMEM((chunks, LANES), jnp.int32),
            pltpu.VMEM((chunks, LANES), F32),
            pltpu.VMEM((members, slots), F32),
            pltpu.SemaphoreType.DMA((6,)),
        ],
        compiler_params=pltpu.CompilerParams(vmem_limit_bytes=STAGE_ROOM),
        cost_estimate=pl.CostEstimate(flops=0, bytes_accessed=8 * 10**6, transcendentals=0),
        name="stage",
    )(
        observed_count.reshape(1), covariance, start_state.reshape(members * rows, LANES),
        diffusion[0, 0], observed_cell.reshape(chunks, LANES),
        observed_weight.reshape(chunks, LANES), observed_value[0, 0].T,
    )

    message_rows = rows * members + chunks * members + META
    message = pl.pallas_call(
        forcing_kernel,
        out_shape=jax.ShapeDtypeStruct((message_rows, LANES), jnp.int16),
        in_specs=[smem, smem] + [vmem] * 8,
        out_specs=vmem,
        scratch_shapes=[
            pltpu.VMEM((blocks + 4, members, order), BF),
            pltpu.VMEM((rows, members, LANES), F32),
        ],
        compiler_params=pltpu.CompilerParams(vmem_limit_bytes=8 * MIB),
        name="forcing",
    )(place, offsets, control, other, near, far, start, packed, meta, cov)

    remote = jnp.concatenate([swap(message, "tile", d) for d in range(1, tiles)])
    swapped = jnp.concatenate([swap(message, "sub", d) for d in range(1, sections)])
    swapped_remote = jnp.concatenate([swap(remote, "sub", d) for d in range(1, sections)])

    all_rows = tiles * rows
    wide = (all_rows, members, LANES)
    flat = (all_rows, 8, LANES)
    room = 4 * all_rows * (members + 8) * LANES
    prepared = pl.pallas_call(
        functools.partial(prepare_kernel, tiles, rows, members, chunks),
        out_shape=[jax.ShapeDtypeStruct(shape, F32) for shape in (wide, flat, wide, flat)],
        in_specs=[smem] + [vmem] * 2,
        out_specs=[vmem] * 4,
        compiler_params=pltpu.CompilerParams(vmem_limit_bytes=6 * MIB + 2 * room),
        cost_estimate=pl.CostEstimate(flops=10**9, bytes_accessed=4 * 10**6, transcendentals=0),
        name="prepare",
    )(place, message, remote)

    result, keep, give = pl.pallas_call(
        functools.partial(chain_kernel, tiles, sections, rows, chunks),
        out_shape=[jax.ShapeDtypeStruct((blocks, members, half), BF)]
        + [jax.ShapeDtypeStruct((4, members, half), F32)] * 2,
        in_specs=[smem, smem] + [vmem] * 7,
        out_specs=[vmem] * 3,
        scratch_shapes=[
            pltpu.VMEM((all_rows + 2, members, LANES), F32),
            pltpu.VMEM((sections,) + wide, F32),
            pltpu.VMEM((sections,) + flat, F32),
            pltpu.VMEM((sections,) + wide, F32),
            pltpu.VMEM((sections,) + flat, F32),
        ],
        compiler_params=pltpu.CompilerParams(vmem_limit_bytes=6 * MIB + (2 * sections + 1) * room),
        name="chain",
    )(place, offsets, *prepared, swapped, swapped_remote, cov)

    ghost_got = swap(give, "lev")
    ghost = swap_facing((keep + ghost_got).astype(BF))
    kept, given = pl.pallas_call(
        core_kernel,
        out_shape=[jax.ShapeDtypeStruct((blocks, members, half), F32)] * 2,
        in_specs=[smem, smem] + [vmem] * 2,
        out_specs=[vmem] * 2,
        compiler_params=pltpu.CompilerParams(vmem_limit_bytes=4 * MIB),
        cost_estimate=pl.CostEstimate(flops=10**9, bytes_accessed=8 * 10**6, transcendentals=0),
        name="core",
    )(place, offsets, result, cov)
    got = swap(given, "lev")
    ghost_far = swap(jnp.where(level == 0, ghost[2:], ghost[:2]), "lev")
    out = pl.pallas_call(
        final_kernel,
        out_shape=jax.ShapeDtypeStruct((members * rows, LANES), F32),
        in_specs=[smem] + [vmem] * 5,
        out_specs=vmem,
        scratch_shapes=[pltpu.VMEM((blocks, members, half), F32)],
        compiler_params=pltpu.CompilerParams(vmem_limit_bytes=4 * MIB),
        name="final",
    )(place, control, kept, got, ghost, ghost_far)
    return out.reshape(1, members, 1, rows, LANES)


def solution(mesh):
    in_specs = (
        P("sub", "grp", "lev", "tile", None),
        P("grp", "lev", "tile", None),
        P("tile", None, "lev", None),
        P("tile", None),
        P("sub", "lev", "tile", None),
        P("sub", "tile", "grp"),
        P("sub", "tile", "grp"),
        P("sub", "tile", None, "grp"),
        P("sub", "tile", "grp"),
    )
    out_specs = P("sub", "grp", "lev", "tile", None)
    return jax.shard_map(body, mesh=mesh, in_specs=in_specs, out_specs=out_specs, check_vma=False)
```

```python
import functools

import jax
import jax.numpy as jnp
from jax import lax
from jax.experimental import pallas as pl
from jax.experimental.pallas import tpu as pltpu
from jax.sharding import PartitionSpec as P

STEPS = 4
LANES = 128
BF = jnp.bfloat16
F32 = jnp.float32
NT = (((1,), (1,)), ((), ()))
MIB = 2**20
META = 16
WEIGHT_UNIT, COEF_UNIT, VALUE_UNIT = 8191.0, 131072.0, 5461.0
STAGE_ROOM = 52 * MIB


def swap(block, axis, mask=1):
    count = lax.axis_size(axis)
    return lax.ppermute(block, axis, [(i, i ^ mask) for i in range(count)])


def swap_facing(block):
    pairs = [(2 * t, 2 * (t + 1) + 1) for t in range(lax.axis_size("tile") - 1)]
    return lax.ppermute(block, ("tile", "lev"), pairs + [(b, a) for a, b in pairs])


def loop(count, step, carry):
    if count <= 4:
        for i in range(count):
            carry = step(i, carry)
        return carry
    return lax.fori_loop(0, count, step, carry)


def halves(value):
    high = value.astype(BF).astype(F32)
    return high, value - high


def to_i16(value):
    return jnp.round(value).astype(jnp.int32).astype(jnp.int16)


def from_i16(value):
    return value.astype(jnp.int32).astype(F32)


def inverse(offsets, i, wanted):
    found = 0
    for k in range(offsets.shape[1]):
        found = found + jnp.where(offsets[i, k] == wanted, k, 0)
    return found


def stage_kernel(
    place, offsets, count, own_hbm, other_hbm, cov_hbm, start_hbm, diffusion_hbm, cells_hbm, weights_hbm,
    values_hbm, cov, packed, meta, sums, own, other, start, diffusion, cells, weights, values, control,
    sems,
):
    blocks, band, half, order = cov.shape
    chunks, members, rows = cells.shape[0], values.shape[0], diffusion.shape[0]
    copies = [pltpu.make_async_copy(cov_hbm.at[i], cov.at[i], sems.at[i]) for i in range(blocks)]
    small = [
        pltpu.make_async_copy(source, target, sems.at[blocks + n])
        for n, (source, target) in enumerate(
            (
                (diffusion_hbm, diffusion), (cells_hbm, cells), (weights_hbm, weights),
                (values_hbm, values), (own_hbm, own), (other_hbm, other), (start_hbm, start),
            )
        )
    ]
    for copy in small + copies:
        copy.start()

    section, level = place[1], place[2]
    for copy in small[4:6]:
        copy.wait()
    for b in range(blocks):
        for r in range(2):
            mine, theirs = own[2 * b + r], other[2 * b + r]
            for part in range(2):
                lane = (part * 2 + r) * LANES
                value = jnp.where(level == part, mine.astype(F32), theirs.astype(F32))
                control[b, :, lane : lane + LANES] = value.astype(BF)

    for copy in small[:4]:
        copy.wait()
    slot = lax.broadcasted_iota(jnp.int32, cells.shape, 0) * LANES + lax.broadcasted_iota(
        jnp.int32, cells.shape, 1
    )
    live = jnp.where(slot < count[0, 0, 0], weights[...], 0.0)
    meta[...] = jnp.zeros_like(meta)
    meta[0:chunks] = cells[...]
    meta[chunks : 2 * chunks] = jnp.round(live * WEIGHT_UNIT).astype(jnp.int32)
    for r in range(rows):
        spot = 2 * chunks + r
        meta[spot : spot + 1] = jnp.round(diffusion[r] * COEF_UNIT).astype(jnp.int32)
    for c in range(chunks):
        value = values[:, c * LANES : (c + 1) * LANES]
        packed[c * members : (c + 1) * members] = to_i16(value * VALUE_UNIT)

    small[6].wait()
    first = jnp.where(section == 0, 1.0, 0.0).astype(F32)
    for i in range(blocks):
        copies[i].wait()
        total = jnp.zeros((members, half), F32)
        for b in range(max(0, i - 2), min(blocks, i + 3)):
            total += lax.dot_general(
                control[b], cov[i, inverse(offsets, i, b + 2 - i)], NT, preferred_element_type=F32
            )
        for r in range(2):
            row = 2 * i + r
            begin = start[pl.ds(row, members, stride=rows), :]
            sums[row] = total[:, r * LANES : (r + 1) * LANES] + first * begin


def forcing_kernel(place, offsets, near, far, sums, packed, meta, cov, message, control, total):
    blocks, band, half, order = cov.shape
    rows, members = sums.shape[0], sums.shape[1]
    level = place[2]

    def fill(b, part, source, at):
        for r in range(2):
            lane = (part * 2 + r) * LANES
            control[b, :, lane : lane + LANES] = source[at + r]

    @pl.when(level == 0)
    def _():
        for b in range(2):
            fill(b, 0, far, 2 * b)
            fill(b, 1, far, 4 + 2 * b)
            fill(2 + b, 0, near, 4 + 2 * b)
            fill(2 + b, 1, near, 2 * b)

    @pl.when(level != 0)
    def _():
        for b in range(2):
            fill(b, 1, near, 4 + 2 * b)
            fill(b, 0, near, 2 * b)
            fill(2 + b, 1, far, 2 * b)
            fill(2 + b, 0, far, 4 + 2 * b)

    most = jnp.zeros((members, LANES), F32)
    for i in range(blocks):
        added = None
        for b, target in enumerate((0, 1, blocks + 2, blocks + 3)):
            if 0 <= target - i < band:
                part = lax.dot_general(
                    control[b], cov[i, inverse(offsets, i, target - i)], NT,
                    preferred_element_type=F32,
                )
                added = part if added is None else added + part
        for r in range(2):
            row = 2 * i + r
            value = sums[row]
            if added is not None:
                value = value + added[:, r * LANES : (r + 1) * LANES]
            total[row] = value
            most = jnp.maximum(most, jnp.abs(value))
    peak = jnp.max(jnp.max(most, axis=0, keepdims=True), axis=1, keepdims=True)
    power = jnp.ceil(jnp.log2(jnp.maximum(peak, 1e-30) * (1.0 / 32000.0)))
    unit = jnp.broadcast_to(jnp.exp2(-power), (1, LANES))
    for row in range(rows):
        message[row * members : (row + 1) * members] = to_i16(total[row] * unit)
    at = rows * members
    message[at : at + packed.shape[0]] = packed[...]
    at = at + packed.shape[0]
    which = lax.broadcasted_iota(jnp.int32, meta.shape, 0)
    spot = meta.shape[0] - 1
    last = jnp.where(which == spot, jnp.broadcast_to(power, meta.shape).astype(jnp.int32), meta[...])
    message[at : at + meta.shape[0]] = last.astype(jnp.int16)


def unpack(ref, at, rows, members, chunks, level, drive, coef, seen, heavy):
    cells, base = rows * LANES, at + rows * members
    meta_at = base + chunks * members
    meta = from_i16(ref[meta_at : meta_at + META])
    unit = jnp.exp2(meta[META - 1 : META])
    for r in range(rows):
        start = at + r * members
        drive[r] = from_i16(ref[start : start + members]) * unit
        spread = meta[2 * chunks + r : 2 * chunks + r + 1] * (1.0 / COEF_UNIT)
        coef[r] = jnp.broadcast_to(spread, (8, LANES))
    weight = meta[chunks : 2 * chunks] * (1.0 / WEIGHT_UNIT)
    local = meta[0:chunks].astype(jnp.int32) - level * cells
    which = lax.broadcasted_iota(jnp.int32, (16, LANES), 0)
    total = jnp.zeros((2 * members + 16, cells), F32)
    for c in range(chunks):
        start = base + c * members
        value = from_i16(ref[start : start + members]) * (1.0 / VALUE_UNIT)
        high, low = halves(value * weight[c : c + 1])
        weight_high, weight_low = halves(weight[c : c + 1])
        ends = jnp.where(which == 0, weight_high, jnp.where(which == 1, weight_low, 0.0))
        left = jnp.concatenate([high, low, ends], axis=0).astype(BF)
        hit = lax.broadcasted_iota(jnp.int32, (cells, LANES), 0) == local[c : c + 1]
        total += lax.dot_general(
            left, jnp.where(hit, 1.0, 0.0).astype(BF), NT, preferred_element_type=F32
        )
    both = total[:members] + total[members : 2 * members]
    sums = total[2 * members : 2 * members + 1] + total[2 * members + 1 : 2 * members + 2]
    for r in range(rows):
        lanes = slice(r * LANES, (r + 1) * LANES)
        seen[r] = both[:, lanes]
        heavy[r] = jnp.broadcast_to(sums[:, lanes], (8, LANES))


def prepare_kernel(sizes, masks, place, *refs):
    rows, members, chunks = sizes
    pieces, outs = refs[: len(masks)], refs[len(masks) :]
    for mask, (ref, at) in zip(masks, [(ref, 0) for ref in pieces]):
        tile = place[0] ^ mask if len(masks) > 2 else (place[0] & 1) ^ mask
        spot = pl.ds(tile * rows, rows)
        unpack(ref, at, rows, members, chunks, place[2], *[out.at[spot] for out in outs])


def target_sum(result, cov, offsets, target):
    blocks, band = cov.shape[0], cov.shape[1]
    total = None
    for i in range(max(0, target - band + 1), min(blocks - 1, target) + 1):
        part = jnp.dot(
            result[i], cov[i, inverse(offsets, i, target - i)], preferred_element_type=F32
        )
        total = part if total is None else total + part
    return total


def chain_kernel(
    tiles, sections, sizes, place, offsets, *refs
):
    rows, members, chunks = sizes
    own_section, early, late, (cov, result, keep, give) = refs[:4], refs[4:8], refs[8], refs[9:13]
    whole = refs[14:18]
    field, (drive, coef, seen, heavy) = refs[13], whole
    blocks, band, half, order = cov.shape
    tile, section, level = place[0], place[1], place[2]
    per_piece = rows * members + chunks * members + META
    pair = early[0].shape[0] // max(1, sections - 1)

    for target, source in zip(whole, own_section):
        target[section] = source[...]
    for ds in range(1, sections):
        base = pl.ds((tile & ~1) * rows, pair)
        for target, source in zip(whole, early):
            target[section ^ ds, base] = source[(ds - 1) * pair : ds * pair]
        for dt in range(2, tiles):
            at = ((ds - 1) * (tiles - 2) + dt - 2) * per_piece
            spot = pl.ds((tile ^ dt) * rows, rows)
            unpack(
                late, at, rows, members, chunks, level,
                *[target.at[section ^ ds, spot] for target in whole],
            )

    all_rows = tiles * rows
    zero = jnp.zeros((members, LANES), F32)
    field[0] = zero
    field[all_rows + 1] = zero

    def times(row_value, value):
        return (row_value[None] * value.reshape(members // 8, 8, LANES)).reshape(members, LANES)

    def beside(value):
        return pltpu.roll(value, 1, 1) + pltpu.roll(value, LANES - 1, 1)

    def forward_step(sec):
        def on_tile(t, before):
            for r in range(rows):
                row = t * rows + r
                now = field[row + 1]
                around = before + field[row + 2] + beside(now) - 4.0 * now
                field[row + 1] = now + times(coef[sec, row], around)
                before = now
            return before

        loop(tiles, on_tile, zero)

    def adjoint_step(sec):
        def on_tile(t, carry):
            before, now = carry
            for r in range(rows):
                row = t * rows + r
                after_row = row + 1
                if isinstance(after_row, int):
                    after_row = min(after_row, all_rows - 1)
                else:
                    after_row = jnp.minimum(after_row, all_rows - 1)
                after = times(coef[sec, after_row], field[row + 2])
                field[row + 1] = field[row + 1] + (before + after + beside(now) - 4.0 * now)
                before, now = now, after
            return before, now

        loop(tiles, on_tile, (zero, times(coef[sec, 0], field[1])))

    def each_row(step):
        def on_tile(t, carry):
            for r in range(rows):
                step(t * rows + r)
            return carry

        loop(tiles, on_tile, 0)

    for sec in range(sections):
        def push(row):
            if sec == 0:
                field[row + 1] = drive[sec, row]
            else:
                field[row + 1] = field[row + 1] + drive[sec, row]

        each_row(push)
        for _ in range(STEPS):
            forward_step(sec)

        def observe(row):
            drive[sec, row] = times(heavy[sec, row], field[row + 1]) - seen[sec, row]

        each_row(observe)

    for sec in range(sections - 1, -1, -1):
        def pull(row):
            if sec == sections - 1:
                field[row + 1] = drive[sec, row]
            else:
                field[row + 1] = field[row + 1] + drive[sec, row]

        each_row(pull)
        for _ in range(STEPS):
            adjoint_step(sec)

        @pl.when(section == sec)
        def _():
            for r in range(rows):
                lane = (r % 2) * LANES
                result[r // 2, :, lane : lane + LANES] = field[tile * rows + r + 1].astype(BF)

    def hand_out(kept_at, given_at):
        for target in (kept_at, kept_at + 1, given_at, given_at + 1):
            sums = target_sum(result, cov, offsets, target)
            out, first = (keep, kept_at) if target in (kept_at, kept_at + 1) else (give, given_at)
            for h in range(2):
                out[2 * h + target - first] = sums[:, h * half : (h + 1) * half]

    @pl.when(level == 0)
    def _():
        hand_out(blocks + 2, 0)

    @pl.when(level != 0)
    def _():
        hand_out(0, blocks + 2)


def core_kernel(place, offsets, result, cov, keep, give):
    blocks, band, half, order = cov.shape
    level = place[2]
    for b in range(blocks):
        sums = target_sum(result, cov, offsets, b + 2)
        low, high = sums[:, :half], sums[:, half:]
        keep[b] = jnp.where(level == 0, low, high)
        give[b] = jnp.where(level == 0, high, low)


def final_kernel(place, control, kept, got, ghost, ghost_far, out, spare):
    rows, members = control.shape[0], control.shape[1]
    blocks, half = rows // 2, kept.shape[2]
    level = place[2]
    for b in range(blocks):
        spare[b] = kept[b] + got[b]

    def add_ghosts(level_now):
        for b in range(2):
            near = ghost[2 * level_now + b].astype(F32)
            far = ghost_far[b].astype(F32)
            below, above = (far, near) if level_now == 0 else (near, far)
            spare[b] = spare[b] + below
            spare[blocks - 2 + b] = spare[blocks - 2 + b] + above

    @pl.when(level == 0)
    def _():
        add_ghosts(0)

    @pl.when(level != 0)
    def _():
        add_ghosts(1)

    for b in range(blocks):
        for r in range(2):
            row = 2 * b + r
            value = control[row].astype(F32) + spare[b, :, r * LANES : (r + 1) * LANES]
            out[pl.ds(row, members, stride=rows), :] = value


def body(
    model_error, start_state, covariance, offsets, diffusion, observed_cell, observed_count,
    observed_value, observed_weight,
):
    members, rows = model_error.shape[1], model_error.shape[3]
    blocks, band, half, order = covariance.shape
    tiles, sections = lax.axis_size("tile"), lax.axis_size("sub")
    slots = observed_cell.shape[2]
    level = lax.axis_index("lev")
    place = jnp.stack([lax.axis_index("tile"), lax.axis_index("sub"), level]).astype(jnp.int32)
    vmem, smem = pl.BlockSpec(memory_space=pltpu.VMEM), pl.BlockSpec(memory_space=pltpu.SMEM)
    hbm = pl.BlockSpec(memory_space=pltpu.HBM)

    control = model_error[0, :, 0].transpose(1, 0, 2)
    other = swap(control, "lev")
    edge = jnp.where(level == 0, rows - 4, 0)
    near = swap_facing(
        jnp.concatenate(
            [lax.dynamic_slice_in_dim(control, edge, 4), lax.dynamic_slice_in_dim(other, edge, 4)]
        )
    )

    chunks = slots // LANES
    sizes = (rows, members, chunks)
    cov, packed, meta, sums = pl.pallas_call(
        stage_kernel,
        out_shape=[
            pltpu.VMEM(covariance.shape, BF),
            pltpu.VMEM((chunks * members, LANES), jnp.int16),
            pltpu.VMEM((META, LANES), jnp.int32),
            pltpu.VMEM((rows, members, LANES), F32),
        ],
        in_specs=[smem] * 3 + [hbm] * 8,
        out_specs=[vmem] * 4,
        scratch_shapes=[
            pltpu.VMEM(control.shape, BF),
            pltpu.VMEM(control.shape, BF),
            pltpu.VMEM((members * rows, LANES), F32),
            pltpu.VMEM((rows, 1, LANES), F32),
            pltpu.VMEM((chunks, LANES), jnp.int32),
            pltpu.VMEM((chunks, LANES), F32),
            pltpu.VMEM((members, slots), F32),
            pltpu.VMEM((blocks, members, order), BF),
            pltpu.SemaphoreType.DMA((blocks + 7,)),
        ],
        compiler_params=pltpu.CompilerParams(vmem_limit_bytes=STAGE_ROOM),
        cost_estimate=pl.CostEstimate(flops=0, bytes_accessed=8 * 10**6, transcendentals=0),
        name="stage",
    )(
        place, offsets, observed_count, control, other, covariance,
        start_state.reshape(members * rows, LANES), diffusion.reshape(rows, 1, LANES),
        observed_cell.reshape(chunks, LANES), observed_weight.reshape(chunks, LANES),
        observed_value[0, 0].T,
    )

    near, sums = lax.optimization_barrier((near, sums))
    far = swap(near, "lev")
    message_rows = rows * members + chunks * members + META
    message = pl.pallas_call(
        forcing_kernel,
        out_shape=jax.ShapeDtypeStruct((message_rows, LANES), jnp.int16),
        in_specs=[smem, smem] + [vmem] * 6,
        out_specs=vmem,
        scratch_shapes=[
            pltpu.VMEM((4, members, order), BF),
            pltpu.VMEM((rows, members, LANES), F32),
        ],
        compiler_params=pltpu.CompilerParams(vmem_limit_bytes=8 * MIB),
        name="forcing",
    )(place, offsets, near, far, sums, packed, meta, cov)

    pieces = [message] + [swap(message, "tile", d) for d in range(1, tiles)]
    early = [swap(piece, "sub", d) for d in range(1, sections) for piece in pieces[:2]]
    held, early = lax.optimization_barrier((pieces[2:], early))
    late = jnp.concatenate(
        [swap(jnp.concatenate(held), "sub", d) for d in range(1, sections)]
    )

    all_rows = tiles * rows
    wide = (all_rows, members, LANES)
    flat = (all_rows, 8, LANES)
    room = 4 * all_rows * (members + 8) * LANES

    def prepare(arrays, masks, count):
        height = count * rows
        return pl.pallas_call(
            functools.partial(prepare_kernel, sizes, masks),
            out_shape=[
                jax.ShapeDtypeStruct((height, size, LANES), F32) for size in (members, 8) * 2
            ],
            in_specs=[smem] + [vmem] * len(arrays),
            out_specs=[vmem] * 4,
            compiler_params=pltpu.CompilerParams(vmem_limit_bytes=6 * MIB + 2 * room),
            cost_estimate=pl.CostEstimate(
                flops=10**8 * count, bytes_accessed=10**6 * count, transcendentals=0
            ),
            name="prepare",
        )(place, *arrays)

    own_section = prepare(pieces, tuple(range(tiles)), tiles)
    others = [prepare(early[2 * d : 2 * d + 2], (0, 1), 2) for d in range(sections - 1)]
    early_section = [jnp.concatenate(group) for group in zip(*others)]

    result, keep, give = pl.pallas_call(
        functools.partial(chain_kernel, tiles, sections, sizes),
        out_shape=[jax.ShapeDtypeStruct((blocks, members, half), BF)]
        + [jax.ShapeDtypeStruct((4, members, half), F32)] * 2,
        in_specs=[smem, smem] + [vmem] * 10,
        out_specs=[vmem] * 3,
        scratch_shapes=[
            pltpu.VMEM((all_rows + 2, members, LANES), F32),
            pltpu.VMEM((sections,) + wide, F32),
            pltpu.VMEM((sections,) + flat, F32),
            pltpu.VMEM((sections,) + wide, F32),
            pltpu.VMEM((sections,) + flat, F32),
        ],
        compiler_params=pltpu.CompilerParams(vmem_limit_bytes=6 * MIB + (3 * sections + 3) * room),
        name="chain",
    )(place, offsets, *own_section, *early_section, late, cov)

    ghost_got = swap(give, "lev")
    ghost = swap_facing((keep + ghost_got).astype(BF))
    kept, given = pl.pallas_call(
        core_kernel,
        out_shape=[jax.ShapeDtypeStruct((blocks, members, half), F32)] * 2,
        in_specs=[smem, smem] + [vmem] * 2,
        out_specs=[vmem] * 2,
        compiler_params=pltpu.CompilerParams(vmem_limit_bytes=4 * MIB),
        cost_estimate=pl.CostEstimate(flops=10**9, bytes_accessed=8 * 10**6, transcendentals=0),
        name="core",
    )(place, offsets, result, cov)
    got = swap(given, "lev")
    ghost_far = swap(jnp.where(level == 0, ghost[2:], ghost[:2]), "lev")
    out = pl.pallas_call(
        final_kernel,
        out_shape=jax.ShapeDtypeStruct((members * rows, LANES), F32),
        in_specs=[smem] + [vmem] * 5,
        out_specs=vmem,
        scratch_shapes=[pltpu.VMEM((blocks, members, half), F32)],
        compiler_params=pltpu.CompilerParams(vmem_limit_bytes=4 * MIB),
        name="final",
    )(place, control, kept, got, ghost, ghost_far)
    return out.reshape(1, members, 1, rows, LANES)


def solution(mesh):
    in_specs = (
        P("sub", "grp", "lev", "tile", None),
        P("grp", "lev", "tile", None),
        P("tile", None, "lev", None),
        P("tile", None),
        P("sub", "lev", "tile", None),
        P("sub", "tile", "grp"),
        P("sub", "tile", "grp"),
        P("sub", "tile", None, "grp"),
        P("sub", "tile", "grp"),
    )
    out_specs = P("sub", "grp", "lev", "tile", None)
    return jax.shard_map(body, mesh=mesh, in_specs=in_specs, out_specs=out_specs, check_vma=False)
```

```python
import functools

import jax
import jax.numpy as jnp
from jax import lax
from jax.experimental import pallas as pl
from jax.experimental.pallas import tpu as pltpu
from jax.sharding import PartitionSpec as P

STEPS = 4
LANES = 128
BF = jnp.bfloat16
F32 = jnp.float32
NT = (((1,), (1,)), ((), ()))
MIB = 2**20
META = 16
WEIGHT_UNIT, COEF_UNIT, VALUE_UNIT = 8191.0, 131072.0, 5461.0
STAGE_ROOM = 52 * MIB


def swap(block, axis, mask=1):
    count = lax.axis_size(axis)
    return lax.ppermute(block, axis, [(i, i ^ mask) for i in range(count)])


def swap_facing(block):
    pairs = [(2 * t, 2 * (t + 1) + 1) for t in range(lax.axis_size("tile") - 1)]
    return lax.ppermute(block, ("tile", "lev"), pairs + [(b, a) for a, b in pairs])


def loop(count, step, carry):
    if count <= 4:
        for i in range(count):
            carry = step(i, carry)
        return carry
    return lax.fori_loop(0, count, step, carry)


def halves(value):
    high = value.astype(BF).astype(F32)
    return high, value - high


def to_i16(value):
    return jnp.round(value).astype(jnp.int32).astype(jnp.int16)


def from_i16(value):
    return value.astype(jnp.int32).astype(F32)


def inverse(offsets, i, wanted):
    found = 0
    for k in range(offsets.shape[1]):
        found = found + jnp.where(offsets[i, k] == wanted, k, 0)
    return found


def stage_kernel(
    count, offsets_hbm, own_hbm, other_hbm, cov_hbm, start_hbm, diffusion_hbm, cells_hbm,
    weights_hbm, values_hbm, offsets, cov, packed, meta, sums, own, other, start, diffusion, cells, weights, values, control,
    sems,
):
    blocks, band, half, order = cov.shape
    chunks, members, rows = cells.shape[0], values.shape[0], diffusion.shape[0]
    copies = [pltpu.make_async_copy(cov_hbm.at[i], cov.at[i], sems.at[i]) for i in range(blocks)]
    small = [
        pltpu.make_async_copy(source, target, sems.at[blocks + n])
        for n, (source, target) in enumerate(
            (
                (diffusion_hbm, diffusion), (cells_hbm, cells), (weights_hbm, weights),
                (values_hbm, values), (own_hbm, own), (other_hbm, other), (start_hbm, start),
                (offsets_hbm, offsets),
            )
        )
    ]
    for copy in small + copies:
        copy.start()

    section, level = lax.axis_index("sub"), lax.axis_index("lev")
    for copy in small[4:6]:
        copy.wait()
    for b in range(blocks):
        for r in range(2):
            mine, theirs = own[2 * b + r], other[2 * b + r]
            for part in range(2):
                lane = (part * 2 + r) * LANES
                value = jnp.where(level == part, mine.astype(F32), theirs.astype(F32))
                control[b, :, lane : lane + LANES] = value.astype(BF)

    for copy in small[:4]:
        copy.wait()
    slot = lax.broadcasted_iota(jnp.int32, cells.shape, 0) * LANES + lax.broadcasted_iota(
        jnp.int32, cells.shape, 1
    )
    live = jnp.where(slot < count[0, 0, 0], weights[...], 0.0)
    meta[...] = jnp.zeros_like(meta)
    meta[0:chunks] = cells[...]
    meta[chunks : 2 * chunks] = jnp.round(live * WEIGHT_UNIT).astype(jnp.int32)
    for r in range(rows):
        spot = 2 * chunks + r
        meta[spot : spot + 1] = jnp.round(diffusion[r] * COEF_UNIT).astype(jnp.int32)
    for c in range(chunks):
        value = values[:, c * LANES : (c + 1) * LANES]
        packed[c * members : (c + 1) * members] = to_i16(value * VALUE_UNIT)

    small[6].wait()
    small[7].wait()
    first = jnp.where(section == 0, 1.0, 0.0).astype(F32)
    for i in range(blocks):
        copies[i].wait()
        total = jnp.zeros((members, half), F32)
        for b in range(max(0, i - 2), min(blocks, i + 3)):
            total += lax.dot_general(
                control[b], cov[i, inverse(offsets, i, b + 2 - i)], NT, preferred_element_type=F32
            )
        for r in range(2):
            row = 2 * i + r
            begin = start[pl.ds(row, members, stride=rows), :]
            sums[row] = total[:, r * LANES : (r + 1) * LANES] + first * begin


def forcing_kernel(offsets, near, far, sums, packed, meta, cov, message, control, total):
    blocks, band, half, order = cov.shape
    rows, members = sums.shape[0], sums.shape[1]
    level = lax.axis_index("lev")

    def fill(b, part, source, at):
        for r in range(2):
            lane = (part * 2 + r) * LANES
            control[b, :, lane : lane + LANES] = source[at + r]

    @pl.when(level == 0)
    def _():
        for b in range(2):
            fill(b, 0, far, 2 * b)
            fill(b, 1, far, 4 + 2 * b)
            fill(2 + b, 0, near, 4 + 2 * b)
            fill(2 + b, 1, near, 2 * b)

    @pl.when(level != 0)
    def _():
        for b in range(2):
            fill(b, 1, near, 4 + 2 * b)
            fill(b, 0, near, 2 * b)
            fill(2 + b, 1, far, 2 * b)
            fill(2 + b, 0, far, 4 + 2 * b)

    most = jnp.zeros((members, LANES), F32)
    for i in range(blocks):
        added = None
        for b, target in enumerate((0, 1, blocks + 2, blocks + 3)):
            if 0 <= target - i < band:
                part = lax.dot_general(
                    control[b], cov[i, inverse(offsets, i, target - i)], NT,
                    preferred_element_type=F32,
                )
                added = part if added is None else added + part
        for r in range(2):
            row = 2 * i + r
            value = sums[row]
            if added is not None:
                value = value + added[:, r * LANES : (r + 1) * LANES]
            total[row] = value
            most = jnp.maximum(most, jnp.abs(value))
    peak = jnp.max(jnp.max(most, axis=0, keepdims=True), axis=1, keepdims=True)
    power = jnp.ceil(jnp.log2(jnp.maximum(peak, 1e-30) * (1.0 / 32000.0)))
    unit = jnp.broadcast_to(jnp.exp2(-power), (1, LANES))
    for row in range(rows):
        message[row * members : (row + 1) * members] = to_i16(total[row] * unit)
    at = rows * members
    message[at : at + packed.shape[0]] = packed[...]
    at = at + packed.shape[0]
    which = lax.broadcasted_iota(jnp.int32, meta.shape, 0)
    spot = meta.shape[0] - 1
    last = jnp.where(which == spot, jnp.broadcast_to(power, meta.shape).astype(jnp.int32), meta[...])
    message[at : at + meta.shape[0]] = last.astype(jnp.int16)


def unpack(ref, at, rows, members, chunks, level, drive, coef, seen, heavy):
    cells, base = rows * LANES, at + rows * members
    meta_at = base + chunks * members
    meta = from_i16(ref[meta_at : meta_at + META])
    unit = jnp.exp2(meta[META - 1 : META])
    for r in range(rows):
        start = at + r * members
        drive[r] = from_i16(ref[start : start + members]) * unit
        spread = meta[2 * chunks + r : 2 * chunks + r + 1] * (1.0 / COEF_UNIT)
        coef[r] = jnp.broadcast_to(spread, (8, LANES))
    weight = meta[chunks : 2 * chunks] * (1.0 / WEIGHT_UNIT)
    local = meta[0:chunks].astype(jnp.int32) - level * cells
    which = lax.broadcasted_iota(jnp.int32, (16, LANES), 0)
    total = jnp.zeros((2 * members + 16, cells), F32)
    for c in range(chunks):
        start = base + c * members
        value = from_i16(ref[start : start + members]) * (1.0 / VALUE_UNIT)
        high, low = halves(value * weight[c : c + 1])
        weight_high, weight_low = halves(weight[c : c + 1])
        ends = jnp.where(which == 0, weight_high, jnp.where(which == 1, weight_low, 0.0))
        left = jnp.concatenate([high, low, ends], axis=0).astype(BF)
        hit = lax.broadcasted_iota(jnp.int32, (cells, LANES), 0) == local[c : c + 1]
        total += lax.dot_general(
            left, jnp.where(hit, 1.0, 0.0).astype(BF), NT, preferred_element_type=F32
        )
    both = total[:members] + total[members : 2 * members]
    sums = total[2 * members : 2 * members + 1] + total[2 * members + 1 : 2 * members + 2]
    for r in range(rows):
        lanes = slice(r * LANES, (r + 1) * LANES)
        seen[r] = both[:, lanes]
        heavy[r] = jnp.broadcast_to(sums[:, lanes], (8, LANES))


def prepare_kernel(sizes, masks, *refs):
    rows, members, chunks = sizes
    pieces, outs = refs[: len(masks)], refs[len(masks) :]
    here, level = lax.axis_index("tile"), lax.axis_index("lev")
    for mask, (ref, at) in zip(masks, [(ref, 0) for ref in pieces]):
        tile = here ^ mask if len(masks) > 2 else (here & 1) ^ mask
        spot = pl.ds(tile * rows, rows)
        unpack(ref, at, rows, members, chunks, level, *[out.at[spot] for out in outs])


def target_sum(result, cov, offsets, target):
    blocks, band = cov.shape[0], cov.shape[1]
    total = None
    for i in range(max(0, target - band + 1), min(blocks - 1, target) + 1):
        part = jnp.dot(
            result[i], cov[i, inverse(offsets, i, target - i)], preferred_element_type=F32
        )
        total = part if total is None else total + part
    return total


def chain_kernel(
    tiles, sections, sizes, offsets, *refs
):
    rows, members, chunks = sizes
    own_section, early, late, (cov, result, keep, give) = refs[:4], refs[4:8], refs[8], refs[9:13]
    whole = refs[14:18]
    field, (drive, coef, seen, heavy) = refs[13], whole
    blocks, band, half, order = cov.shape
    tile, section, level = (lax.axis_index(axis) for axis in ("tile", "sub", "lev"))
    per_piece = rows * members + chunks * members + META
    pair = early[0].shape[0] // max(1, sections - 1)

    for target, source in zip(whole, own_section):
        target[section] = source[...]
    for ds in range(1, sections):
        base = pl.ds((tile & ~1) * rows, pair)
        for target, source in zip(whole, early):
            target[section ^ ds, base] = source[(ds - 1) * pair : ds * pair]
        for dt in range(2, tiles):
            at = ((ds - 1) * (tiles - 2) + dt - 2) * per_piece
            spot = pl.ds((tile ^ dt) * rows, rows)
            unpack(
                late, at, rows, members, chunks, level,
                *[target.at[section ^ ds, spot] for target in whole],
            )

    all_rows = tiles * rows
    zero = jnp.zeros((members, LANES), F32)
    field[0] = zero
    field[all_rows + 1] = zero

    def times(row_value, value):
        return (row_value[None] * value.reshape(members // 8, 8, LANES)).reshape(members, LANES)

    def beside(value):
        return pltpu.roll(value, 1, 1) + pltpu.roll(value, LANES - 1, 1)

    def forward_step(sec):
        def on_tile(t, before):
            for r in range(rows):
                row = t * rows + r
                now = field[row + 1]
                around = before + field[row + 2] + beside(now) - 4.0 * now
                field[row + 1] = now + times(coef[sec, row], around)
                before = now
            return before

        loop(tiles, on_tile, zero)

    def adjoint_step(sec):
        def on_tile(t, carry):
            before, now = carry
            for r in range(rows):
                row = t * rows + r
                after_row = row + 1
                if isinstance(after_row, int):
                    after_row = min(after_row, all_rows - 1)
                else:
                    after_row = jnp.minimum(after_row, all_rows - 1)
                after = times(coef[sec, after_row], field[row + 2])
                field[row + 1] = field[row + 1] + (before + after + beside(now) - 4.0 * now)
                before, now = now, after
            return before, now

        loop(tiles, on_tile, (zero, times(coef[sec, 0], field[1])))

    def each_row(step):
        def on_tile(t, carry):
            for r in range(rows):
                step(t * rows + r)
            return carry

        loop(tiles, on_tile, 0)

    for sec in range(sections):
        def push(row):
            if sec == 0:
                field[row + 1] = drive[sec, row]
            else:
                field[row + 1] = field[row + 1] + drive[sec, row]

        each_row(push)
        for _ in range(STEPS):
            forward_step(sec)

        def observe(row):
            drive[sec, row] = times(heavy[sec, row], field[row + 1]) - seen[sec, row]

        each_row(observe)

    for sec in range(sections - 1, -1, -1):
        def pull(row):
            if sec == sections - 1:
                field[row + 1] = drive[sec, row]
            else:
                field[row + 1] = field[row + 1] + drive[sec, row]

        each_row(pull)
        for _ in range(STEPS):
            adjoint_step(sec)

        @pl.when(section == sec)
        def _():
            for r in range(rows):
                lane = (r % 2) * LANES
                result[r // 2, :, lane : lane + LANES] = field[tile * rows + r + 1].astype(BF)

    def hand_out(kept_at, given_at):
        for target in (kept_at, kept_at + 1, given_at, given_at + 1):
            sums = target_sum(result, cov, offsets, target)
            out, first = (keep, kept_at) if target in (kept_at, kept_at + 1) else (give, given_at)
            for h in range(2):
                out[2 * h + target - first] = sums[:, h * half : (h + 1) * half]

    @pl.when(level == 0)
    def _():
        hand_out(blocks + 2, 0)

    @pl.when(level != 0)
    def _():
        hand_out(0, blocks + 2)


def core_kernel(offsets, result, cov, keep, give):
    blocks, band, half, order = cov.shape
    level = lax.axis_index("lev")
    for b in range(blocks):
        sums = target_sum(result, cov, offsets, b + 2)
        low, high = sums[:, :half], sums[:, half:]
        keep[b] = jnp.where(level == 0, low, high)
        give[b] = jnp.where(level == 0, high, low)


def final_kernel(control, kept, got, ghost, ghost_far, out, spare):
    rows, members = control.shape[0], control.shape[1]
    blocks, half = rows // 2, kept.shape[2]
    level = lax.axis_index("lev")
    for b in range(blocks):
        spare[b] = kept[b] + got[b]

    def add_ghosts(level_now):
        for b in range(2):
            near = ghost[2 * level_now + b].astype(F32)
            far = ghost_far[b].astype(F32)
            below, above = (far, near) if level_now == 0 else (near, far)
            spare[b] = spare[b] + below
            spare[blocks - 2 + b] = spare[blocks - 2 + b] + above

    @pl.when(level == 0)
    def _():
        add_ghosts(0)

    @pl.when(level != 0)
    def _():
        add_ghosts(1)

    for b in range(blocks):
        for r in range(2):
            row = 2 * b + r
            value = control[row].astype(F32) + spare[b, :, r * LANES : (r + 1) * LANES]
            out[pl.ds(row, members, stride=rows), :] = value


def body(
    model_error, start_state, covariance, offsets, diffusion, observed_cell, observed_count,
    observed_value, observed_weight,
):
    members, rows = model_error.shape[1], model_error.shape[3]
    blocks, band, half, order = covariance.shape
    tiles, sections = lax.axis_size("tile"), lax.axis_size("sub")
    slots = observed_cell.shape[2]
    level = lax.axis_index("lev")
    vmem, smem = pl.BlockSpec(memory_space=pltpu.VMEM), pl.BlockSpec(memory_space=pltpu.SMEM)
    hbm = pl.BlockSpec(memory_space=pltpu.HBM)

    control = model_error[0, :, 0].transpose(1, 0, 2)
    other = swap(control, "lev")
    edge = jnp.where(level == 0, rows - 4, 0)
    near = swap_facing(
        jnp.concatenate(
            [lax.dynamic_slice_in_dim(control, edge, 4), lax.dynamic_slice_in_dim(other, edge, 4)]
        )
    )

    chunks = slots // LANES
    sizes = (rows, members, chunks)
    offsets, cov, packed, meta, sums = pl.pallas_call(
        stage_kernel,
        out_shape=[
            pltpu.SMEM(offsets.shape, jnp.int32),
            pltpu.VMEM(covariance.shape, BF),
            pltpu.VMEM((chunks * members, LANES), jnp.int16),
            pltpu.VMEM((META, LANES), jnp.int32),
            pltpu.VMEM((rows, members, LANES), F32),
        ],
        in_specs=[smem] + [hbm] * 9,
        out_specs=[smem] + [vmem] * 4,
        scratch_shapes=[
            pltpu.VMEM(control.shape, BF),
            pltpu.VMEM(control.shape, BF),
            pltpu.VMEM((members * rows, LANES), F32),
            pltpu.VMEM((rows, 1, LANES), F32),
            pltpu.VMEM((chunks, LANES), jnp.int32),
            pltpu.VMEM((chunks, LANES), F32),
            pltpu.VMEM((members, slots), F32),
            pltpu.VMEM((blocks, members, order), BF),
            pltpu.SemaphoreType.DMA((blocks + 8,)),
        ],
        compiler_params=pltpu.CompilerParams(vmem_limit_bytes=STAGE_ROOM),
        cost_estimate=pl.CostEstimate(flops=0, bytes_accessed=8 * 10**6, transcendentals=0),
        name="stage",
    )(
        observed_count, offsets, control, other, covariance,
        start_state.reshape(members * rows, LANES), diffusion.reshape(rows, 1, LANES),
        observed_cell.reshape(chunks, LANES), observed_weight.reshape(chunks, LANES),
        observed_value[0, 0].T,
    )

    near, sums = lax.optimization_barrier((near, sums))
    far = swap(near, "lev")
    message_rows = rows * members + chunks * members + META
    message = pl.pallas_call(
        forcing_kernel,
        out_shape=jax.ShapeDtypeStruct((message_rows, LANES), jnp.int16),
        in_specs=[smem] + [vmem] * 6,
        out_specs=vmem,
        scratch_shapes=[
            pltpu.VMEM((4, members, order), BF),
            pltpu.VMEM((rows, members, LANES), F32),
        ],
        compiler_params=pltpu.CompilerParams(vmem_limit_bytes=8 * MIB),
        name="forcing",
    )(offsets, near, far, sums, packed, meta, cov)

    pieces = [message] + [swap(message, "tile", d) for d in range(1, tiles)]
    early = [swap(piece, "sub", d) for d in range(1, sections) for piece in pieces[:2]]
    held, early = lax.optimization_barrier((pieces[2:], early))
    late = jnp.concatenate(
        [swap(jnp.concatenate(held), "sub", d) for d in range(1, sections)]
    )

    all_rows = tiles * rows
    wide = (all_rows, members, LANES)
    flat = (all_rows, 8, LANES)
    room = 4 * all_rows * (members + 8) * LANES

    def prepare(arrays, masks, count):
        height = count * rows
        return pl.pallas_call(
            functools.partial(prepare_kernel, sizes, masks),
            out_shape=[
                jax.ShapeDtypeStruct((height, size, LANES), F32) for size in (members, 8) * 2
            ],
            in_specs=[vmem] * len(arrays),
            out_specs=[vmem] * 4,
            compiler_params=pltpu.CompilerParams(vmem_limit_bytes=6 * MIB + 2 * room),
            cost_estimate=pl.CostEstimate(
                flops=10**8 * count, bytes_accessed=10**6 * count, transcendentals=0
            ),
            name="prepare",
        )(*arrays)

    own_section = prepare(pieces, tuple(range(tiles)), tiles)
    others = [prepare(early[2 * d : 2 * d + 2], (0, 1), 2) for d in range(sections - 1)]
    early_section = [jnp.concatenate(group) for group in zip(*others)]

    result, keep, give = pl.pallas_call(
        functools.partial(chain_kernel, tiles, sections, sizes),
        out_shape=[jax.ShapeDtypeStruct((blocks, members, half), BF)]
        + [jax.ShapeDtypeStruct((4, members, half), F32)] * 2,
        in_specs=[smem] + [vmem] * 10,
        out_specs=[vmem] * 3,
        scratch_shapes=[
            pltpu.VMEM((all_rows + 2, members, LANES), F32),
            pltpu.VMEM((sections,) + wide, F32),
            pltpu.VMEM((sections,) + flat, F32),
            pltpu.VMEM((sections,) + wide, F32),
            pltpu.VMEM((sections,) + flat, F32),
        ],
        compiler_params=pltpu.CompilerParams(vmem_limit_bytes=6 * MIB + (3 * sections + 3) * room),
        name="chain",
    )(offsets, *own_section, *early_section, late, cov)

    ghost_got = swap(give, "lev")
    ghost = swap_facing((keep + ghost_got).astype(BF))
    kept, given = pl.pallas_call(
        core_kernel,
        out_shape=[jax.ShapeDtypeStruct((blocks, members, half), F32)] * 2,
        in_specs=[smem] + [vmem] * 2,
        out_specs=[vmem] * 2,
        compiler_params=pltpu.CompilerParams(vmem_limit_bytes=4 * MIB),
        cost_estimate=pl.CostEstimate(flops=10**9, bytes_accessed=8 * 10**6, transcendentals=0),
        name="core",
    )(offsets, result, cov)
    got = swap(given, "lev")
    ghost_far = swap(jnp.where(level == 0, ghost[2:], ghost[:2]), "lev")
    out = pl.pallas_call(
        final_kernel,
        out_shape=jax.ShapeDtypeStruct((members * rows, LANES), F32),
        in_specs=[vmem] * 5,
        out_specs=vmem,
        scratch_shapes=[pltpu.VMEM((blocks, members, half), F32)],
        compiler_params=pltpu.CompilerParams(vmem_limit_bytes=4 * MIB),
        name="final",
    )(control, kept, got, ghost, ghost_far)
    return out.reshape(1, members, 1, rows, LANES)


def solution(mesh):
    in_specs = (
        P("sub", "grp", "lev", "tile", None),
        P("grp", "lev", "tile", None),
        P("tile", None, "lev", None),
        P("tile", None),
        P("sub", "lev", "tile", None),
        P("sub", "tile", "grp"),
        P("sub", "tile", "grp"),
        P("sub", "tile", None, "grp"),
        P("sub", "tile", "grp"),
    )
    out_specs = P("sub", "grp", "lev", "tile", None)
    return jax.shard_map(body, mesh=mesh, in_specs=in_specs, out_specs=out_specs, check_vma=False)
```

```python
import functools

import jax
import jax.numpy as jnp
from jax import lax
from jax.experimental import pallas as pl
from jax.experimental.pallas import tpu as pltpu
from jax.sharding import PartitionSpec as P

STEPS = 4
LANES = 128
BF = jnp.bfloat16
F32 = jnp.float32
NT = (((1,), (1,)), ((), ()))
MIB = 2**20
META = 16
WEIGHT_UNIT, COEF_UNIT, VALUE_UNIT = 8191.0, 131072.0, 5461.0
STAGE_ROOM = 52 * MIB


def swap(block, axis, mask=1):
    count = lax.axis_size(axis)
    return lax.ppermute(block, axis, [(i, i ^ mask) for i in range(count)])


def swap_facing(block):
    pairs = [(2 * t, 2 * (t + 1) + 1) for t in range(lax.axis_size("tile") - 1)]
    return lax.ppermute(block, ("tile", "lev"), pairs + [(b, a) for a, b in pairs])


def loop(count, step, carry):
    if count <= 4:
        for i in range(count):
            carry = step(i, carry)
        return carry
    return lax.fori_loop(0, count, step, carry)


def halves(value):
    high = value.astype(BF).astype(F32)
    return high, value - high


def to_i16(value):
    return jnp.round(value).astype(jnp.int32).astype(jnp.int16)


def from_i16(value):
    return value.astype(jnp.int32).astype(F32)


def inverse(offsets, i, wanted):
    found = 0
    for k in range(offsets.shape[1]):
        found = found + jnp.where(offsets[i, k] == wanted, k, 0)
    return found


def stage_kernel(
    count, offsets_hbm, own_hbm, other_hbm, cov_hbm, start_hbm, diffusion_hbm, cells_hbm,
    weights_hbm, values_hbm, offsets, cov, packed, meta, sums, own, other, start, diffusion, cells, weights, values, control,
    sems,
):
    blocks, band, half, order = cov.shape
    chunks, members, rows = cells.shape[0], values.shape[0], diffusion.shape[0]
    copies = [pltpu.make_async_copy(cov_hbm.at[i], cov.at[i], sems.at[i]) for i in range(blocks)]
    small = [
        pltpu.make_async_copy(source, target, sems.at[blocks + n])
        for n, (source, target) in enumerate(
            (
                (diffusion_hbm, diffusion), (cells_hbm, cells), (weights_hbm, weights),
                (values_hbm, values), (own_hbm, own), (other_hbm, other), (start_hbm, start),
                (offsets_hbm, offsets),
            )
        )
    ]
    for copy in small + copies:
        copy.start()

    section, level = lax.axis_index("sub"), lax.axis_index("lev")
    for copy in small[4:6]:
        copy.wait()
    for b in range(blocks):
        for r in range(2):
            mine, theirs = own[2 * b + r], other[2 * b + r]
            for part in range(2):
                lane = (part * 2 + r) * LANES
                value = jnp.where(level == part, mine.astype(F32), theirs.astype(F32))
                control[b, :, lane : lane + LANES] = value.astype(BF)

    for copy in small[:4]:
        copy.wait()
    slot = lax.broadcasted_iota(jnp.int32, cells.shape, 0) * LANES + lax.broadcasted_iota(
        jnp.int32, cells.shape, 1
    )
    live = jnp.where(slot < count[0, 0, 0], weights[...], 0.0)
    meta[...] = jnp.zeros_like(meta)
    meta[0:chunks] = cells[...]
    meta[chunks : 2 * chunks] = jnp.round(live * WEIGHT_UNIT).astype(jnp.int32)
    for r in range(rows):
        spot = 2 * chunks + r
        meta[spot : spot + 1] = jnp.round(diffusion[r] * COEF_UNIT).astype(jnp.int32)
    for c in range(chunks):
        value = values[:, c * LANES : (c + 1) * LANES]
        packed[c * members : (c + 1) * members] = to_i16(value * VALUE_UNIT)

    small[6].wait()
    small[7].wait()
    first = jnp.where(section == 0, 1.0, 0.0).astype(F32)
    for i in range(blocks):
        copies[i].wait()
        total = jnp.zeros((members, half), F32)
        for b in range(max(0, i - 2), min(blocks, i + 3)):
            total += lax.dot_general(
                control[b], cov[i, inverse(offsets, i, b + 2 - i)], NT, preferred_element_type=F32
            )
        for r in range(2):
            row = 2 * i + r
            begin = start[pl.ds(row, members, stride=rows), :]
            sums[row] = total[:, r * LANES : (r + 1) * LANES] + first * begin


def forcing_kernel(offsets, near, far, sums, packed, meta, cov, message, control, total):
    blocks, band, half, order = cov.shape
    rows, members = sums.shape[0], sums.shape[1]
    level = lax.axis_index("lev")

    def fill(b, part, source, at):
        for r in range(2):
            lane = (part * 2 + r) * LANES
            control[b, :, lane : lane + LANES] = source[at + r]

    @pl.when(level == 0)
    def _():
        for b in range(2):
            fill(b, 0, far, 2 * b)
            fill(b, 1, far, 4 + 2 * b)
            fill(2 + b, 0, near, 4 + 2 * b)
            fill(2 + b, 1, near, 2 * b)

    @pl.when(level != 0)
    def _():
        for b in range(2):
            fill(b, 1, near, 4 + 2 * b)
            fill(b, 0, near, 2 * b)
            fill(2 + b, 1, far, 2 * b)
            fill(2 + b, 0, far, 4 + 2 * b)

    most = jnp.zeros((members, LANES), F32)
    for i in range(blocks):
        added = None
        for b, target in enumerate((0, 1, blocks + 2, blocks + 3)):
            if 0 <= target - i < band:
                part = lax.dot_general(
                    control[b], cov[i, inverse(offsets, i, target - i)], NT,
                    preferred_element_type=F32,
                )
                added = part if added is None else added + part
        for r in range(2):
            row = 2 * i + r
            value = sums[row]
            if added is not None:
                value = value + added[:, r * LANES : (r + 1) * LANES]
            total[row] = value
            most = jnp.maximum(most, jnp.abs(value))
    peak = jnp.max(jnp.max(most, axis=0, keepdims=True), axis=1, keepdims=True)
    power = jnp.ceil(jnp.log2(jnp.maximum(peak, 1e-30) * (1.0 / 32000.0)))
    unit = jnp.broadcast_to(jnp.exp2(-power), (1, LANES))
    for row in range(rows):
        message[row * members : (row + 1) * members] = to_i16(total[row] * unit)
    at = rows * members
    message[at : at + packed.shape[0]] = packed[...]
    at = at + packed.shape[0]
    which = lax.broadcasted_iota(jnp.int32, meta.shape, 0)
    spot = meta.shape[0] - 1
    last = jnp.where(which == spot, jnp.broadcast_to(power, meta.shape).astype(jnp.int32), meta[...])
    message[at : at + meta.shape[0]] = last.astype(jnp.int16)


def unpack(ref, at, rows, members, chunks, level, mirror, drive, coef, seen, heavy):
    cells, base = rows * LANES, at + rows * members
    meta_at = base + chunks * members
    meta = from_i16(ref[meta_at : meta_at + META])
    unit = jnp.exp2(meta[META - 1 : META])
    spots = [jnp.where(mirror, rows - 1 - r, r) for r in range(rows)]
    for r, spot in enumerate(spots):
        start = at + r * members
        drive[spot] = from_i16(ref[start : start + members]) * unit
        spread = meta[2 * chunks + r : 2 * chunks + r + 1] * (1.0 / COEF_UNIT)
        coef[spot] = jnp.broadcast_to(spread, (8, LANES))
    weight = meta[chunks : 2 * chunks] * (1.0 / WEIGHT_UNIT)
    local = meta[0:chunks].astype(jnp.int32) - level * cells
    which = lax.broadcasted_iota(jnp.int32, (16, LANES), 0)
    total = jnp.zeros((2 * members + 16, cells), F32)
    for c in range(chunks):
        start = base + c * members
        value = from_i16(ref[start : start + members]) * (1.0 / VALUE_UNIT)
        high, low = halves(value * weight[c : c + 1])
        weight_high, weight_low = halves(weight[c : c + 1])
        ends = jnp.where(which == 0, weight_high, jnp.where(which == 1, weight_low, 0.0))
        left = jnp.concatenate([high, low, ends], axis=0).astype(BF)
        hit = lax.broadcasted_iota(jnp.int32, (cells, LANES), 0) == local[c : c + 1]
        total += lax.dot_general(
            left, jnp.where(hit, 1.0, 0.0).astype(BF), NT, preferred_element_type=F32
        )
    both = total[:members] + total[members : 2 * members]
    sums = total[2 * members : 2 * members + 1] + total[2 * members + 1 : 2 * members + 2]
    for r, spot in enumerate(spots):
        lanes = slice(r * LANES, (r + 1) * LANES)
        seen[spot] = both[:, lanes]
        heavy[spot] = jnp.broadcast_to(sums[:, lanes], (8, LANES))


def facing_tile(tiles):
    tile = lax.axis_index("tile")
    mirror = tile >= (tiles + 1) // 2
    return jnp.where(mirror, tiles - 1 - tile, tile), mirror


def prepare_kernel(tiles, sizes, masks, *refs):
    rows, members, chunks = sizes
    pieces, outs = refs[: len(masks)], refs[len(masks) :]
    (here, mirror), level = facing_tile(tiles), lax.axis_index("lev")
    for mask, (ref, at) in zip(masks, [(ref, 0) for ref in pieces]):
        tile = here ^ mask if len(masks) > 2 else (here & 1) ^ mask
        spot = pl.ds(tile * rows, rows)
        unpack(ref, at, rows, members, chunks, level, mirror, *[out.at[spot] for out in outs])


def target_sum(result, cov, offsets, target):
    blocks, band = cov.shape[0], cov.shape[1]
    total = None
    for i in range(max(0, target - band + 1), min(blocks - 1, target) + 1):
        part = jnp.dot(
            result[i], cov[i, inverse(offsets, i, target - i)], preferred_element_type=F32
        )
        total = part if total is None else total + part
    return total


def chain_kernel(
    tiles, sections, sizes, offsets, *refs
):
    rows, members, chunks = sizes
    own_section, early, late, (cov, result, keep, give) = refs[:4], refs[4:8], refs[8], refs[9:13]
    whole = refs[14:18]
    field, (drive, coef, seen, heavy) = refs[13], whole
    blocks, band, half, order = cov.shape
    (tile, mirror), section, level = facing_tile(tiles), lax.axis_index("sub"), lax.axis_index("lev")
    per_piece = rows * members + chunks * members + META
    pair = early[0].shape[0] // max(1, sections - 1)

    for target, source in zip(whole, own_section):
        target[section] = source[...]
    for ds in range(1, sections):
        base = pl.ds((tile & ~1) * rows, pair)
        for target, source in zip(whole, early):
            target[section ^ ds, base] = source[(ds - 1) * pair : ds * pair]
        for dt in range(2, tiles):
            at = ((ds - 1) * (tiles - 2) + dt - 2) * per_piece
            spot = pl.ds((tile ^ dt) * rows, rows)
            unpack(
                late, at, rows, members, chunks, level, mirror,
                *[target.at[section ^ ds, spot] for target in whole],
            )

    all_rows = tiles * rows
    zero = jnp.zeros((members, LANES), F32)
    field[0] = zero
    field[all_rows + 1] = zero

    def times(row_value, value):
        return (row_value[None] * value.reshape(members // 8, 8, LANES)).reshape(members, LANES)

    def beside(value):
        return pltpu.roll(value, 1, 1) + pltpu.roll(value, LANES - 1, 1)

    def reach(steps):
        return min(all_rows, (tiles + 1) // 2 * rows + steps)

    def over_rows(limit, step, carry):
        def on_tile(t, carry):
            for r in range(rows):
                if not isinstance(t, int) or t * rows + r < limit:
                    carry = step(t * rows + r, carry)
            return carry

        return loop(-(-limit // rows), on_tile, carry)

    def each_row(limit, step):
        def once(row, carry):
            step(row)
            return carry

        over_rows(limit, once, 0)

    def forward_step(sec, limit):
        def step(row, before):
            now = field[row + 1]
            around = before + field[row + 2] + beside(now) - 4.0 * now
            field[row + 1] = now + times(coef[sec, row], around)
            return now

        over_rows(limit, step, zero)

    def adjoint_step(sec, limit):
        def step(row, carry):
            before, now = carry
            if isinstance(row, int):
                after_row = min(row + 1, all_rows - 1)
            else:
                after_row = jnp.minimum(row + 1, all_rows - 1)
            after = times(coef[sec, after_row], field[row + 2])
            field[row + 1] = field[row + 1] + (before + after + beside(now) - 4.0 * now)
            return now, after

        over_rows(limit, step, (zero, times(coef[sec, 0], field[1])))

    for sec in range(sections):
        left = STEPS * (2 * sections - sec)

        def push(row):
            if sec == 0:
                field[row + 1] = drive[sec, row]
            else:
                field[row + 1] = field[row + 1] + drive[sec, row]

        each_row(reach(left), push)
        for j in range(STEPS):
            forward_step(sec, reach(left - 1 - j))

        def observe(row):
            drive[sec, row] = times(heavy[sec, row], field[row + 1]) - seen[sec, row]

        each_row(reach(STEPS * (sec + 1)), observe)

    for sec in range(sections - 1, -1, -1):
        left = STEPS * (sec + 1)

        def pull(row):
            if sec == sections - 1:
                field[row + 1] = drive[sec, row]
            else:
                field[row + 1] = field[row + 1] + drive[sec, row]

        each_row(reach(left), pull)
        for j in range(STEPS):
            adjoint_step(sec, reach(left - 1 - j))

        @pl.when(section == sec)
        def _():
            for r in range(rows):
                lane = (r % 2) * LANES
                spot = tile * rows + jnp.where(mirror, rows - 1 - r, r)
                result[r // 2, :, lane : lane + LANES] = field[spot + 1].astype(BF)

    def hand_out(kept_at, given_at):
        for target in (kept_at, kept_at + 1, given_at, given_at + 1):
            sums = target_sum(result, cov, offsets, target)
            out, first = (keep, kept_at) if target in (kept_at, kept_at + 1) else (give, given_at)
            for h in range(2):
                out[2 * h + target - first] = sums[:, h * half : (h + 1) * half]

    @pl.when(level == 0)
    def _():
        hand_out(blocks + 2, 0)

    @pl.when(level != 0)
    def _():
        hand_out(0, blocks + 2)


def core_kernel(offsets, result, cov, keep, give):
    blocks, band, half, order = cov.shape
    level = lax.axis_index("lev")
    for b in range(blocks):
        sums = target_sum(result, cov, offsets, b + 2)
        low, high = sums[:, :half], sums[:, half:]
        keep[b] = jnp.where(level == 0, low, high)
        give[b] = jnp.where(level == 0, high, low)


def final_kernel(control, kept, got, ghost, ghost_far, out, spare):
    rows, members = control.shape[0], control.shape[1]
    blocks, half = rows // 2, kept.shape[2]
    level = lax.axis_index("lev")
    for b in range(blocks):
        spare[b] = kept[b] + got[b]

    def add_ghosts(level_now):
        for b in range(2):
            near = ghost[2 * level_now + b].astype(F32)
            far = ghost_far[b].astype(F32)
            below, above = (far, near) if level_now == 0 else (near, far)
            spare[b] = spare[b] + below
            spare[blocks - 2 + b] = spare[blocks - 2 + b] + above

    @pl.when(level == 0)
    def _():
        add_ghosts(0)

    @pl.when(level != 0)
    def _():
        add_ghosts(1)

    for b in range(blocks):
        for r in range(2):
            row = 2 * b + r
            value = control[row].astype(F32) + spare[b, :, r * LANES : (r + 1) * LANES]
            out[pl.ds(row, members, stride=rows), :] = value


def body(
    model_error, start_state, covariance, offsets, diffusion, observed_cell, observed_count,
    observed_value, observed_weight,
):
    members, rows = model_error.shape[1], model_error.shape[3]
    blocks, band, half, order = covariance.shape
    tiles, sections = lax.axis_size("tile"), lax.axis_size("sub")
    slots = observed_cell.shape[2]
    level = lax.axis_index("lev")
    vmem, smem = pl.BlockSpec(memory_space=pltpu.VMEM), pl.BlockSpec(memory_space=pltpu.SMEM)
    hbm = pl.BlockSpec(memory_space=pltpu.HBM)

    control = model_error[0, :, 0].transpose(1, 0, 2)
    other = swap(control, "lev")
    edge = jnp.where(level == 0, rows - 4, 0)
    near = swap_facing(
        jnp.concatenate(
            [lax.dynamic_slice_in_dim(control, edge, 4), lax.dynamic_slice_in_dim(other, edge, 4)]
        )
    )

    chunks = slots // LANES
    sizes = (rows, members, chunks)
    offsets, cov, packed, meta, sums = pl.pallas_call(
        stage_kernel,
        out_shape=[
            pltpu.SMEM(offsets.shape, jnp.int32),
            pltpu.VMEM(covariance.shape, BF),
            pltpu.VMEM((chunks * members, LANES), jnp.int16),
            pltpu.VMEM((META, LANES), jnp.int32),
            pltpu.VMEM((rows, members, LANES), F32),
        ],
        in_specs=[smem] + [hbm] * 9,
        out_specs=[smem] + [vmem] * 4,
        scratch_shapes=[
            pltpu.VMEM(control.shape, BF),
            pltpu.VMEM(control.shape, BF),
            pltpu.VMEM((members * rows, LANES), F32),
            pltpu.VMEM((rows, 1, LANES), F32),
            pltpu.VMEM((chunks, LANES), jnp.int32),
            pltpu.VMEM((chunks, LANES), F32),
            pltpu.VMEM((members, slots), F32),
            pltpu.VMEM((blocks, members, order), BF),
            pltpu.SemaphoreType.DMA((blocks + 8,)),
        ],
        compiler_params=pltpu.CompilerParams(vmem_limit_bytes=STAGE_ROOM),
        cost_estimate=pl.CostEstimate(flops=0, bytes_accessed=8 * 10**6, transcendentals=0),
        name="stage",
    )(
        observed_count, offsets, control, other, covariance,
        start_state.reshape(members * rows, LANES), diffusion.reshape(rows, 1, LANES),
        observed_cell.reshape(chunks, LANES), observed_weight.reshape(chunks, LANES),
        observed_value[0, 0].T,
    )

    near, sums = lax.optimization_barrier((near, sums))
    far = swap(near, "lev")
    message_rows = rows * members + chunks * members + META
    message = pl.pallas_call(
        forcing_kernel,
        out_shape=jax.ShapeDtypeStruct((message_rows, LANES), jnp.int16),
        in_specs=[smem] + [vmem] * 6,
        out_specs=vmem,
        scratch_shapes=[
            pltpu.VMEM((4, members, order), BF),
            pltpu.VMEM((rows, members, LANES), F32),
        ],
        compiler_params=pltpu.CompilerParams(vmem_limit_bytes=8 * MIB),
        name="forcing",
    )(offsets, near, far, sums, packed, meta, cov)

    pieces = [message] + [swap(message, "tile", d) for d in range(1, tiles)]
    early = [swap(piece, "sub", d) for d in range(1, sections) for piece in pieces[:2]]
    held, early = lax.optimization_barrier((pieces[2:], early))
    late = jnp.concatenate(
        [swap(jnp.concatenate(held), "sub", d) for d in range(1, sections)]
    )

    all_rows = tiles * rows
    wide = (all_rows, members, LANES)
    flat = (all_rows, 8, LANES)
    room = 4 * all_rows * (members + 8) * LANES

    def prepare(arrays, masks, count):
        height = count * rows
        return pl.pallas_call(
            functools.partial(prepare_kernel, tiles, sizes, masks),
            out_shape=[
                jax.ShapeDtypeStruct((height, size, LANES), F32) for size in (members, 8) * 2
            ],
            in_specs=[vmem] * len(arrays),
            out_specs=[vmem] * 4,
            compiler_params=pltpu.CompilerParams(vmem_limit_bytes=6 * MIB + 2 * room),
            cost_estimate=pl.CostEstimate(
                flops=10**8 * count, bytes_accessed=10**6 * count, transcendentals=0
            ),
            name="prepare",
        )(*arrays)

    own_section = prepare(pieces, tuple(range(tiles)), tiles)
    others = [prepare(early[2 * d : 2 * d + 2], (0, 1), 2) for d in range(sections - 1)]
    early_section = [jnp.concatenate(group) for group in zip(*others)]

    result, keep, give = pl.pallas_call(
        functools.partial(chain_kernel, tiles, sections, sizes),
        out_shape=[jax.ShapeDtypeStruct((blocks, members, half), BF)]
        + [jax.ShapeDtypeStruct((4, members, half), F32)] * 2,
        in_specs=[smem] + [vmem] * 10,
        out_specs=[vmem] * 3,
        scratch_shapes=[
            pltpu.VMEM((all_rows + 2, members, LANES), F32),
            pltpu.VMEM((sections,) + wide, F32),
            pltpu.VMEM((sections,) + flat, F32),
            pltpu.VMEM((sections,) + wide, F32),
            pltpu.VMEM((sections,) + flat, F32),
        ],
        compiler_params=pltpu.CompilerParams(vmem_limit_bytes=6 * MIB + (3 * sections + 3) * room),
        name="chain",
    )(offsets, *own_section, *early_section, late, cov)

    ghost_got = swap(give, "lev")
    ghost = swap_facing((keep + ghost_got).astype(BF))
    kept, given = pl.pallas_call(
        core_kernel,
        out_shape=[jax.ShapeDtypeStruct((blocks, members, half), F32)] * 2,
        in_specs=[smem] + [vmem] * 2,
        out_specs=[vmem] * 2,
        compiler_params=pltpu.CompilerParams(vmem_limit_bytes=4 * MIB),
        cost_estimate=pl.CostEstimate(flops=10**9, bytes_accessed=8 * 10**6, transcendentals=0),
        name="core",
    )(offsets, result, cov)
    got = swap(given, "lev")
    ghost_far = swap(jnp.where(level == 0, ghost[2:], ghost[:2]), "lev")
    out = pl.pallas_call(
        final_kernel,
        out_shape=jax.ShapeDtypeStruct((members * rows, LANES), F32),
        in_specs=[vmem] * 5,
        out_specs=vmem,
        scratch_shapes=[pltpu.VMEM((blocks, members, half), F32)],
        compiler_params=pltpu.CompilerParams(vmem_limit_bytes=4 * MIB),
        name="final",
    )(control, kept, got, ghost, ghost_far)
    return out.reshape(1, members, 1, rows, LANES)


def solution(mesh):
    in_specs = (
        P("sub", "grp", "lev", "tile", None),
        P("grp", "lev", "tile", None),
        P("tile", None, "lev", None),
        P("tile", None),
        P("sub", "lev", "tile", None),
        P("sub", "tile", "grp"),
        P("sub", "tile", "grp"),
        P("sub", "tile", None, "grp"),
        P("sub", "tile", "grp"),
    )
    out_specs = P("sub", "grp", "lev", "tile", None)
    return jax.shard_map(body, mesh=mesh, in_specs=in_specs, out_specs=out_specs, check_vma=False)
```

```python
import functools

import jax
import jax.numpy as jnp
from jax import lax
from jax.experimental import pallas as pl
from jax.experimental.pallas import tpu as pltpu
from jax.sharding import PartitionSpec as P

STEPS = 4
LANES = 128
BF = jnp.bfloat16
F32 = jnp.float32
NT = (((1,), (1,)), ((), ()))
MIB = 2**20
META = 16
WEIGHT_UNIT, COEF_UNIT, VALUE_UNIT = 8191.0, 131072.0, 5461.0
STAGE_ROOM = 56 * MIB
OWN_ROOM = 16 * MIB


def swap(block, axis, mask=1):
    count = lax.axis_size(axis)
    return lax.ppermute(block, axis, [(i, i ^ mask) for i in range(count)])


def swap_facing(block):
    pairs = [(2 * t, 2 * (t + 1) + 1) for t in range(lax.axis_size("tile") - 1)]
    return lax.ppermute(block, ("tile", "lev"), pairs + [(b, a) for a, b in pairs])


def loop(count, step, carry):
    if count <= 4:
        for i in range(count):
            carry = step(i, carry)
        return carry
    return lax.fori_loop(0, count, step, carry)


def halves(value):
    high = value.astype(BF).astype(F32)
    return high, value - high


def to_i16(value):
    return jnp.round(value).astype(jnp.int32).astype(jnp.int16)


def from_i16(value):
    return value.astype(jnp.int32).astype(F32)


def inverse(offsets, i, wanted):
    found = 0
    for k in range(offsets.shape[1]):
        found = found + jnp.where(offsets[i, k] == wanted, k, 0)
    return found


def stage_kernel(
    offsets_hbm, own_hbm, start_hbm, diffusion_hbm, cells_hbm, weights_hbm, values_hbm, cov_hbm,
    offsets, edge, start, packed, meta, own, diffusion, cells, weights, values, sems,
):
    chunks, members, rows = cells.shape[0], values.shape[0], diffusion.shape[0]
    pairs = (
        (own_hbm, own), (diffusion_hbm, diffusion), (cells_hbm, cells), (weights_hbm, weights),
        (values_hbm, values), (offsets_hbm, offsets), (start_hbm, start),
    )
    copies = [
        pltpu.make_async_copy(source, target, sems.at[n]) for n, (source, target) in enumerate(pairs)
    ]
    for copy in copies:
        copy.start()
    for copy in copies:
        copy.wait()
    first = jnp.where(lax.axis_index("lev") == 0, rows - 4, 0)
    for r in range(4):
        edge[r] = own[first + r]
    meta[...] = jnp.zeros_like(meta)
    meta[0:chunks] = cells[...]
    meta[chunks : 2 * chunks] = jnp.round(weights[...] * WEIGHT_UNIT).astype(jnp.int32)
    for r in range(rows):
        spot = 2 * chunks + r
        meta[spot : spot + 1] = jnp.round(diffusion[r] * COEF_UNIT).astype(jnp.int32)
    for c in range(chunks):
        value = values[:, c * LANES : (c + 1) * LANES]
        packed[c * members : (c + 1) * members] = to_i16(value * VALUE_UNIT)


def own_kernel(chunks, offsets, count, start, meta, own, other, cov, sums, live_meta, control):
    blocks, band, half, order = cov.shape
    rows, members = own.shape[0], own.shape[1]
    section, level = lax.axis_index("sub"), lax.axis_index("lev")
    which = lax.broadcasted_iota(jnp.int32, meta.shape, 0)
    slot = (which - chunks) * LANES + lax.broadcasted_iota(jnp.int32, meta.shape, 1)
    weights = (which >= chunks) & (which < 2 * chunks)
    live_meta[...] = jnp.where(weights & (slot >= count[0, 0, 0]), 0, meta[...])
    for b in range(blocks):
        for r in range(2):
            mine, theirs = own[2 * b + r], other[2 * b + r]
            for part in range(2):
                lane = (part * 2 + r) * LANES
                value = jnp.where(level == part, mine.astype(F32), theirs.astype(F32))
                control[b, :, lane : lane + LANES] = value.astype(BF)
    first = jnp.where(section == 0, 1.0, 0.0).astype(F32)
    for i in range(blocks):
        total = jnp.zeros((members, half), F32)
        for b in range(max(0, i - 2), min(blocks, i + 3)):
            total += lax.dot_general(
                control[b], cov[i, inverse(offsets, i, b + 2 - i)], NT, preferred_element_type=F32
            )
        for r in range(2):
            row = 2 * i + r
            begin = start[pl.ds(row, members, stride=rows), :]
            sums[row] = total[:, r * LANES : (r + 1) * LANES] + first * begin


def forcing_kernel(offsets, near, far, sums, packed, meta, cov, message, control, total):
    blocks, band, half, order = cov.shape
    rows, members = sums.shape[0], sums.shape[1]
    level = lax.axis_index("lev")

    def fill(b, part, source, at):
        for r in range(2):
            lane = (part * 2 + r) * LANES
            control[b, :, lane : lane + LANES] = source[at + r]

    @pl.when(level == 0)
    def _():
        for b in range(2):
            fill(b, 0, far, 2 * b)
            fill(b, 1, far, 4 + 2 * b)
            fill(2 + b, 0, near, 4 + 2 * b)
            fill(2 + b, 1, near, 2 * b)

    @pl.when(level != 0)
    def _():
        for b in range(2):
            fill(b, 1, near, 4 + 2 * b)
            fill(b, 0, near, 2 * b)
            fill(2 + b, 1, far, 2 * b)
            fill(2 + b, 0, far, 4 + 2 * b)

    most = jnp.zeros((members, LANES), F32)
    for i in range(blocks):
        added = None
        for b, target in enumerate((0, 1, blocks + 2, blocks + 3)):
            if 0 <= target - i < band:
                part = lax.dot_general(
                    control[b], cov[i, inverse(offsets, i, target - i)], NT,
                    preferred_element_type=F32,
                )
                added = part if added is None else added + part
        for r in range(2):
            row = 2 * i + r
            value = sums[row]
            if added is not None:
                value = value + added[:, r * LANES : (r + 1) * LANES]
            total[row] = value
            most = jnp.maximum(most, jnp.abs(value))
    peak = jnp.max(jnp.max(most, axis=0, keepdims=True), axis=1, keepdims=True)
    power = jnp.ceil(jnp.log2(jnp.maximum(peak, 1e-30) * (1.0 / 32000.0)))
    unit = jnp.broadcast_to(jnp.exp2(-power), (1, LANES))
    for row in range(rows):
        message[row * members : (row + 1) * members] = to_i16(total[row] * unit)
    at = rows * members
    message[at : at + packed.shape[0]] = packed[...]
    at = at + packed.shape[0]
    which = lax.broadcasted_iota(jnp.int32, meta.shape, 0)
    spot = meta.shape[0] - 1
    last = jnp.where(which == spot, jnp.broadcast_to(power, meta.shape).astype(jnp.int32), meta[...])
    message[at : at + meta.shape[0]] = last.astype(jnp.int16)


def unpack(ref, at, rows, members, chunks, level, mirror, drive, coef, seen, heavy):
    cells, base = rows * LANES, at + rows * members
    meta_at = base + chunks * members
    meta = from_i16(ref[meta_at : meta_at + META])
    unit = jnp.exp2(meta[META - 1 : META])
    spots = [jnp.where(mirror, rows - 1 - r, r) for r in range(rows)]
    for r, spot in enumerate(spots):
        start = at + r * members
        drive[spot] = from_i16(ref[start : start + members]) * unit
        spread = meta[2 * chunks + r : 2 * chunks + r + 1] * (1.0 / COEF_UNIT)
        coef[spot] = jnp.broadcast_to(spread, (8, LANES))
    weight = meta[chunks : 2 * chunks] * (1.0 / WEIGHT_UNIT)
    local = meta[0:chunks].astype(jnp.int32) - level * cells
    which = lax.broadcasted_iota(jnp.int32, (16, LANES), 0)
    total = jnp.zeros((2 * members + 16, cells), F32)
    for c in range(chunks):
        start = base + c * members
        value = from_i16(ref[start : start + members]) * (1.0 / VALUE_UNIT)
        high, low = halves(value * weight[c : c + 1])
        weight_high, weight_low = halves(weight[c : c + 1])
        ends = jnp.where(which == 0, weight_high, jnp.where(which == 1, weight_low, 0.0))
        left = jnp.concatenate([high, low, ends], axis=0).astype(BF)
        hit = lax.broadcasted_iota(jnp.int32, (cells, LANES), 0) == local[c : c + 1]
        total += lax.dot_general(
            left, jnp.where(hit, 1.0, 0.0).astype(BF), NT, preferred_element_type=F32
        )
    both = total[:members] + total[members : 2 * members]
    sums = total[2 * members : 2 * members + 1] + total[2 * members + 1 : 2 * members + 2]
    for r, spot in enumerate(spots):
        lanes = slice(r * LANES, (r + 1) * LANES)
        seen[spot] = both[:, lanes]
        heavy[spot] = jnp.broadcast_to(sums[:, lanes], (8, LANES))


def facing_tile(tiles):
    tile = lax.axis_index("tile")
    mirror = tile >= (tiles + 1) // 2
    return jnp.where(mirror, tiles - 1 - tile, tile), mirror


def prepare_kernel(tiles, sizes, masks, *refs):
    rows, members, chunks = sizes
    pieces, outs = refs[: len(masks)], refs[len(masks) :]
    (here, mirror), level = facing_tile(tiles), lax.axis_index("lev")
    for mask, (ref, at) in zip(masks, [(ref, 0) for ref in pieces]):
        tile = here ^ mask if len(masks) > 2 else (here & 1) ^ mask
        spot = pl.ds(tile * rows, rows)
        unpack(ref, at, rows, members, chunks, level, mirror, *[out.at[spot] for out in outs])


def target_sum(result, cov, offsets, target):
    blocks, band = cov.shape[0], cov.shape[1]
    total = None
    for i in range(max(0, target - band + 1), min(blocks - 1, target) + 1):
        part = jnp.dot(
            result[i], cov[i, inverse(offsets, i, target - i)], preferred_element_type=F32
        )
        total = part if total is None else total + part
    return total


def chain_kernel(
    tiles, sections, sizes, offsets, *refs
):
    rows, members, chunks = sizes
    own_section, early, late, (cov, result, keep, give) = refs[:4], refs[4:8], refs[8], refs[9:13]
    whole = refs[14:18]
    field, (drive, coef, seen, heavy) = refs[13], whole
    blocks, band, half, order = cov.shape
    (tile, mirror), section, level = facing_tile(tiles), lax.axis_index("sub"), lax.axis_index("lev")
    per_piece = rows * members + chunks * members + META
    pair = early[0].shape[0] // max(1, sections - 1)

    for target, source in zip(whole, own_section):
        target[section] = source[...]
    for ds in range(1, sections):
        base = pl.ds((tile & ~1) * rows, pair)
        for target, source in zip(whole, early):
            target[section ^ ds, base] = source[(ds - 1) * pair : ds * pair]
        for dt in range(2, tiles):
            at = ((ds - 1) * (tiles - 2) + dt - 2) * per_piece
            spot = pl.ds((tile ^ dt) * rows, rows)
            unpack(
                late, at, rows, members, chunks, level, mirror,
                *[target.at[section ^ ds, spot] for target in whole],
            )

    all_rows = tiles * rows
    zero = jnp.zeros((members, LANES), F32)
    field[0] = zero
    field[all_rows + 1] = zero

    def times(row_value, value):
        return (row_value[None] * value.reshape(members // 8, 8, LANES)).reshape(members, LANES)

    def beside(value):
        return pltpu.roll(value, 1, 1) + pltpu.roll(value, LANES - 1, 1)

    def reach(steps):
        return min(all_rows, (tiles + 1) // 2 * rows + steps)

    def over_rows(limit, step, carry):
        def on_tile(t, carry):
            for r in range(rows):
                if not isinstance(t, int) or t * rows + r < limit:
                    carry = step(t * rows + r, carry)
            return carry

        return loop(-(-limit // rows), on_tile, carry)

    def each_row(limit, step):
        def once(row, carry):
            step(row)
            return carry

        over_rows(limit, once, 0)

    def forward_step(sec, limit):
        def step(row, before):
            now = field[row + 1]
            around = before + field[row + 2] + beside(now) - 4.0 * now
            field[row + 1] = now + times(coef[sec, row], around)
            return now

        over_rows(limit, step, zero)

    def adjoint_step(sec, limit):
        def step(row, carry):
            before, now = carry
            if isinstance(row, int):
                after_row = min(row + 1, all_rows - 1)
            else:
                after_row = jnp.minimum(row + 1, all_rows - 1)
            after = times(coef[sec, after_row], field[row + 2])
            field[row + 1] = field[row + 1] + (before + after + beside(now) - 4.0 * now)
            return now, after

        over_rows(limit, step, (zero, times(coef[sec, 0], field[1])))

    for sec in range(sections):
        left = STEPS * (2 * sections - sec)

        def push(row):
            if sec == 0:
                field[row + 1] = drive[sec, row]
            else:
                field[row + 1] = field[row + 1] + drive[sec, row]

        each_row(reach(left), push)
        for j in range(STEPS):
            forward_step(sec, reach(left - 1 - j))

        def observe(row):
            drive[sec, row] = times(heavy[sec, row], field[row + 1]) - seen[sec, row]

        each_row(reach(STEPS * (sec + 1)), observe)

    for sec in range(sections - 1, -1, -1):
        left = STEPS * (sec + 1)

        def pull(row):
            if sec == sections - 1:
                field[row + 1] = drive[sec, row]
            else:
                field[row + 1] = field[row + 1] + drive[sec, row]

        each_row(reach(left), pull)
        for j in range(STEPS):
            adjoint_step(sec, reach(left - 1 - j))

        @pl.when(section == sec)
        def _():
            for r in range(rows):
                lane = (r % 2) * LANES
                spot = tile * rows + jnp.where(mirror, rows - 1 - r, r)
                result[r // 2, :, lane : lane + LANES] = field[spot + 1].astype(BF)

    def hand_out(kept_at, given_at):
        for target in (kept_at, kept_at + 1, given_at, given_at + 1):
            sums = target_sum(result, cov, offsets, target)
            out, first = (keep, kept_at) if target in (kept_at, kept_at + 1) else (give, given_at)
            for h in range(2):
                out[2 * h + target - first] = sums[:, h * half : (h + 1) * half]

    @pl.when(level == 0)
    def _():
        hand_out(blocks + 2, 0)

    @pl.when(level != 0)
    def _():
        hand_out(0, blocks + 2)


def core_kernel(offsets, result, cov, keep, give):
    blocks, band, half, order = cov.shape
    level = lax.axis_index("lev")
    for b in range(blocks):
        sums = target_sum(result, cov, offsets, b + 2)
        low, high = sums[:, :half], sums[:, half:]
        keep[b] = jnp.where(level == 0, low, high)
        give[b] = jnp.where(level == 0, high, low)


def final_kernel(control, kept, got, ghost, ghost_far, out, spare):
    rows, members = control.shape[0], control.shape[1]
    blocks, half = rows // 2, kept.shape[2]
    level = lax.axis_index("lev")
    for b in range(blocks):
        spare[b] = kept[b] + got[b]

    def add_ghosts(level_now):
        for b in range(2):
            near = ghost[2 * level_now + b].astype(F32)
            far = ghost_far[b].astype(F32)
            below, above = (far, near) if level_now == 0 else (near, far)
            spare[b] = spare[b] + below
            spare[blocks - 2 + b] = spare[blocks - 2 + b] + above

    @pl.when(level == 0)
    def _():
        add_ghosts(0)

    @pl.when(level != 0)
    def _():
        add_ghosts(1)

    for b in range(blocks):
        for r in range(2):
            row = 2 * b + r
            value = control[row].astype(F32) + spare[b, :, r * LANES : (r + 1) * LANES]
            out[pl.ds(row, members, stride=rows), :] = value


def body(
    model_error, start_state, covariance, offsets, diffusion, observed_cell, observed_count,
    observed_value, observed_weight,
):
    members, rows = model_error.shape[1], model_error.shape[3]
    blocks, band, half, order = covariance.shape
    tiles, sections = lax.axis_size("tile"), lax.axis_size("sub")
    slots = observed_cell.shape[2]
    level = lax.axis_index("lev")
    vmem, smem = pl.BlockSpec(memory_space=pltpu.VMEM), pl.BlockSpec(memory_space=pltpu.SMEM)
    hbm = pl.BlockSpec(memory_space=pltpu.HBM)

    control = model_error[0, :, 0].transpose(1, 0, 2)
    other = swap(control, "lev")
    chunks = slots // LANES
    sizes = (rows, members, chunks)
    offsets, edge, start, packed, meta, control_here = pl.pallas_call(
        stage_kernel,
        out_shape=[
            pltpu.SMEM(offsets.shape, jnp.int32),
            pltpu.VMEM((4, members, LANES), BF),
            pltpu.VMEM((members * rows, LANES), F32),
            pltpu.VMEM((chunks * members, LANES), jnp.int16),
            pltpu.VMEM((META, LANES), jnp.int32),
            pltpu.VMEM(control.shape, BF),
        ],
        in_specs=[hbm] * 8,
        out_specs=[smem] + [vmem] * 5,
        scratch_shapes=[
            pltpu.VMEM((rows, 1, LANES), F32),
            pltpu.VMEM((chunks, LANES), jnp.int32),
            pltpu.VMEM((chunks, LANES), F32),
            pltpu.VMEM((members, slots), F32),
            pltpu.SemaphoreType.DMA((7,)),
        ],
        compiler_params=pltpu.CompilerParams(vmem_limit_bytes=STAGE_ROOM),
        cost_estimate=pl.CostEstimate(flops=0, bytes_accessed=2 * 10**6, transcendentals=0),
        name="stage",
    )(
        offsets, control, start_state.reshape(members * rows, LANES),
        diffusion.reshape(rows, 1, LANES), observed_cell.reshape(chunks, LANES),
        observed_weight.reshape(chunks, LANES), observed_value[0, 0].T, covariance,
    )

    far_edge = lax.dynamic_slice_in_dim(other, jnp.where(level == 0, rows - 4, 0), 4)
    near = swap_facing(jnp.concatenate([edge, far_edge]))
    cov = covariance
    sums, meta = pl.pallas_call(
        functools.partial(own_kernel, chunks),
        out_shape=[
            pltpu.VMEM((rows, members, LANES), F32),
            pltpu.VMEM((META, LANES), jnp.int32),
        ],
        in_specs=[smem] * 2 + [vmem] * 5,
        out_specs=[vmem] * 2,
        scratch_shapes=[pltpu.VMEM((blocks, members, order), BF)],
        compiler_params=pltpu.CompilerParams(vmem_limit_bytes=OWN_ROOM),
        cost_estimate=pl.CostEstimate(flops=0, bytes_accessed=6 * 10**6, transcendentals=0),
        name="own",
    )(offsets, observed_count, start, meta, control_here, other, cov)

    near, sums = lax.optimization_barrier((near, sums))
    far = swap(near, "lev")
    message_rows = rows * members + chunks * members + META
    message = pl.pallas_call(
        forcing_kernel,
        out_shape=jax.ShapeDtypeStruct((message_rows, LANES), jnp.int16),
        in_specs=[smem] + [vmem] * 6,
        out_specs=vmem,
        scratch_shapes=[
            pltpu.VMEM((4, members, order), BF),
            pltpu.VMEM((rows, members, LANES), F32),
        ],
        compiler_params=pltpu.CompilerParams(vmem_limit_bytes=8 * MIB),
        name="forcing",
    )(offsets, near, far, sums, packed, meta, cov)

    pieces = [message] + [swap(message, "tile", d) for d in range(1, tiles)]
    early = [swap(piece, "sub", d) for d in range(1, sections) for piece in pieces[:2]]
    held, early = lax.optimization_barrier((pieces[2:], early))
    late = jnp.concatenate(
        [swap(jnp.concatenate(held), "sub", d) for d in range(1, sections)]
    )

    all_rows = tiles * rows
    wide = (all_rows, members, LANES)
    flat = (all_rows, 8, LANES)
    room = 4 * all_rows * (members + 8) * LANES

    def prepare(arrays, masks, count):
        height = count * rows
        return pl.pallas_call(
            functools.partial(prepare_kernel, tiles, sizes, masks),
            out_shape=[
                jax.ShapeDtypeStruct((height, size, LANES), F32) for size in (members, 8) * 2
            ],
            in_specs=[vmem] * len(arrays),
            out_specs=[vmem] * 4,
            compiler_params=pltpu.CompilerParams(vmem_limit_bytes=6 * MIB + 2 * room),
            cost_estimate=pl.CostEstimate(
                flops=10**8 * count, bytes_accessed=10**6 * count, transcendentals=0
            ),
            name="prepare",
        )(*arrays)

    own_section = prepare(pieces, tuple(range(tiles)), tiles)
    others = [prepare(early[2 * d : 2 * d + 2], (0, 1), 2) for d in range(sections - 1)]
    early_section = [jnp.concatenate(group) for group in zip(*others)]

    result, keep, give = pl.pallas_call(
        functools.partial(chain_kernel, tiles, sections, sizes),
        out_shape=[jax.ShapeDtypeStruct((blocks, members, half), BF)]
        + [jax.ShapeDtypeStruct((4, members, half), F32)] * 2,
        in_specs=[smem] + [vmem] * 10,
        out_specs=[vmem] * 3,
        scratch_shapes=[
            pltpu.VMEM((all_rows + 2, members, LANES), F32),
            pltpu.VMEM((sections,) + wide, F32),
            pltpu.VMEM((sections,) + flat, F32),
            pltpu.VMEM((sections,) + wide, F32),
            pltpu.VMEM((sections,) + flat, F32),
        ],
        compiler_params=pltpu.CompilerParams(vmem_limit_bytes=6 * MIB + (3 * sections + 3) * room),
        name="chain",
    )(offsets, *own_section, *early_section, late, cov)

    ghost_got = swap(give, "lev")
    ghost = swap_facing((keep + ghost_got).astype(BF))
    kept, given = pl.pallas_call(
        core_kernel,
        out_shape=[jax.ShapeDtypeStruct((blocks, members, half), F32)] * 2,
        in_specs=[smem] + [vmem] * 2,
        out_specs=[vmem] * 2,
        compiler_params=pltpu.CompilerParams(vmem_limit_bytes=4 * MIB),
        cost_estimate=pl.CostEstimate(flops=10**9, bytes_accessed=8 * 10**6, transcendentals=0),
        name="core",
    )(offsets, result, cov)
    got = swap(given, "lev")
    ghost_far = swap(jnp.where(level == 0, ghost[2:], ghost[:2]), "lev")
    out = pl.pallas_call(
        final_kernel,
        out_shape=jax.ShapeDtypeStruct((members * rows, LANES), F32),
        in_specs=[vmem] * 5,
        out_specs=vmem,
        scratch_shapes=[pltpu.VMEM((blocks, members, half), F32)],
        compiler_params=pltpu.CompilerParams(vmem_limit_bytes=4 * MIB),
        name="final",
    )(control_here, kept, got, ghost, ghost_far)
    return out.reshape(1, members, 1, rows, LANES)


def solution(mesh):
    in_specs = (
        P("sub", "grp", "lev", "tile", None),
        P("grp", "lev", "tile", None),
        P("tile", None, "lev", None),
        P("tile", None),
        P("sub", "lev", "tile", None),
        P("sub", "tile", "grp"),
        P("sub", "tile", "grp"),
        P("sub", "tile", None, "grp"),
        P("sub", "tile", "grp"),
    )
    out_specs = P("sub", "grp", "lev", "tile", None)
    return jax.shard_map(body, mesh=mesh, in_specs=in_specs, out_specs=out_specs, check_vma=False)
```

```python
import functools

import jax
import jax.numpy as jnp
from jax import lax
from jax.experimental import pallas as pl
from jax.experimental.pallas import tpu as pltpu
from jax.sharding import PartitionSpec as P

STEPS = 4
LANES = 128
BF = jnp.bfloat16
F32 = jnp.float32
NT = (((1,), (1,)), ((), ()))
MIB = 2**20
META = 16
WEIGHT_UNIT, COEF_UNIT, VALUE_UNIT = 8191.0, 131072.0, 5461.0
STAGE_ROOM = 56 * MIB
OWN_ROOM = 16 * MIB


def swap(block, axis, mask=1):
    count = lax.axis_size(axis)
    return lax.ppermute(block, axis, [(i, i ^ mask) for i in range(count)])


def swap_facing(block):
    pairs = [(2 * t, 2 * (t + 1) + 1) for t in range(lax.axis_size("tile") - 1)]
    return lax.ppermute(block, ("tile", "lev"), pairs + [(b, a) for a, b in pairs])


def loop(count, step, carry):
    if count <= 4:
        for i in range(count):
            carry = step(i, carry)
        return carry
    return lax.fori_loop(0, count, step, carry)


def halves(value):
    high = value.astype(BF).astype(F32)
    return high, value - high


def to_i16(value):
    return jnp.round(value).astype(jnp.int32).astype(jnp.int16)


def from_i16(value):
    return value.astype(jnp.int32).astype(F32)


def inverse(offsets, i, wanted):
    found = 0
    for k in range(offsets.shape[1]):
        found = found + jnp.where(offsets[i, k] == wanted, k, 0)
    return found


def stage_kernel(
    offsets_hbm, own_hbm, start_hbm, diffusion_hbm, cells_hbm, weights_hbm, values_hbm, cov_hbm,
    offsets, edge, start, packed, meta, own, diffusion, cells, weights, values, sems,
):
    chunks, members, rows = cells.shape[0], values.shape[0], diffusion.shape[0]
    pairs = (
        (own_hbm, own), (diffusion_hbm, diffusion), (cells_hbm, cells), (weights_hbm, weights),
        (values_hbm, values), (offsets_hbm, offsets), (start_hbm, start),
    )
    copies = [
        pltpu.make_async_copy(source, target, sems.at[n]) for n, (source, target) in enumerate(pairs)
    ]
    for copy in copies:
        copy.start()
    for copy in copies:
        copy.wait()
    first = jnp.where(lax.axis_index("lev") == 0, rows - 4, 0)
    for r in range(4):
        edge[r] = own[first + r]
    meta[...] = jnp.zeros_like(meta)
    meta[0:chunks] = cells[...]
    meta[chunks : 2 * chunks] = jnp.round(weights[...] * WEIGHT_UNIT).astype(jnp.int32)
    for r in range(rows):
        spot = 2 * chunks + r
        meta[spot : spot + 1] = jnp.round(diffusion[r] * COEF_UNIT).astype(jnp.int32)
    for c in range(chunks):
        value = values[:, c * LANES : (c + 1) * LANES]
        packed[c * members : (c + 1) * members] = to_i16(value * VALUE_UNIT)


def own_kernel(chunks, offsets, count, start, meta, own, other, cov, sums, live_meta, control):
    blocks, band, half, order = cov.shape
    rows, members = own.shape[0], own.shape[1]
    section, level = lax.axis_index("sub"), lax.axis_index("lev")
    which = lax.broadcasted_iota(jnp.int32, meta.shape, 0)
    slot = (which - chunks) * LANES + lax.broadcasted_iota(jnp.int32, meta.shape, 1)
    weights = (which >= chunks) & (which < 2 * chunks)
    live_meta[...] = jnp.where(weights & (slot >= count[0, 0, 0]), 0, meta[...])
    for b in range(blocks):
        for r in range(2):
            mine, theirs = own[2 * b + r], other[2 * b + r]
            for part in range(2):
                lane = (part * 2 + r) * LANES
                value = jnp.where(level == part, mine.astype(F32), theirs.astype(F32))
                control[b, :, lane : lane + LANES] = value.astype(BF)
    first = jnp.where(section == 0, 1.0, 0.0).astype(F32)
    for i in range(blocks):
        total = jnp.zeros((members, half), F32)
        for b in range(max(0, i - 2), min(blocks, i + 3)):
            total += lax.dot_general(
                control[b], cov[i, inverse(offsets, i, b + 2 - i)], NT, preferred_element_type=F32
            )
        for r in range(2):
            row = 2 * i + r
            begin = start[pl.ds(row, members, stride=rows), :]
            sums[row] = total[:, r * LANES : (r + 1) * LANES] + first * begin


def forcing_kernel(offsets, near, far, sums, packed, meta, cov, message, control, total):
    blocks, band, half, order = cov.shape
    rows, members = sums.shape[0], sums.shape[1]
    level = lax.axis_index("lev")

    def fill(b, part, source, at):
        for r in range(2):
            lane = (part * 2 + r) * LANES
            control[b, :, lane : lane + LANES] = source[at + r]

    @pl.when(level == 0)
    def _():
        for b in range(2):
            fill(b, 0, far, 2 * b)
            fill(b, 1, far, 4 + 2 * b)
            fill(2 + b, 0, near, 4 + 2 * b)
            fill(2 + b, 1, near, 2 * b)

    @pl.when(level != 0)
    def _():
        for b in range(2):
            fill(b, 1, near, 4 + 2 * b)
            fill(b, 0, near, 2 * b)
            fill(2 + b, 1, far, 2 * b)
            fill(2 + b, 0, far, 4 + 2 * b)

    most = jnp.zeros((members, LANES), F32)
    for i in range(blocks):
        added = None
        for b, target in enumerate((0, 1, blocks + 2, blocks + 3)):
            if 0 <= target - i < band:
                part = lax.dot_general(
                    control[b], cov[i, inverse(offsets, i, target - i)], NT,
                    preferred_element_type=F32,
                )
                added = part if added is None else added + part
        for r in range(2):
            row = 2 * i + r
            value = sums[row]
            if added is not None:
                value = value + added[:, r * LANES : (r + 1) * LANES]
            total[row] = value
            most = jnp.maximum(most, jnp.abs(value))
    peak = jnp.max(jnp.max(most, axis=0, keepdims=True), axis=1, keepdims=True)
    power = jnp.ceil(jnp.log2(jnp.maximum(peak, 1e-30) * (1.0 / 32000.0)))
    unit = jnp.broadcast_to(jnp.exp2(-power), (1, LANES))
    for row in range(rows):
        message[row * members : (row + 1) * members] = to_i16(total[row] * unit)
    at = rows * members
    message[at : at + packed.shape[0]] = packed[...]
    at = at + packed.shape[0]
    which = lax.broadcasted_iota(jnp.int32, meta.shape, 0)
    spot = meta.shape[0] - 1
    last = jnp.where(which == spot, jnp.broadcast_to(power, meta.shape).astype(jnp.int32), meta[...])
    message[at : at + meta.shape[0]] = last.astype(jnp.int16)


def unpack(ref, at, rows, members, chunks, level, mirror, drive, coef, seen, heavy):
    cells, base = rows * LANES, at + rows * members
    meta_at = base + chunks * members
    meta = from_i16(ref[meta_at : meta_at + META])
    unit = jnp.exp2(meta[META - 1 : META])
    spots = [jnp.where(mirror, rows - 1 - r, r) for r in range(rows)]
    for r, spot in enumerate(spots):
        start = at + r * members
        drive[spot] = from_i16(ref[start : start + members]) * unit
        spread = meta[2 * chunks + r : 2 * chunks + r + 1] * (1.0 / COEF_UNIT)
        coef[spot] = jnp.broadcast_to(spread, (8, LANES))
    weight = meta[chunks : 2 * chunks] * (1.0 / WEIGHT_UNIT)
    local = meta[0:chunks].astype(jnp.int32) - level * cells
    which = lax.broadcasted_iota(jnp.int32, (16, LANES), 0)
    total = jnp.zeros((2 * members + 16, cells), F32)
    for c in range(chunks):
        start = base + c * members
        value = from_i16(ref[start : start + members]) * (1.0 / VALUE_UNIT)
        high, low = halves(value * weight[c : c + 1])
        weight_high, weight_low = halves(weight[c : c + 1])
        ends = jnp.where(which == 0, weight_high, jnp.where(which == 1, weight_low, 0.0))
        left = jnp.concatenate([high, low, ends], axis=0).astype(BF)
        hit = lax.broadcasted_iota(jnp.int32, (cells, LANES), 0) == local[c : c + 1]
        total += lax.dot_general(
            left, jnp.where(hit, 1.0, 0.0).astype(BF), NT, preferred_element_type=F32
        )
    both = total[:members] + total[members : 2 * members]
    sums = total[2 * members : 2 * members + 1] + total[2 * members + 1 : 2 * members + 2]
    for r, spot in enumerate(spots):
        lanes = slice(r * LANES, (r + 1) * LANES)
        seen[spot] = both[:, lanes]
        heavy[spot] = jnp.broadcast_to(sums[:, lanes], (8, LANES))


def facing_tile(tiles):
    tile = lax.axis_index("tile")
    mirror = tile >= (tiles + 1) // 2
    return jnp.where(mirror, tiles - 1 - tile, tile), mirror


def prepare_kernel(tiles, sizes, masks, *refs):
    rows, members, chunks = sizes
    pieces, outs = refs[: len(masks)], refs[len(masks) :]
    (here, mirror), level = facing_tile(tiles), lax.axis_index("lev")
    for mask, (ref, at) in zip(masks, [(ref, 0) for ref in pieces]):
        tile = here ^ mask if len(masks) > 2 else (here & 1) ^ mask
        spot = pl.ds(tile * rows, rows)
        unpack(ref, at, rows, members, chunks, level, mirror, *[out.at[spot] for out in outs])


def target_sum(result, cov, offsets, target):
    blocks, band = cov.shape[0], cov.shape[1]
    total = None
    for i in range(max(0, target - band + 1), min(blocks - 1, target) + 1):
        part = jnp.dot(
            result[i], cov[i, inverse(offsets, i, target - i)], preferred_element_type=F32
        )
        total = part if total is None else total + part
    return total


def chain_kernel(
    tiles, sections, sizes, offsets, *refs
):
    rows, members, chunks = sizes
    early, own_section, late, (cov, result, keep, give) = refs[:4], refs[4:8], refs[8], refs[9:13]
    whole = refs[14:18]
    field, (drive, coef, seen, heavy) = refs[13], whole
    blocks, band, half, order = cov.shape
    (tile, mirror), section, level = facing_tile(tiles), lax.axis_index("sub"), lax.axis_index("lev")
    per_piece = rows * members + chunks * members + META
    pair = early[0].shape[0] // max(1, sections - 1)

    for target, source in zip(whole, own_section):
        target[section] = source[...]
    for ds in range(1, sections):
        base = pl.ds((tile & ~1) * rows, pair)
        for target, source in zip(whole, early):
            target[section ^ ds, base] = source[(ds - 1) * pair : ds * pair]
        for dt in range(2, tiles):
            at = ((ds - 1) * (tiles - 2) + dt - 2) * per_piece
            spot = pl.ds((tile ^ dt) * rows, rows)
            unpack(
                late, at, rows, members, chunks, level, mirror,
                *[target.at[section ^ ds, spot] for target in whole],
            )

    all_rows = tiles * rows
    zero = jnp.zeros((members, LANES), F32)
    field[0] = zero
    field[all_rows + 1] = zero

    def times(row_value, value):
        return (row_value[None] * value.reshape(members // 8, 8, LANES)).reshape(members, LANES)

    def beside(value):
        return pltpu.roll(value, 1, 1) + pltpu.roll(value, LANES - 1, 1)

    def reach(steps):
        return min(all_rows, (tiles + 1) // 2 * rows + steps)

    def over_rows(limit, step, carry):
        def on_tile(t, carry):
            for r in range(rows):
                if not isinstance(t, int) or t * rows + r < limit:
                    carry = step(t * rows + r, carry)
            return carry

        return loop(-(-limit // rows), on_tile, carry)

    def each_row(limit, step):
        def once(row, carry):
            step(row)
            return carry

        over_rows(limit, once, 0)

    def forward_step(sec, limit):
        def step(row, before):
            now = field[row + 1]
            around = before + field[row + 2] + beside(now) - 4.0 * now
            field[row + 1] = now + times(coef[sec, row], around)
            return now

        over_rows(limit, step, zero)

    def adjoint_step(sec, limit):
        def step(row, carry):
            before, now = carry
            if isinstance(row, int):
                after_row = min(row + 1, all_rows - 1)
            else:
                after_row = jnp.minimum(row + 1, all_rows - 1)
            after = times(coef[sec, after_row], field[row + 2])
            field[row + 1] = field[row + 1] + (before + after + beside(now) - 4.0 * now)
            return now, after

        over_rows(limit, step, (zero, times(coef[sec, 0], field[1])))

    for sec in range(sections):
        left = STEPS * (2 * sections - sec)

        def push(row):
            if sec == 0:
                field[row + 1] = drive[sec, row]
            else:
                field[row + 1] = field[row + 1] + drive[sec, row]

        each_row(reach(left), push)
        for j in range(STEPS):
            forward_step(sec, reach(left - 1 - j))

        def observe(row):
            drive[sec, row] = times(heavy[sec, row], field[row + 1]) - seen[sec, row]

        each_row(reach(STEPS * (sec + 1)), observe)

    for sec in range(sections - 1, -1, -1):
        left = STEPS * (sec + 1)

        def pull(row):
            if sec == sections - 1:
                field[row + 1] = drive[sec, row]
            else:
                field[row + 1] = field[row + 1] + drive[sec, row]

        each_row(reach(left), pull)
        for j in range(STEPS):
            adjoint_step(sec, reach(left - 1 - j))

        @pl.when(section == sec)
        def _():
            for r in range(rows):
                lane = (r % 2) * LANES
                spot = tile * rows + jnp.where(mirror, rows - 1 - r, r)
                result[r // 2, :, lane : lane + LANES] = field[spot + 1].astype(BF)

    def hand_out(kept_at, given_at):
        for target in (kept_at, kept_at + 1, given_at, given_at + 1):
            sums = target_sum(result, cov, offsets, target)
            out, first = (keep, kept_at) if target in (kept_at, kept_at + 1) else (give, given_at)
            for h in range(2):
                out[2 * h + target - first] = sums[:, h * half : (h + 1) * half]

    @pl.when(level == 0)
    def _():
        hand_out(blocks + 2, 0)

    @pl.when(level != 0)
    def _():
        hand_out(0, blocks + 2)


def core_kernel(offsets, result, cov, keep, give):
    blocks, band, half, order = cov.shape
    level = lax.axis_index("lev")
    for b in range(blocks):
        sums = target_sum(result, cov, offsets, b + 2)
        low, high = sums[:, :half], sums[:, half:]
        keep[b] = jnp.where(level == 0, low, high)
        give[b] = jnp.where(level == 0, high, low)


def final_kernel(control, kept, got, ghost, ghost_far, out, spare):
    rows, members = control.shape[0], control.shape[1]
    blocks, half = rows // 2, kept.shape[2]
    level = lax.axis_index("lev")
    for b in range(blocks):
        spare[b] = kept[b] + got[b]

    def add_ghosts(level_now):
        for b in range(2):
            near = ghost[2 * level_now + b].astype(F32)
            far = ghost_far[b].astype(F32)
            below, above = (far, near) if level_now == 0 else (near, far)
            spare[b] = spare[b] + below
            spare[blocks - 2 + b] = spare[blocks - 2 + b] + above

    @pl.when(level == 0)
    def _():
        add_ghosts(0)

    @pl.when(level != 0)
    def _():
        add_ghosts(1)

    for b in range(blocks):
        for r in range(2):
            row = 2 * b + r
            value = control[row].astype(F32) + spare[b, :, r * LANES : (r + 1) * LANES]
            out[pl.ds(row, members, stride=rows), :] = value


def body(
    model_error, start_state, covariance, offsets, diffusion, observed_cell, observed_count,
    observed_value, observed_weight,
):
    members, rows = model_error.shape[1], model_error.shape[3]
    blocks, band, half, order = covariance.shape
    tiles, sections = lax.axis_size("tile"), lax.axis_size("sub")
    slots = observed_cell.shape[2]
    level = lax.axis_index("lev")
    vmem, smem = pl.BlockSpec(memory_space=pltpu.VMEM), pl.BlockSpec(memory_space=pltpu.SMEM)
    hbm = pl.BlockSpec(memory_space=pltpu.HBM)

    control = model_error[0, :, 0].transpose(1, 0, 2)
    other = swap(control, "lev")
    chunks = slots // LANES
    sizes = (rows, members, chunks)
    offsets, edge, start, packed, meta, control_here = pl.pallas_call(
        stage_kernel,
        out_shape=[
            pltpu.SMEM(offsets.shape, jnp.int32),
            pltpu.VMEM((4, members, LANES), BF),
            pltpu.VMEM((members * rows, LANES), F32),
            pltpu.VMEM((chunks * members, LANES), jnp.int16),
            pltpu.VMEM((META, LANES), jnp.int32),
            pltpu.VMEM(control.shape, BF),
        ],
        in_specs=[hbm] * 8,
        out_specs=[smem] + [vmem] * 5,
        scratch_shapes=[
            pltpu.VMEM((rows, 1, LANES), F32),
            pltpu.VMEM((chunks, LANES), jnp.int32),
            pltpu.VMEM((chunks, LANES), F32),
            pltpu.VMEM((members, slots), F32),
            pltpu.SemaphoreType.DMA((7,)),
        ],
        compiler_params=pltpu.CompilerParams(vmem_limit_bytes=STAGE_ROOM),
        cost_estimate=pl.CostEstimate(flops=0, bytes_accessed=2 * 10**6, transcendentals=0),
        name="stage",
    )(
        offsets, control, start_state.reshape(members * rows, LANES),
        diffusion.reshape(rows, 1, LANES), observed_cell.reshape(chunks, LANES),
        observed_weight.reshape(chunks, LANES), observed_value[0, 0].T, covariance,
    )

    far_edge = lax.dynamic_slice_in_dim(other, jnp.where(level == 0, rows - 4, 0), 4)
    near = swap_facing(jnp.concatenate([edge, far_edge]))
    cov = covariance
    sums, meta = pl.pallas_call(
        functools.partial(own_kernel, chunks),
        out_shape=[
            pltpu.VMEM((rows, members, LANES), F32),
            pltpu.VMEM((META, LANES), jnp.int32),
        ],
        in_specs=[smem] * 2 + [vmem] * 5,
        out_specs=[vmem] * 2,
        scratch_shapes=[pltpu.VMEM((blocks, members, order), BF)],
        compiler_params=pltpu.CompilerParams(vmem_limit_bytes=OWN_ROOM),
        cost_estimate=pl.CostEstimate(flops=0, bytes_accessed=6 * 10**6, transcendentals=0),
        name="own",
    )(offsets, observed_count, start, meta, control_here, other, cov)

    near, sums = lax.optimization_barrier((near, sums))
    far = swap(near, "lev")
    message_rows = rows * members + chunks * members + META
    message = pl.pallas_call(
        forcing_kernel,
        out_shape=jax.ShapeDtypeStruct((message_rows, LANES), jnp.int16),
        in_specs=[smem] + [vmem] * 6,
        out_specs=vmem,
        scratch_shapes=[
            pltpu.VMEM((4, members, order), BF),
            pltpu.VMEM((rows, members, LANES), F32),
        ],
        compiler_params=pltpu.CompilerParams(vmem_limit_bytes=8 * MIB),
        name="forcing",
    )(offsets, near, far, sums, packed, meta, cov)

    pieces = [message] + [swap(message, "tile", d) for d in range(1, tiles)]
    early = [swap(piece, "sub", d) for d in range(1, sections) for piece in pieces[:2]]
    early, held = lax.optimization_barrier((early, pieces[2:]))
    late = jnp.concatenate(
        [swap(jnp.concatenate(held), "sub", d) for d in range(1, sections)]
    )

    all_rows = tiles * rows
    wide = (all_rows, members, LANES)
    flat = (all_rows, 8, LANES)
    room = 4 * all_rows * (members + 8) * LANES

    def prepare(arrays, masks, count):
        height = count * rows
        return pl.pallas_call(
            functools.partial(prepare_kernel, tiles, sizes, masks),
            out_shape=[
                jax.ShapeDtypeStruct((height, size, LANES), F32) for size in (members, 8) * 2
            ],
            in_specs=[vmem] * len(arrays),
            out_specs=[vmem] * 4,
            compiler_params=pltpu.CompilerParams(vmem_limit_bytes=6 * MIB + 2 * room),
            cost_estimate=pl.CostEstimate(
                flops=10**8 * count, bytes_accessed=10**6 * count, transcendentals=0
            ),
            name="prepare",
        )(*arrays)

    own_section = prepare(pieces, tuple(range(tiles)), tiles)
    others = [prepare(early[2 * d : 2 * d + 2], (0, 1), 2) for d in range(sections - 1)]
    early_section = [jnp.concatenate(group) for group in zip(*others)]

    result, keep, give = pl.pallas_call(
        functools.partial(chain_kernel, tiles, sections, sizes),
        out_shape=[jax.ShapeDtypeStruct((blocks, members, half), BF)]
        + [jax.ShapeDtypeStruct((4, members, half), F32)] * 2,
        in_specs=[smem] + [vmem] * 10,
        out_specs=[vmem] * 3,
        scratch_shapes=[
            pltpu.VMEM((all_rows + 2, members, LANES), F32),
            pltpu.VMEM((sections,) + wide, F32),
            pltpu.VMEM((sections,) + flat, F32),
            pltpu.VMEM((sections,) + wide, F32),
            pltpu.VMEM((sections,) + flat, F32),
        ],
        compiler_params=pltpu.CompilerParams(vmem_limit_bytes=6 * MIB + (3 * sections + 3) * room),
        name="chain",
    )(offsets, *early_section, *own_section, late, cov)

    ghost_got = swap(give, "lev")
    ghost = swap_facing((keep + ghost_got).astype(BF))
    kept, given = pl.pallas_call(
        core_kernel,
        out_shape=[jax.ShapeDtypeStruct((blocks, members, half), F32)] * 2,
        in_specs=[smem] + [vmem] * 2,
        out_specs=[vmem] * 2,
        compiler_params=pltpu.CompilerParams(vmem_limit_bytes=4 * MIB),
        cost_estimate=pl.CostEstimate(flops=10**9, bytes_accessed=8 * 10**6, transcendentals=0),
        name="core",
    )(offsets, result, cov)
    got = swap(given, "lev")
    ghost_far = swap(jnp.where(level == 0, ghost[2:], ghost[:2]), "lev")
    out = pl.pallas_call(
        final_kernel,
        out_shape=jax.ShapeDtypeStruct((members * rows, LANES), F32),
        in_specs=[vmem] * 5,
        out_specs=vmem,
        scratch_shapes=[pltpu.VMEM((blocks, members, half), F32)],
        compiler_params=pltpu.CompilerParams(vmem_limit_bytes=4 * MIB),
        name="final",
    )(control_here, kept, got, ghost, ghost_far)
    return out.reshape(1, members, 1, rows, LANES)


def solution(mesh):
    in_specs = (
        P("sub", "grp", "lev", "tile", None),
        P("grp", "lev", "tile", None),
        P("tile", None, "lev", None),
        P("tile", None),
        P("sub", "lev", "tile", None),
        P("sub", "tile", "grp"),
        P("sub", "tile", "grp"),
        P("sub", "tile", None, "grp"),
        P("sub", "tile", "grp"),
    )
    out_specs = P("sub", "grp", "lev", "tile", None)
    return jax.shard_map(body, mesh=mesh, in_specs=in_specs, out_specs=out_specs, check_vma=False)
```

```python
import functools

import jax
import jax.numpy as jnp
from jax import lax
from jax.experimental import pallas as pl
from jax.experimental.pallas import tpu as pltpu
from jax.sharding import PartitionSpec as P

STEPS = 4
LANES = 128
BF = jnp.bfloat16
F32 = jnp.float32
NT = (((1,), (1,)), ((), ()))
MIB = 2**20
META = 16
WEIGHT_UNIT, COEF_UNIT, VALUE_UNIT = 8191.0, 131072.0, 5461.0
STAGE_ROOM = 56 * MIB
OWN_ROOM = 16 * MIB


def swap(block, axis, mask=1):
    count = lax.axis_size(axis)
    return lax.ppermute(block, axis, [(i, i ^ mask) for i in range(count)])


def swap_facing(block):
    pairs = [(2 * t, 2 * (t + 1) + 1) for t in range(lax.axis_size("tile") - 1)]
    return lax.ppermute(block, ("tile", "lev"), pairs + [(b, a) for a, b in pairs])


def loop(count, step, carry):
    if count <= 4:
        for i in range(count):
            carry = step(i, carry)
        return carry
    return lax.fori_loop(0, count, step, carry)


def halves(value):
    high = value.astype(BF).astype(F32)
    return high, value - high


def to_i16(value):
    return jnp.round(value).astype(jnp.int32).astype(jnp.int16)


def from_i16(value):
    return value.astype(jnp.int32).astype(F32)


def inverse(offsets, i, wanted):
    found = 0
    for k in range(offsets.shape[1]):
        found = found + jnp.where(offsets[i, k] == wanted, k, 0)
    return found


def stage_kernel(
    offsets_hbm, own_hbm, start_hbm, diffusion_hbm, cells_hbm, weights_hbm, values_hbm, cov_hbm,
    offsets, edge, start, packed, meta, own, diffusion, cells, weights, values, sems,
):
    chunks, members, rows = cells.shape[0], values.shape[0], diffusion.shape[0]
    pairs = (
        (own_hbm, own), (diffusion_hbm, diffusion), (cells_hbm, cells), (weights_hbm, weights),
        (values_hbm, values), (offsets_hbm, offsets), (start_hbm, start),
    )
    copies = [
        pltpu.make_async_copy(source, target, sems.at[n]) for n, (source, target) in enumerate(pairs)
    ]
    for copy in copies:
        copy.start()
    for copy in copies:
        copy.wait()
    first = jnp.where(lax.axis_index("lev") == 0, rows - 4, 0)
    for r in range(4):
        edge[r] = own[first + r]
    meta[...] = jnp.zeros_like(meta)
    meta[0:chunks] = cells[...]
    meta[chunks : 2 * chunks] = jnp.round(weights[...] * WEIGHT_UNIT).astype(jnp.int32)
    for r in range(rows):
        spot = 2 * chunks + r
        meta[spot : spot + 1] = jnp.round(diffusion[r] * COEF_UNIT).astype(jnp.int32)
    for c in range(chunks):
        value = values[:, c * LANES : (c + 1) * LANES]
        packed[c * members : (c + 1) * members] = to_i16(value * VALUE_UNIT)


def own_kernel(chunks, offsets, count, start, meta, own, other, cov, sums, live_meta, control):
    blocks, band, half, order = cov.shape
    rows, members = own.shape[0], own.shape[1]
    section, level = lax.axis_index("sub"), lax.axis_index("lev")
    which = lax.broadcasted_iota(jnp.int32, meta.shape, 0)
    slot = (which - chunks) * LANES + lax.broadcasted_iota(jnp.int32, meta.shape, 1)
    weights = (which >= chunks) & (which < 2 * chunks)
    live_meta[...] = jnp.where(weights & (slot >= count[0, 0, 0]), 0, meta[...])
    for b in range(blocks):
        for r in range(2):
            mine, theirs = own[2 * b + r], other[2 * b + r]
            for part in range(2):
                lane = (part * 2 + r) * LANES
                value = jnp.where(level == part, mine.astype(F32), theirs.astype(F32))
                control[b, :, lane : lane + LANES] = value.astype(BF)
    first = jnp.where(section == 0, 1.0, 0.0).astype(F32)
    for i in range(blocks):
        total = jnp.zeros((members, half), F32)
        for b in range(max(0, i - 2), min(blocks, i + 3)):
            total += lax.dot_general(
                control[b], cov[i, inverse(offsets, i, b + 2 - i)], NT, preferred_element_type=F32
            )
        for r in range(2):
            row = 2 * i + r
            begin = start[pl.ds(row, members, stride=rows), :]
            sums[row] = total[:, r * LANES : (r + 1) * LANES] + first * begin


def forcing_kernel(offsets, near, far, sums, packed, meta, cov, message, control, total):
    blocks, band, half, order = cov.shape
    rows, members = sums.shape[0], sums.shape[1]
    level = lax.axis_index("lev")

    def fill(b, part, source, at):
        for r in range(2):
            lane = (part * 2 + r) * LANES
            control[b, :, lane : lane + LANES] = source[at + r]

    @pl.when(level == 0)
    def _():
        for b in range(2):
            fill(b, 0, far, 2 * b)
            fill(b, 1, far, 4 + 2 * b)
            fill(2 + b, 0, near, 4 + 2 * b)
            fill(2 + b, 1, near, 2 * b)

    @pl.when(level != 0)
    def _():
        for b in range(2):
            fill(b, 1, near, 4 + 2 * b)
            fill(b, 0, near, 2 * b)
            fill(2 + b, 1, far, 2 * b)
            fill(2 + b, 0, far, 4 + 2 * b)

    most = jnp.zeros((members, LANES), F32)
    for i in range(blocks):
        added = None
        for b, target in enumerate((0, 1, blocks + 2, blocks + 3)):
            if 0 <= target - i < band:
                part = lax.dot_general(
                    control[b], cov[i, inverse(offsets, i, target - i)], NT,
                    preferred_element_type=F32,
                )
                added = part if added is None else added + part
        for r in range(2):
            row = 2 * i + r
            value = sums[row]
            if added is not None:
                value = value + added[:, r * LANES : (r + 1) * LANES]
            total[row] = value
            most = jnp.maximum(most, jnp.abs(value))
    peak = jnp.max(jnp.max(most, axis=0, keepdims=True), axis=1, keepdims=True)
    power = jnp.ceil(jnp.log2(jnp.maximum(peak, 1e-30) * (1.0 / 32000.0)))
    unit = jnp.broadcast_to(jnp.exp2(-power), (1, LANES))
    for row in range(rows):
        message[row * members : (row + 1) * members] = to_i16(total[row] * unit)
    at = rows * members
    message[at : at + packed.shape[0]] = packed[...]
    at = at + packed.shape[0]
    which = lax.broadcasted_iota(jnp.int32, meta.shape, 0)
    spot = meta.shape[0] - 1
    last = jnp.where(which == spot, jnp.broadcast_to(power, meta.shape).astype(jnp.int32), meta[...])
    message[at : at + meta.shape[0]] = last.astype(jnp.int16)


def unpack(ref, at, rows, members, chunks, level, mirror, drive, coef, seen, heavy):
    cells, base = rows * LANES, at + rows * members
    meta_at = base + chunks * members
    meta = from_i16(ref[meta_at : meta_at + META])
    unit = jnp.exp2(meta[META - 1 : META])
    spots = [jnp.where(mirror, rows - 1 - r, r) for r in range(rows)]
    for r, spot in enumerate(spots):
        start = at + r * members
        drive[spot] = from_i16(ref[start : start + members]) * unit
        spread = meta[2 * chunks + r : 2 * chunks + r + 1] * (1.0 / COEF_UNIT)
        coef[spot] = jnp.broadcast_to(spread, (8, LANES))
    weight = meta[chunks : 2 * chunks] * (1.0 / WEIGHT_UNIT)
    local = meta[0:chunks].astype(jnp.int32) - level * cells
    which = lax.broadcasted_iota(jnp.int32, (16, LANES), 0)
    total = jnp.zeros((2 * members + 16, cells), F32)
    for c in range(chunks):
        start = base + c * members
        value = from_i16(ref[start : start + members]) * (1.0 / VALUE_UNIT)
        high, low = halves(value * weight[c : c + 1])
        weight_high, weight_low = halves(weight[c : c + 1])
        ends = jnp.where(which == 0, weight_high, jnp.where(which == 1, weight_low, 0.0))
        left = jnp.concatenate([high, low, ends], axis=0).astype(BF)
        hit = lax.broadcasted_iota(jnp.int32, (cells, LANES), 0) == local[c : c + 1]
        total += lax.dot_general(
            left, jnp.where(hit, 1.0, 0.0).astype(BF), NT, preferred_element_type=F32
        )
    both = total[:members] + total[members : 2 * members]
    sums = total[2 * members : 2 * members + 1] + total[2 * members + 1 : 2 * members + 2]
    for r, spot in enumerate(spots):
        lanes = slice(r * LANES, (r + 1) * LANES)
        seen[spot] = both[:, lanes]
        heavy[spot] = jnp.broadcast_to(sums[:, lanes], (8, LANES))


def facing_tile(tiles):
    tile = lax.axis_index("tile")
    mirror = tile >= (tiles + 1) // 2
    return jnp.where(mirror, tiles - 1 - tile, tile), mirror


def prepare_kernel(tiles, sizes, masks, *refs):
    rows, members, chunks = sizes
    pieces, outs = refs[: len(masks)], refs[len(masks) :]
    (here, mirror), level = facing_tile(tiles), lax.axis_index("lev")
    for mask, (ref, at) in zip(masks, [(ref, 0) for ref in pieces]):
        tile = here ^ mask if len(masks) > 2 else (here & 1) ^ mask
        spot = pl.ds(tile * rows, rows)
        unpack(ref, at, rows, members, chunks, level, mirror, *[out.at[spot] for out in outs])


def target_sum(result, cov, offsets, target):
    blocks, band = cov.shape[0], cov.shape[1]
    total = None
    for i in range(max(0, target - band + 1), min(blocks - 1, target) + 1):
        part = jnp.dot(
            result[i], cov[i, inverse(offsets, i, target - i)], preferred_element_type=F32
        )
        total = part if total is None else total + part
    return total


def chain_kernel(
    tiles, sections, sizes, offsets, *refs
):
    rows, members, chunks = sizes
    early, own_section, late, (cov, result, keep, give) = refs[:4], refs[4:8], refs[8], refs[9:13]
    whole = refs[14:18]
    field, (drive, coef, seen, heavy) = refs[13], whole
    blocks, band, half, order = cov.shape
    (tile, mirror), section, level = facing_tile(tiles), lax.axis_index("sub"), lax.axis_index("lev")
    per_piece = rows * members + chunks * members + META
    pair = early[0].shape[0] // max(1, sections - 1)

    for target, source in zip(whole, own_section):
        target[section] = source[...]
    for ds in range(1, sections):
        base = pl.ds((tile & ~1) * rows, pair)
        for target, source in zip(whole, early):
            target[section ^ ds, base] = source[(ds - 1) * pair : ds * pair]
        for dt in range(2, tiles):
            at = ((ds - 1) * (tiles - 2) + dt - 2) * per_piece
            spot = pl.ds((tile ^ dt) * rows, rows)
            unpack(
                late, at, rows, members, chunks, level, mirror,
                *[target.at[section ^ ds, spot] for target in whole],
            )

    all_rows = tiles * rows
    zero = jnp.zeros((members, LANES), F32)
    field[0] = zero
    field[all_rows + 1] = zero

    def times(row_value, value):
        return (row_value[None] * value.reshape(members // 8, 8, LANES)).reshape(members, LANES)

    def beside(value):
        return pltpu.roll(value, 1, 1) + pltpu.roll(value, LANES - 1, 1)

    def reach(steps):
        return min(all_rows, (tiles + 1) // 2 * rows + steps)

    def over_rows(limit, step, carry):
        def on_tile(t, carry):
            for r in range(rows):
                if not isinstance(t, int) or t * rows + r < limit:
                    carry = step(t * rows + r, carry)
            return carry

        return loop(-(-limit // rows), on_tile, carry)

    def each_row(limit, step):
        def once(row, carry):
            step(row)
            return carry

        over_rows(limit, once, 0)

    def forward_step(sec, limit):
        def step(row, before):
            now = field[row + 1]
            around = before + field[row + 2] + beside(now) - 4.0 * now
            field[row + 1] = now + times(coef[sec, row], around)
            return now

        over_rows(limit, step, zero)

    def adjoint_step(sec, limit):
        def step(row, carry):
            before, now = carry
            if isinstance(row, int):
                after_row = min(row + 1, all_rows - 1)
            else:
                after_row = jnp.minimum(row + 1, all_rows - 1)
            after = times(coef[sec, after_row], field[row + 2])
            field[row + 1] = field[row + 1] + (before + after + beside(now) - 4.0 * now)
            return now, after

        over_rows(limit, step, (zero, times(coef[sec, 0], field[1])))

    for sec in range(sections):
        left = STEPS * (2 * sections - sec)

        def push(row):
            if sec == 0:
                field[row + 1] = drive[sec, row]
            else:
                field[row + 1] = field[row + 1] + drive[sec, row]

        each_row(reach(left), push)
        for j in range(STEPS):
            forward_step(sec, reach(left - 1 - j))

        def observe(row):
            drive[sec, row] = times(heavy[sec, row], field[row + 1]) - seen[sec, row]

        each_row(reach(STEPS * (sec + 1)), observe)

    for sec in range(sections - 1, -1, -1):
        left = STEPS * (sec + 1)

        def pull(row):
            if sec == sections - 1:
                field[row + 1] = drive[sec, row]
            else:
                field[row + 1] = field[row + 1] + drive[sec, row]

        each_row(reach(left), pull)
        for j in range(STEPS):
            adjoint_step(sec, reach(left - 1 - j))

        @pl.when(section == sec)
        def _():
            for r in range(rows):
                lane = (r % 2) * LANES
                spot = tile * rows + jnp.where(mirror, rows - 1 - r, r)
                result[r // 2, :, lane : lane + LANES] = field[spot + 1].astype(BF)

    def hand_out(kept_at, given_at):
        for target in (kept_at, kept_at + 1, given_at, given_at + 1):
            sums = target_sum(result, cov, offsets, target)
            out, first = (keep, kept_at) if target in (kept_at, kept_at + 1) else (give, given_at)
            for h in range(2):
                out[2 * h + target - first] = sums[:, h * half : (h + 1) * half]

    @pl.when(level == 0)
    def _():
        hand_out(blocks + 2, 0)

    @pl.when(level != 0)
    def _():
        hand_out(0, blocks + 2)


def core_kernel(offsets, result, cov, keep, give):
    blocks, band, half, order = cov.shape
    level = lax.axis_index("lev")
    for b in range(blocks):
        sums = target_sum(result, cov, offsets, b + 2)
        low, high = sums[:, :half], sums[:, half:]
        keep[b] = jnp.where(level == 0, low, high)
        give[b] = jnp.where(level == 0, high, low)


def final_kernel(control, kept, got, ghost, ghost_far, out, spare):
    rows, members = control.shape[0], control.shape[1]
    blocks, half = rows // 2, kept.shape[2]
    level = lax.axis_index("lev")
    for b in range(blocks):
        spare[b] = kept[b] + got[b]

    def add_ghosts(level_now):
        for b in range(2):
            near = ghost[2 * level_now + b].astype(F32)
            far = ghost_far[b].astype(F32)
            below, above = (far, near) if level_now == 0 else (near, far)
            spare[b] = spare[b] + below
            spare[blocks - 2 + b] = spare[blocks - 2 + b] + above

    @pl.when(level == 0)
    def _():
        add_ghosts(0)

    @pl.when(level != 0)
    def _():
        add_ghosts(1)

    for b in range(blocks):
        for r in range(2):
            row = 2 * b + r
            value = control[row].astype(F32) + spare[b, :, r * LANES : (r + 1) * LANES]
            out[pl.ds(row, members, stride=rows), :] = value


def body(
    model_error, start_state, covariance, offsets, diffusion, observed_cell, observed_count,
    observed_value, observed_weight,
):
    members, rows = model_error.shape[1], model_error.shape[3]
    blocks, band, half, order = covariance.shape
    tiles, sections = lax.axis_size("tile"), lax.axis_size("sub")
    slots = observed_cell.shape[2]
    level = lax.axis_index("lev")
    vmem, smem = pl.BlockSpec(memory_space=pltpu.VMEM), pl.BlockSpec(memory_space=pltpu.SMEM)
    hbm = pl.BlockSpec(memory_space=pltpu.HBM)

    control = model_error[0, :, 0].transpose(1, 0, 2)
    other = swap(control, "lev")
    chunks = slots // LANES
    sizes = (rows, members, chunks)
    offsets, edge, start, packed, meta, control_here = pl.pallas_call(
        stage_kernel,
        out_shape=[
            pltpu.SMEM(offsets.shape, jnp.int32),
            pltpu.VMEM((4, members, LANES), BF),
            pltpu.VMEM((members * rows, LANES), F32),
            pltpu.VMEM((chunks * members, LANES), jnp.int16),
            pltpu.VMEM((META, LANES), jnp.int32),
            pltpu.VMEM(control.shape, BF),
        ],
        in_specs=[hbm] * 8,
        out_specs=[smem] + [vmem] * 5,
        scratch_shapes=[
            pltpu.VMEM((rows, 1, LANES), F32),
            pltpu.VMEM((chunks, LANES), jnp.int32),
            pltpu.VMEM((chunks, LANES), F32),
            pltpu.VMEM((members, slots), F32),
            pltpu.SemaphoreType.DMA((7,)),
        ],
        compiler_params=pltpu.CompilerParams(vmem_limit_bytes=STAGE_ROOM),
        cost_estimate=pl.CostEstimate(flops=0, bytes_accessed=2 * 10**6, transcendentals=0),
        name="stage",
    )(
        offsets, control, start_state.reshape(members * rows, LANES),
        diffusion.reshape(rows, 1, LANES), observed_cell.reshape(chunks, LANES),
        observed_weight.reshape(chunks, LANES), observed_value[0, 0].T, covariance,
    )

    far_edge = lax.dynamic_slice_in_dim(other, jnp.where(level == 0, rows - 4, 0), 4)
    near = swap_facing(jnp.concatenate([edge, far_edge]))
    cov = covariance
    sums, meta = pl.pallas_call(
        functools.partial(own_kernel, chunks),
        out_shape=[
            pltpu.VMEM((rows, members, LANES), F32),
            pltpu.VMEM((META, LANES), jnp.int32),
        ],
        in_specs=[smem] * 2 + [vmem] * 5,
        out_specs=[vmem] * 2,
        scratch_shapes=[pltpu.VMEM((blocks, members, order), BF)],
        compiler_params=pltpu.CompilerParams(vmem_limit_bytes=OWN_ROOM),
        cost_estimate=pl.CostEstimate(flops=0, bytes_accessed=6 * 10**6, transcendentals=0),
        name="own",
    )(offsets, observed_count, start, meta, control_here, other, cov)

    near, sums = lax.optimization_barrier((near, sums))
    far = swap(near, "lev")
    message_rows = rows * members + chunks * members + META
    message = pl.pallas_call(
        forcing_kernel,
        out_shape=jax.ShapeDtypeStruct((message_rows, LANES), jnp.int16),
        in_specs=[smem] + [vmem] * 6,
        out_specs=vmem,
        scratch_shapes=[
            pltpu.VMEM((4, members, order), BF),
            pltpu.VMEM((rows, members, LANES), F32),
        ],
        compiler_params=pltpu.CompilerParams(vmem_limit_bytes=8 * MIB),
        name="forcing",
    )(offsets, near, far, sums, packed, meta, cov)

    pieces = [message] + [swap(message, "tile", d) for d in range(1, tiles)]
    early = [swap(piece, "sub", d) for d in range(1, sections) for piece in pieces[:2]]
    early, held = lax.optimization_barrier((early, pieces[:1:-1]))
    late = jnp.concatenate(
        [swap(jnp.concatenate(held[::-1]), "sub", d) for d in range(1, sections)]
    )

    all_rows = tiles * rows
    wide = (all_rows, members, LANES)
    flat = (all_rows, 8, LANES)
    room = 4 * all_rows * (members + 8) * LANES

    def prepare(arrays, masks, count):
        height = count * rows
        return pl.pallas_call(
            functools.partial(prepare_kernel, tiles, sizes, masks),
            out_shape=[
                jax.ShapeDtypeStruct((height, size, LANES), F32) for size in (members, 8) * 2
            ],
            in_specs=[vmem] * len(arrays),
            out_specs=[vmem] * 4,
            compiler_params=pltpu.CompilerParams(vmem_limit_bytes=6 * MIB + 2 * room),
            cost_estimate=pl.CostEstimate(
                flops=10**8 * count, bytes_accessed=10**6 * count, transcendentals=0
            ),
            name="prepare",
        )(*arrays)

    own_section = prepare(pieces, tuple(range(tiles)), tiles)
    others = [prepare(early[2 * d : 2 * d + 2], (0, 1), 2) for d in range(sections - 1)]
    early_section = [jnp.concatenate(group) for group in zip(*others)]

    result, keep, give = pl.pallas_call(
        functools.partial(chain_kernel, tiles, sections, sizes),
        out_shape=[jax.ShapeDtypeStruct((blocks, members, half), BF)]
        + [jax.ShapeDtypeStruct((4, members, half), F32)] * 2,
        in_specs=[smem] + [vmem] * 10,
        out_specs=[vmem] * 3,
        scratch_shapes=[
            pltpu.VMEM((all_rows + 2, members, LANES), F32),
            pltpu.VMEM((sections,) + wide, F32),
            pltpu.VMEM((sections,) + flat, F32),
            pltpu.VMEM((sections,) + wide, F32),
            pltpu.VMEM((sections,) + flat, F32),
        ],
        compiler_params=pltpu.CompilerParams(vmem_limit_bytes=6 * MIB + (3 * sections + 3) * room),
        name="chain",
    )(offsets, *early_section, *own_section, late, cov)

    ghost_got = swap(give, "lev")
    ghost = swap_facing((keep + ghost_got).astype(BF))
    kept, given = pl.pallas_call(
        core_kernel,
        out_shape=[jax.ShapeDtypeStruct((blocks, members, half), F32)] * 2,
        in_specs=[smem] + [vmem] * 2,
        out_specs=[vmem] * 2,
        compiler_params=pltpu.CompilerParams(vmem_limit_bytes=4 * MIB),
        cost_estimate=pl.CostEstimate(flops=10**9, bytes_accessed=8 * 10**6, transcendentals=0),
        name="core",
    )(offsets, result, cov)
    got = swap(given, "lev")
    ghost_far = swap(jnp.where(level == 0, ghost[2:], ghost[:2]), "lev")
    out = pl.pallas_call(
        final_kernel,
        out_shape=jax.ShapeDtypeStruct((members * rows, LANES), F32),
        in_specs=[vmem] * 5,
        out_specs=vmem,
        scratch_shapes=[pltpu.VMEM((blocks, members, half), F32)],
        compiler_params=pltpu.CompilerParams(vmem_limit_bytes=4 * MIB),
        name="final",
    )(control_here, kept, got, ghost, ghost_far)
    return out.reshape(1, members, 1, rows, LANES)


def solution(mesh):
    in_specs = (
        P("sub", "grp", "lev", "tile", None),
        P("grp", "lev", "tile", None),
        P("tile", None, "lev", None),
        P("tile", None),
        P("sub", "lev", "tile", None),
        P("sub", "tile", "grp"),
        P("sub", "tile", "grp"),
        P("sub", "tile", None, "grp"),
        P("sub", "tile", "grp"),
    )
    out_specs = P("sub", "grp", "lev", "tile", None)
    return jax.shard_map(body, mesh=mesh, in_specs=in_specs, out_specs=out_specs, check_vma=False)
```

```python
import functools

import jax
import jax.numpy as jnp
from jax import lax
from jax.experimental import pallas as pl
from jax.experimental.pallas import tpu as pltpu
from jax.sharding import PartitionSpec as P

STEPS = 4
LANES = 128
BF = jnp.bfloat16
F32 = jnp.float32
NT = (((1,), (1,)), ((), ()))
MIB = 2**20
META = 16
WEIGHT_UNIT, COEF_UNIT, VALUE_UNIT = 8191.0, 131072.0, 5461.0
STAGE_ROOM = 56 * MIB
OWN_ROOM = 16 * MIB


def swap(block, axis, mask=1):
    count = lax.axis_size(axis)
    return lax.ppermute(block, axis, [(i, i ^ mask) for i in range(count)])


def swap_facing(block):
    pairs = [(2 * t, 2 * (t + 1) + 1) for t in range(lax.axis_size("tile") - 1)]
    return lax.ppermute(block, ("tile", "lev"), pairs + [(b, a) for a, b in pairs])


def loop(count, step, carry):
    if count <= 4:
        for i in range(count):
            carry = step(i, carry)
        return carry
    return lax.fori_loop(0, count, step, carry)


def halves(value):
    high = value.astype(BF).astype(F32)
    return high, value - high


def to_i16(value):
    return jnp.round(value).astype(jnp.int32).astype(jnp.int16)


def from_i16(value):
    return value.astype(jnp.int32).astype(F32)


def inverse(offsets, i, wanted):
    found = 0
    for k in range(offsets.shape[1]):
        found = found + jnp.where(offsets[i, k] == wanted, k, 0)
    return found


def stage_kernel(
    offsets_hbm, own_hbm, start_hbm, diffusion_hbm, cells_hbm, weights_hbm, values_hbm, cov_hbm,
    offsets, edge, start, packed, meta, own, diffusion, cells, weights, values, sems,
):
    chunks, members, rows = cells.shape[0], values.shape[0], diffusion.shape[0]
    pairs = (
        (own_hbm, own), (diffusion_hbm, diffusion), (cells_hbm, cells), (weights_hbm, weights),
        (values_hbm, values), (offsets_hbm, offsets), (start_hbm, start),
    )
    copies = [
        pltpu.make_async_copy(source, target, sems.at[n]) for n, (source, target) in enumerate(pairs)
    ]
    for copy in copies:
        copy.start()
    for copy in copies:
        copy.wait()
    first = jnp.where(lax.axis_index("lev") == 0, rows - 4, 0)
    for r in range(4):
        edge[r] = own[first + r]
    meta[...] = jnp.zeros_like(meta)
    meta[0:chunks] = cells[...]
    meta[chunks : 2 * chunks] = jnp.round(weights[...] * WEIGHT_UNIT).astype(jnp.int32)
    for r in range(rows):
        spot = 2 * chunks + r
        meta[spot : spot + 1] = jnp.round(diffusion[r] * COEF_UNIT).astype(jnp.int32)
    for c in range(chunks):
        value = values[:, c * LANES : (c + 1) * LANES]
        packed[c * members : (c + 1) * members] = to_i16(value * VALUE_UNIT)


def own_kernel(chunks, offsets, count, start, meta, own, other, cov, sums, live_meta, control):
    blocks, band, half, order = cov.shape
    rows, members = own.shape[0], own.shape[1]
    section, level = lax.axis_index("sub"), lax.axis_index("lev")
    which = lax.broadcasted_iota(jnp.int32, meta.shape, 0)
    slot = (which - chunks) * LANES + lax.broadcasted_iota(jnp.int32, meta.shape, 1)
    weights = (which >= chunks) & (which < 2 * chunks)
    live_meta[...] = jnp.where(weights & (slot >= count[0, 0, 0]), 0, meta[...])
    for b in range(blocks):
        for r in range(2):
            mine, theirs = own[2 * b + r], other[2 * b + r]
            for part in range(2):
                lane = (part * 2 + r) * LANES
                value = jnp.where(level == part, mine.astype(F32), theirs.astype(F32))
                control[b, :, lane : lane + LANES] = value.astype(BF)
    first = jnp.where(section == 0, 1.0, 0.0).astype(F32)
    for i in range(blocks):
        total = jnp.zeros((members, half), F32)
        for b in range(max(0, i - 2), min(blocks, i + 3)):
            total += lax.dot_general(
                control[b], cov[i, inverse(offsets, i, b + 2 - i)], NT, preferred_element_type=F32
            )
        for r in range(2):
            row = 2 * i + r
            begin = start[pl.ds(row, members, stride=rows), :]
            sums[row] = total[:, r * LANES : (r + 1) * LANES] + first * begin


def forcing_kernel(offsets, near, far, sums, packed, meta, cov, message, control, total):
    blocks, band, half, order = cov.shape
    rows, members = sums.shape[0], sums.shape[1]
    level = lax.axis_index("lev")

    def fill(b, part, source, at):
        for r in range(2):
            lane = (part * 2 + r) * LANES
            control[b, :, lane : lane + LANES] = source[at + r]

    @pl.when(level == 0)
    def _():
        for b in range(2):
            fill(b, 0, far, 2 * b)
            fill(b, 1, far, 4 + 2 * b)
            fill(2 + b, 0, near, 4 + 2 * b)
            fill(2 + b, 1, near, 2 * b)

    @pl.when(level != 0)
    def _():
        for b in range(2):
            fill(b, 1, near, 4 + 2 * b)
            fill(b, 0, near, 2 * b)
            fill(2 + b, 1, far, 2 * b)
            fill(2 + b, 0, far, 4 + 2 * b)

    most = jnp.zeros((members, LANES), F32)
    for i in range(blocks):
        added = None
        for b, target in enumerate((0, 1, blocks + 2, blocks + 3)):
            if 0 <= target - i < band:
                part = lax.dot_general(
                    control[b], cov[i, inverse(offsets, i, target - i)], NT,
                    preferred_element_type=F32,
                )
                added = part if added is None else added + part
        for r in range(2):
            row = 2 * i + r
            value = sums[row]
            if added is not None:
                value = value + added[:, r * LANES : (r + 1) * LANES]
            total[row] = value
            most = jnp.maximum(most, jnp.abs(value))
    peak = jnp.max(jnp.max(most, axis=0, keepdims=True), axis=1, keepdims=True)
    power = jnp.ceil(jnp.log2(jnp.maximum(peak, 1e-30) * (1.0 / 32000.0)))
    unit = jnp.broadcast_to(jnp.exp2(-power), (1, LANES))
    for row in range(rows):
        message[row * members : (row + 1) * members] = to_i16(total[row] * unit)
    at = rows * members
    message[at : at + packed.shape[0]] = packed[...]
    at = at + packed.shape[0]
    which = lax.broadcasted_iota(jnp.int32, meta.shape, 0)
    spot = meta.shape[0] - 1
    last = jnp.where(which == spot, jnp.broadcast_to(power, meta.shape).astype(jnp.int32), meta[...])
    message[at : at + meta.shape[0]] = last.astype(jnp.int16)


def unpack(ref, at, rows, members, chunks, level, mirror, drive, coef, seen, heavy):
    cells, base = rows * LANES, at + rows * members
    meta_at = base + chunks * members
    meta = from_i16(ref[meta_at : meta_at + META])
    unit = jnp.exp2(meta[META - 1 : META])
    spots = [jnp.where(mirror, rows - 1 - r, r) for r in range(rows)]
    for r, spot in enumerate(spots):
        start = at + r * members
        drive[spot] = from_i16(ref[start : start + members]) * unit
        spread = meta[2 * chunks + r : 2 * chunks + r + 1] * (1.0 / COEF_UNIT)
        coef[spot] = jnp.broadcast_to(spread, (8, LANES))
    weight = meta[chunks : 2 * chunks] * (1.0 / WEIGHT_UNIT)
    local = meta[0:chunks].astype(jnp.int32) - level * cells
    which = lax.broadcasted_iota(jnp.int32, (16, LANES), 0)
    total = jnp.zeros((2 * members + 16, cells), F32)
    for c in range(chunks):
        start = base + c * members
        value = from_i16(ref[start : start + members]) * (1.0 / VALUE_UNIT)
        high, low = halves(value * weight[c : c + 1])
        weight_high, weight_low = halves(weight[c : c + 1])
        ends = jnp.where(which == 0, weight_high, jnp.where(which == 1, weight_low, 0.0))
        left = jnp.concatenate([high, low, ends], axis=0).astype(BF)
        hit = lax.broadcasted_iota(jnp.int32, (cells, LANES), 0) == local[c : c + 1]
        total += lax.dot_general(
            left, jnp.where(hit, 1.0, 0.0).astype(BF), NT, preferred_element_type=F32
        )
    both = total[:members] + total[members : 2 * members]
    sums = total[2 * members : 2 * members + 1] + total[2 * members + 1 : 2 * members + 2]
    for r, spot in enumerate(spots):
        lanes = slice(r * LANES, (r + 1) * LANES)
        seen[spot] = both[:, lanes]
        heavy[spot] = jnp.broadcast_to(sums[:, lanes], (8, LANES))


def facing_tile(tiles):
    tile = lax.axis_index("tile")
    mirror = tile >= (tiles + 1) // 2
    return jnp.where(mirror, tiles - 1 - tile, tile), mirror


def prepare_kernel(tiles, sizes, masks, *refs):
    rows, members, chunks = sizes
    pieces, outs = refs[: len(masks)], refs[len(masks) :]
    (here, mirror), level = facing_tile(tiles), lax.axis_index("lev")
    for mask, (ref, at) in zip(masks, [(ref, 0) for ref in pieces]):
        tile = here ^ mask if len(masks) > 2 else (here & 1) ^ mask
        spot = pl.ds(tile * rows, rows)
        unpack(ref, at, rows, members, chunks, level, mirror, *[out.at[spot] for out in outs])


def target_sum(result, cov, offsets, target):
    blocks, band = cov.shape[0], cov.shape[1]
    total = None
    for i in range(max(0, target - band + 1), min(blocks - 1, target) + 1):
        part = jnp.dot(
            result[i], cov[i, inverse(offsets, i, target - i)], preferred_element_type=F32
        )
        total = part if total is None else total + part
    return total


def chain_kernel(
    tiles, sections, sizes, offsets, *refs
):
    rows, members, chunks = sizes
    early, own_section, late, (cov, result, keep, give) = refs[:4], refs[4:8], refs[8], refs[9:13]
    whole = refs[14:18]
    field, (drive, coef, seen, heavy) = refs[13], whole
    blocks, band, half, order = cov.shape
    (tile, mirror), section, level = facing_tile(tiles), lax.axis_index("sub"), lax.axis_index("lev")
    per_piece = rows * members + chunks * members + META
    pair = early[0].shape[0] // max(1, sections - 1)

    for target, source in zip(whole, own_section):
        target[section] = source[...]
    for ds in range(1, sections):
        base = pl.ds((tile & ~1) * rows, pair)
        for target, source in zip(whole, early):
            target[section ^ ds, base] = source[(ds - 1) * pair : ds * pair]
        for dt in range(2, tiles):
            at = ((ds - 1) * (tiles - 2) + dt - 2) * per_piece
            spot = pl.ds((tile ^ dt) * rows, rows)
            unpack(
                late, at, rows, members, chunks, level, mirror,
                *[target.at[section ^ ds, spot] for target in whole],
            )

    all_rows = tiles * rows
    zero = jnp.zeros((members, LANES), F32)
    field[0] = zero
    field[all_rows + 1] = zero

    def times(row_value, value):
        return (row_value[None] * value.reshape(members // 8, 8, LANES)).reshape(members, LANES)

    def beside(value):
        return pltpu.roll(value, 1, 1) + pltpu.roll(value, LANES - 1, 1)

    def reach(steps):
        return min(all_rows, (tiles + 1) // 2 * rows + steps)

    def over_rows(limit, step, carry):
        def on_tile(t, carry):
            for r in range(rows):
                if not isinstance(t, int) or t * rows + r < limit:
                    carry = step(t * rows + r, carry)
            return carry

        return loop(-(-limit // rows), on_tile, carry)

    def each_row(limit, step):
        def once(row, carry):
            step(row)
            return carry

        over_rows(limit, once, 0)

    def forward_step(sec, limit):
        def step(row, before):
            now = field[row + 1]
            around = before + field[row + 2] + beside(now) - 4.0 * now
            field[row + 1] = now + times(coef[sec, row], around)
            return now

        over_rows(limit, step, zero)

    def adjoint_step(sec, limit):
        def step(row, carry):
            before, now = carry
            if isinstance(row, int):
                after_row = min(row + 1, all_rows - 1)
            else:
                after_row = jnp.minimum(row + 1, all_rows - 1)
            after = times(coef[sec, after_row], field[row + 2])
            field[row + 1] = field[row + 1] + (before + after + beside(now) - 4.0 * now)
            return now, after

        over_rows(limit, step, (zero, times(coef[sec, 0], field[1])))

    for sec in range(sections):
        left = STEPS * (2 * sections - sec)

        def push(row):
            if sec == 0:
                field[row + 1] = drive[sec, row]
            else:
                field[row + 1] = field[row + 1] + drive[sec, row]

        each_row(reach(left), push)
        for j in range(STEPS):
            forward_step(sec, reach(left - 1 - j))

        def observe(row):
            drive[sec, row] = times(heavy[sec, row], field[row + 1]) - seen[sec, row]

        each_row(reach(STEPS * (sec + 1)), observe)

    for sec in range(sections - 1, -1, -1):
        left = STEPS * (sec + 1)

        def pull(row):
            if sec == sections - 1:
                field[row + 1] = drive[sec, row]
            else:
                field[row + 1] = field[row + 1] + drive[sec, row]

        each_row(reach(left), pull)
        for j in range(STEPS):
            adjoint_step(sec, reach(left - 1 - j))

        @pl.when(section == sec)
        def _():
            for r in range(rows):
                lane = (r % 2) * LANES
                spot = tile * rows + jnp.where(mirror, rows - 1 - r, r)
                result[r // 2, :, lane : lane + LANES] = field[spot + 1].astype(BF)

    def hand_out(kept_at, given_at):
        for target in (kept_at, kept_at + 1, given_at, given_at + 1):
            sums = target_sum(result, cov, offsets, target)
            out, first = (keep, kept_at) if target in (kept_at, kept_at + 1) else (give, given_at)
            for h in range(2):
                out[2 * h + target - first] = sums[:, h * half : (h + 1) * half].astype(out.dtype)

    @pl.when(level == 0)
    def _():
        hand_out(blocks + 2, 0)

    @pl.when(level != 0)
    def _():
        hand_out(0, blocks + 2)


def core_kernel(offsets, result, cov, keep, give):
    blocks, band, half, order = cov.shape
    level = lax.axis_index("lev")
    for b in range(blocks):
        sums = target_sum(result, cov, offsets, b + 2)
        low, high = sums[:, :half], sums[:, half:]
        keep[b] = jnp.where(level == 0, low, high)
        give[b] = jnp.where(level == 0, high, low)


def final_kernel(control, kept, got, ghost, ghost_far, out, spare):
    rows, members = control.shape[0], control.shape[1]
    blocks, half = rows // 2, kept.shape[2]
    level = lax.axis_index("lev")
    for b in range(blocks):
        spare[b] = kept[b] + got[b]

    def add_ghosts(level_now):
        for b in range(2):
            near = ghost[2 * level_now + b].astype(F32)
            far = ghost_far[b].astype(F32)
            below, above = (far, near) if level_now == 0 else (near, far)
            spare[b] = spare[b] + below
            spare[blocks - 2 + b] = spare[blocks - 2 + b] + above

    @pl.when(level == 0)
    def _():
        add_ghosts(0)

    @pl.when(level != 0)
    def _():
        add_ghosts(1)

    for b in range(blocks):
        for r in range(2):
            row = 2 * b + r
            value = control[row].astype(F32) + spare[b, :, r * LANES : (r + 1) * LANES]
            out[pl.ds(row, members, stride=rows), :] = value


def body(
    model_error, start_state, covariance, offsets, diffusion, observed_cell, observed_count,
    observed_value, observed_weight,
):
    members, rows = model_error.shape[1], model_error.shape[3]
    blocks, band, half, order = covariance.shape
    tiles, sections = lax.axis_size("tile"), lax.axis_size("sub")
    slots = observed_cell.shape[2]
    level = lax.axis_index("lev")
    vmem, smem = pl.BlockSpec(memory_space=pltpu.VMEM), pl.BlockSpec(memory_space=pltpu.SMEM)
    hbm = pl.BlockSpec(memory_space=pltpu.HBM)

    control = model_error[0, :, 0].transpose(1, 0, 2)
    other = swap(control, "lev")
    chunks = slots // LANES
    sizes = (rows, members, chunks)
    offsets, edge, start, packed, meta, control_here = pl.pallas_call(
        stage_kernel,
        out_shape=[
            pltpu.SMEM(offsets.shape, jnp.int32),
            pltpu.VMEM((4, members, LANES), BF),
            pltpu.VMEM((members * rows, LANES), F32),
            pltpu.VMEM((chunks * members, LANES), jnp.int16),
            pltpu.VMEM((META, LANES), jnp.int32),
            pltpu.VMEM(control.shape, BF),
        ],
        in_specs=[hbm] * 8,
        out_specs=[smem] + [vmem] * 5,
        scratch_shapes=[
            pltpu.VMEM((rows, 1, LANES), F32),
            pltpu.VMEM((chunks, LANES), jnp.int32),
            pltpu.VMEM((chunks, LANES), F32),
            pltpu.VMEM((members, slots), F32),
            pltpu.SemaphoreType.DMA((7,)),
        ],
        compiler_params=pltpu.CompilerParams(vmem_limit_bytes=STAGE_ROOM),
        cost_estimate=pl.CostEstimate(flops=0, bytes_accessed=2 * 10**6, transcendentals=0),
        name="stage",
    )(
        offsets, control, start_state.reshape(members * rows, LANES),
        diffusion.reshape(rows, 1, LANES), observed_cell.reshape(chunks, LANES),
        observed_weight.reshape(chunks, LANES), observed_value[0, 0].T, covariance,
    )

    far_edge = lax.dynamic_slice_in_dim(other, jnp.where(level == 0, rows - 4, 0), 4)
    near = swap_facing(jnp.concatenate([edge, far_edge]))
    cov = covariance
    sums, meta = pl.pallas_call(
        functools.partial(own_kernel, chunks),
        out_shape=[
            pltpu.VMEM((rows, members, LANES), F32),
            pltpu.VMEM((META, LANES), jnp.int32),
        ],
        in_specs=[smem] * 2 + [vmem] * 5,
        out_specs=[vmem] * 2,
        scratch_shapes=[pltpu.VMEM((blocks, members, order), BF)],
        compiler_params=pltpu.CompilerParams(vmem_limit_bytes=OWN_ROOM),
        cost_estimate=pl.CostEstimate(flops=0, bytes_accessed=6 * 10**6, transcendentals=0),
        name="own",
    )(offsets, observed_count, start, meta, control_here, other, cov)

    near, sums = lax.optimization_barrier((near, sums))
    far = swap(near, "lev")
    message_rows = rows * members + chunks * members + META
    message = pl.pallas_call(
        forcing_kernel,
        out_shape=jax.ShapeDtypeStruct((message_rows, LANES), jnp.int16),
        in_specs=[smem] + [vmem] * 6,
        out_specs=vmem,
        scratch_shapes=[
            pltpu.VMEM((4, members, order), BF),
            pltpu.VMEM((rows, members, LANES), F32),
        ],
        compiler_params=pltpu.CompilerParams(vmem_limit_bytes=8 * MIB),
        name="forcing",
    )(offsets, near, far, sums, packed, meta, cov)

    pieces = [message] + [swap(message, "tile", d) for d in range(1, tiles)]
    early = [swap(piece, "sub", d) for d in range(1, sections) for piece in pieces[:2]]
    early, held = lax.optimization_barrier((early, pieces[:1:-1]))
    late = jnp.concatenate(
        [swap(jnp.concatenate(held[::-1]), "sub", d) for d in range(1, sections)]
    )

    all_rows = tiles * rows
    wide = (all_rows, members, LANES)
    flat = (all_rows, 8, LANES)
    room = 4 * all_rows * (members + 8) * LANES

    def prepare(arrays, masks, count):
        height = count * rows
        return pl.pallas_call(
            functools.partial(prepare_kernel, tiles, sizes, masks),
            out_shape=[
                jax.ShapeDtypeStruct((height, size, LANES), F32) for size in (members, 8) * 2
            ],
            in_specs=[vmem] * len(arrays),
            out_specs=[vmem] * 4,
            compiler_params=pltpu.CompilerParams(vmem_limit_bytes=6 * MIB + 2 * room),
            cost_estimate=pl.CostEstimate(
                flops=10**8 * count, bytes_accessed=10**6 * count, transcendentals=0
            ),
            name="prepare",
        )(*arrays)

    own_section = prepare(pieces, tuple(range(tiles)), tiles)
    others = [prepare(early[2 * d : 2 * d + 2], (0, 1), 2) for d in range(sections - 1)]
    early_section = [jnp.concatenate(group) for group in zip(*others)]

    result, keep, give = pl.pallas_call(
        functools.partial(chain_kernel, tiles, sections, sizes),
        out_shape=[jax.ShapeDtypeStruct((blocks, members, half), BF)]
        + [jax.ShapeDtypeStruct((4, members, half), kind) for kind in (F32, BF)],
        in_specs=[smem] + [vmem] * 10,
        out_specs=[vmem] * 3,
        scratch_shapes=[
            pltpu.VMEM((all_rows + 2, members, LANES), F32),
            pltpu.VMEM((sections,) + wide, F32),
            pltpu.VMEM((sections,) + flat, F32),
            pltpu.VMEM((sections,) + wide, F32),
            pltpu.VMEM((sections,) + flat, F32),
        ],
        compiler_params=pltpu.CompilerParams(vmem_limit_bytes=6 * MIB + (3 * sections + 3) * room),
        name="chain",
    )(offsets, *early_section, *own_section, late, cov)

    ghost_got = swap(give, "lev")
    ghost = swap_facing((keep + ghost_got).astype(BF))
    kept, given = pl.pallas_call(
        core_kernel,
        out_shape=[jax.ShapeDtypeStruct((blocks, members, half), F32)] * 2,
        in_specs=[smem] + [vmem] * 2,
        out_specs=[vmem] * 2,
        compiler_params=pltpu.CompilerParams(vmem_limit_bytes=4 * MIB),
        cost_estimate=pl.CostEstimate(flops=10**9, bytes_accessed=8 * 10**6, transcendentals=0),
        name="core",
    )(offsets, result, cov)
    got = swap(given, "lev")
    ghost_far = swap(jnp.where(level == 0, ghost[2:], ghost[:2]), "lev")
    out = pl.pallas_call(
        final_kernel,
        out_shape=jax.ShapeDtypeStruct((members * rows, LANES), F32),
        in_specs=[vmem] * 5,
        out_specs=vmem,
        scratch_shapes=[pltpu.VMEM((blocks, members, half), F32)],
        compiler_params=pltpu.CompilerParams(vmem_limit_bytes=4 * MIB),
        name="final",
    )(control_here, kept, got, ghost, ghost_far)
    return out.reshape(1, members, 1, rows, LANES)


def solution(mesh):
    in_specs = (
        P("sub", "grp", "lev", "tile", None),
        P("grp", "lev", "tile", None),
        P("tile", None, "lev", None),
        P("tile", None),
        P("sub", "lev", "tile", None),
        P("sub", "tile", "grp"),
        P("sub", "tile", "grp"),
        P("sub", "tile", None, "grp"),
        P("sub", "tile", "grp"),
    )
    out_specs = P("sub", "grp", "lev", "tile", None)
    return jax.shard_map(body, mesh=mesh, in_specs=in_specs, out_specs=out_specs, check_vma=False)
```

```python
import functools

import jax
import jax.numpy as jnp
from jax import lax
from jax.experimental import pallas as pl
from jax.experimental.pallas import tpu as pltpu
from jax.sharding import PartitionSpec as P

STEPS = 4
LANES = 128
BF = jnp.bfloat16
F32 = jnp.float32
NT = (((1,), (1,)), ((), ()))
MIB = 2**20
META = 16
WEIGHT_UNIT, COEF_UNIT, VALUE_UNIT = 8191.0, 131072.0, 5461.0
STAGE_ROOM = 56 * MIB
OWN_ROOM = 16 * MIB


def swap(block, axis, mask=1):
    count = lax.axis_size(axis)
    return lax.ppermute(block, axis, [(i, i ^ mask) for i in range(count)])


def swap_facing(block):
    pairs = [(2 * t, 2 * (t + 1) + 1) for t in range(lax.axis_size("tile") - 1)]
    return lax.ppermute(block, ("tile", "lev"), pairs + [(b, a) for a, b in pairs])


def loop(count, step, carry):
    if count <= 4:
        for i in range(count):
            carry = step(i, carry)
        return carry
    return lax.fori_loop(0, count, step, carry)


def halves(value):
    high = value.astype(BF).astype(F32)
    return high, value - high


def to_i16(value):
    return jnp.round(value).astype(jnp.int32).astype(jnp.int16)


def from_i16(value):
    return value.astype(jnp.int32).astype(F32)


def inverse(offsets, i, wanted):
    found = 0
    for k in range(offsets.shape[1]):
        found = found + jnp.where(offsets[i, k] == wanted, k, 0)
    return found


def stage_kernel(
    offsets_hbm, own_hbm, start_hbm, diffusion_hbm, cells_hbm, weights_hbm, values_hbm, cov_hbm,
    offsets, edge, start, packed, meta, own, diffusion, cells, weights, values, sems,
):
    chunks, members, rows = cells.shape[0], values.shape[0], diffusion.shape[0]
    pairs = (
        (own_hbm, own), (diffusion_hbm, diffusion), (cells_hbm, cells), (weights_hbm, weights),
        (values_hbm, values), (offsets_hbm, offsets), (start_hbm, start),
    )
    copies = [
        pltpu.make_async_copy(source, target, sems.at[n]) for n, (source, target) in enumerate(pairs)
    ]
    for copy in copies:
        copy.start()
    for copy in copies:
        copy.wait()
    first = jnp.where(lax.axis_index("lev") == 0, rows - 4, 0)
    for r in range(4):
        edge[r] = own[first + r]
    meta[...] = jnp.zeros_like(meta)
    meta[0:chunks] = cells[...]
    meta[chunks : 2 * chunks] = jnp.round(weights[...] * WEIGHT_UNIT).astype(jnp.int32)
    for r in range(rows):
        spot = 2 * chunks + r
        meta[spot : spot + 1] = jnp.round(diffusion[r] * COEF_UNIT).astype(jnp.int32)
    for c in range(chunks):
        value = values[:, c * LANES : (c + 1) * LANES]
        packed[c * members : (c + 1) * members] = to_i16(value * VALUE_UNIT)


def own_kernel(chunks, offsets, count, start, meta, own, other, cov, sums, live_meta, control):
    blocks, band, half, order = cov.shape
    rows, members = own.shape[0], own.shape[1]
    section, level = lax.axis_index("sub"), lax.axis_index("lev")
    which = lax.broadcasted_iota(jnp.int32, meta.shape, 0)
    slot = (which - chunks) * LANES + lax.broadcasted_iota(jnp.int32, meta.shape, 1)
    weights = (which >= chunks) & (which < 2 * chunks)
    live_meta[...] = jnp.where(weights & (slot >= count[0, 0, 0]), 0, meta[...])
    for b in range(blocks):
        for r in range(2):
            mine, theirs = own[2 * b + r], other[2 * b + r]
            for part in range(2):
                lane = (part * 2 + r) * LANES
                value = jnp.where(level == part, mine.astype(F32), theirs.astype(F32))
                control[b, :, lane : lane + LANES] = value.astype(BF)
    first = jnp.where(section == 0, 1.0, 0.0).astype(F32)
    for i in range(blocks):
        total = jnp.zeros((members, half), F32)
        for b in range(max(0, i - 2), min(blocks, i + 3)):
            total += lax.dot_general(
                control[b], cov[i, inverse(offsets, i, b + 2 - i)], NT, preferred_element_type=F32
            )
        for r in range(2):
            row = 2 * i + r
            begin = start[pl.ds(row, members, stride=rows), :]
            sums[row] = total[:, r * LANES : (r + 1) * LANES] + first * begin


def forcing_kernel(offsets, near, far, sums, packed, meta, cov, message, control, total):
    blocks, band, half, order = cov.shape
    rows, members = sums.shape[0], sums.shape[1]
    level = lax.axis_index("lev")

    def fill(b, part, source, at):
        for r in range(2):
            lane = (part * 2 + r) * LANES
            control[b, :, lane : lane + LANES] = source[at + r]

    @pl.when(level == 0)
    def _():
        for b in range(2):
            fill(b, 0, far, 2 * b)
            fill(b, 1, far, 4 + 2 * b)
            fill(2 + b, 0, near, 4 + 2 * b)
            fill(2 + b, 1, near, 2 * b)

    @pl.when(level != 0)
    def _():
        for b in range(2):
            fill(b, 1, near, 4 + 2 * b)
            fill(b, 0, near, 2 * b)
            fill(2 + b, 1, far, 2 * b)
            fill(2 + b, 0, far, 4 + 2 * b)

    most = jnp.zeros((members, LANES), F32)
    for i in range(blocks):
        added = None
        for b, target in enumerate((0, 1, blocks + 2, blocks + 3)):
            if 0 <= target - i < band:
                part = lax.dot_general(
                    control[b], cov[i, inverse(offsets, i, target - i)], NT,
                    preferred_element_type=F32,
                )
                added = part if added is None else added + part
        for r in range(2):
            row = 2 * i + r
            value = sums[row]
            if added is not None:
                value = value + added[:, r * LANES : (r + 1) * LANES]
            total[row] = value
            most = jnp.maximum(most, jnp.abs(value))
    peak = jnp.max(jnp.max(most, axis=0, keepdims=True), axis=1, keepdims=True)
    power = jnp.ceil(jnp.log2(jnp.maximum(peak, 1e-30) * (1.0 / 32000.0)))
    unit = jnp.broadcast_to(jnp.exp2(-power), (1, LANES))
    for row in range(rows):
        message[row * members : (row + 1) * members] = to_i16(total[row] * unit)
    at = rows * members
    message[at : at + packed.shape[0]] = packed[...]
    at = at + packed.shape[0]
    which = lax.broadcasted_iota(jnp.int32, meta.shape, 0)
    spot = meta.shape[0] - 1
    last = jnp.where(which == spot, jnp.broadcast_to(power, meta.shape).astype(jnp.int32), meta[...])
    message[at : at + meta.shape[0]] = last.astype(jnp.int16)


def unpack(ref, at, rows, members, chunks, level, mirror, drive, coef, seen, heavy):
    cells, base = rows * LANES, at + rows * members
    meta_at = base + chunks * members
    meta = from_i16(ref[meta_at : meta_at + META])
    unit = jnp.exp2(meta[META - 1 : META])
    spots = [jnp.where(mirror, rows - 1 - r, r) for r in range(rows)]
    for r, spot in enumerate(spots):
        start = at + r * members
        drive[spot] = from_i16(ref[start : start + members]) * unit
        spread = meta[2 * chunks + r : 2 * chunks + r + 1] * (1.0 / COEF_UNIT)
        coef[spot] = jnp.broadcast_to(spread, (8, LANES))
    weight = meta[chunks : 2 * chunks] * (1.0 / WEIGHT_UNIT)
    local = meta[0:chunks].astype(jnp.int32) - level * cells
    which = lax.broadcasted_iota(jnp.int32, (16, LANES), 0)
    total = jnp.zeros((2 * members + 16, cells), F32)
    for c in range(chunks):
        start = base + c * members
        value = from_i16(ref[start : start + members]) * (1.0 / VALUE_UNIT)
        high, low = halves(value * weight[c : c + 1])
        weight_high, weight_low = halves(weight[c : c + 1])
        ends = jnp.where(which == 0, weight_high, jnp.where(which == 1, weight_low, 0.0))
        left = jnp.concatenate([high, low, ends], axis=0).astype(BF)
        hit = lax.broadcasted_iota(jnp.int32, (cells, LANES), 0) == local[c : c + 1]
        total += lax.dot_general(
            left, jnp.where(hit, 1.0, 0.0).astype(BF), NT, preferred_element_type=F32
        )
    both = total[:members] + total[members : 2 * members]
    sums = total[2 * members : 2 * members + 1] + total[2 * members + 1 : 2 * members + 2]
    for r, spot in enumerate(spots):
        lanes = slice(r * LANES, (r + 1) * LANES)
        seen[spot] = both[:, lanes]
        heavy[spot] = jnp.broadcast_to(sums[:, lanes], (8, LANES))


def facing_tile(tiles):
    tile = lax.axis_index("tile")
    mirror = tile >= (tiles + 1) // 2
    return jnp.where(mirror, tiles - 1 - tile, tile), mirror


def prepare_kernel(tiles, sizes, masks, *refs):
    rows, members, chunks = sizes
    pieces, outs = refs[: len(masks)], refs[len(masks) :]
    (here, mirror), level = facing_tile(tiles), lax.axis_index("lev")
    for mask, (ref, at) in zip(masks, [(ref, 0) for ref in pieces]):
        tile = here ^ mask if len(masks) > 2 else (here & 1) ^ mask
        spot = pl.ds(tile * rows, rows)
        unpack(ref, at, rows, members, chunks, level, mirror, *[out.at[spot] for out in outs])


def target_sum(result, cov, offsets, target):
    blocks, band = cov.shape[0], cov.shape[1]
    total = None
    for i in range(max(0, target - band + 1), min(blocks - 1, target) + 1):
        part = jnp.dot(
            result[i], cov[i, inverse(offsets, i, target - i)], preferred_element_type=F32
        )
        total = part if total is None else total + part
    return total


def chain_kernel(
    tiles, sections, sizes, offsets, *refs
):
    rows, members, chunks = sizes
    early, own_section, late, (cov, result, keep, give) = refs[:4], refs[4:8], refs[8], refs[9:13]
    whole = refs[14:18]
    field, (drive, coef, seen, heavy) = refs[13], whole
    blocks, band, half, order = cov.shape
    (tile, mirror), section, level = facing_tile(tiles), lax.axis_index("sub"), lax.axis_index("lev")
    per_piece = rows * members + chunks * members + META
    pair = early[0].shape[0] // max(1, sections - 1)

    for target, source in zip(whole, own_section):
        target[section] = source[...]
    for ds in range(1, sections):
        base = pl.ds((tile & ~1) * rows, pair)
        for target, source in zip(whole, early):
            target[section ^ ds, base] = source[(ds - 1) * pair : ds * pair]
        for dt in range(2, tiles):
            at = ((ds - 1) * (tiles - 2) + dt - 2) * per_piece
            spot = pl.ds((tile ^ dt) * rows, rows)
            unpack(
                late, at, rows, members, chunks, level, mirror,
                *[target.at[section ^ ds, spot] for target in whole],
            )

    all_rows = tiles * rows
    zero = jnp.zeros((members, LANES), F32)
    field[0] = zero
    field[all_rows + 1] = zero

    def times(row_value, value):
        return (row_value[None] * value.reshape(members // 8, 8, LANES)).reshape(members, LANES)

    def beside(value):
        return pltpu.roll(value, 1, 1) + pltpu.roll(value, LANES - 1, 1)

    def reach(steps):
        return min(all_rows, (tiles + 1) // 2 * rows + steps)

    def over_rows(limit, step, carry):
        def on_tile(t, carry):
            for r in range(rows):
                if not isinstance(t, int) or t * rows + r < limit:
                    carry = step(t * rows + r, carry)
            return carry

        return loop(-(-limit // rows), on_tile, carry)

    def each_row(limit, step):
        def once(row, carry):
            step(row)
            return carry

        over_rows(limit, once, 0)

    def forward_step(sec, limit):
        def step(row, before):
            now = field[row + 1]
            around = before + field[row + 2] + beside(now) - 4.0 * now
            field[row + 1] = now + times(coef[sec, row], around)
            return now

        over_rows(limit, step, zero)

    def adjoint_step(sec, limit):
        def step(row, carry):
            before, now = carry
            if isinstance(row, int):
                after_row = min(row + 1, all_rows - 1)
            else:
                after_row = jnp.minimum(row + 1, all_rows - 1)
            after = times(coef[sec, after_row], field[row + 2])
            field[row + 1] = field[row + 1] + (before + after + beside(now) - 4.0 * now)
            return now, after

        over_rows(limit, step, (zero, times(coef[sec, 0], field[1])))

    for sec in range(sections):
        left = STEPS * (2 * sections - sec)

        def push(row):
            if sec == 0:
                field[row + 1] = drive[sec, row]
            else:
                field[row + 1] = field[row + 1] + drive[sec, row]

        each_row(reach(left), push)
        for j in range(STEPS):
            forward_step(sec, reach(left - 1 - j))

        def observe(row):
            drive[sec, row] = times(heavy[sec, row], field[row + 1]) - seen[sec, row]

        each_row(reach(STEPS * (sec + 1)), observe)

    for sec in range(sections - 1, -1, -1):
        left = STEPS * (sec + 1)

        def pull(row):
            if sec == sections - 1:
                field[row + 1] = drive[sec, row]
            else:
                field[row + 1] = field[row + 1] + drive[sec, row]

        each_row(reach(left), pull)
        for j in range(STEPS):
            adjoint_step(sec, reach(left - 1 - j))

        @pl.when(section == sec)
        def _():
            for r in range(rows):
                lane = (r % 2) * LANES
                spot = tile * rows + jnp.where(mirror, rows - 1 - r, r)
                result[r // 2, :, lane : lane + LANES] = field[spot + 1].astype(BF)

    def hand_out(kept_at, given_at):
        for target in (kept_at, kept_at + 1, given_at, given_at + 1):
            sums = target_sum(result, cov, offsets, target)
            out, first = (keep, kept_at) if target in (kept_at, kept_at + 1) else (give, given_at)
            for h in range(2):
                out[2 * h + target - first] = sums[:, h * half : (h + 1) * half]

    @pl.when(level == 0)
    def _():
        hand_out(blocks + 2, 0)

    @pl.when(level != 0)
    def _():
        hand_out(0, blocks + 2)


def core_kernel(offsets, result, cov, keep, give):
    blocks, band, half, order = cov.shape
    level = lax.axis_index("lev")
    for b in range(blocks):
        sums = target_sum(result, cov, offsets, b + 2)
        low, high = sums[:, :half], sums[:, half:]
        keep[b] = jnp.where(level == 0, low, high)
        give[b] = jnp.where(level == 0, high, low)


def final_kernel(control, kept, got, ghost, ghost_far, out, spare):
    rows, members = control.shape[0], control.shape[1]
    blocks, half = rows // 2, kept.shape[2]
    level = lax.axis_index("lev")
    for b in range(blocks):
        spare[b] = kept[b] + got[b]

    def add_ghosts(level_now):
        for b in range(2):
            near = ghost[2 * level_now + b].astype(F32)
            far = ghost_far[b].astype(F32)
            below, above = (far, near) if level_now == 0 else (near, far)
            spare[b] = spare[b] + below
            spare[blocks - 2 + b] = spare[blocks - 2 + b] + above

    @pl.when(level == 0)
    def _():
        add_ghosts(0)

    @pl.when(level != 0)
    def _():
        add_ghosts(1)

    for b in range(blocks):
        for r in range(2):
            row = 2 * b + r
            value = control[row].astype(F32) + spare[b, :, r * LANES : (r + 1) * LANES]
            out[pl.ds(row, members, stride=rows), :] = value


def body(
    model_error, start_state, covariance, offsets, diffusion, observed_cell, observed_count,
    observed_value, observed_weight,
):
    members, rows = model_error.shape[1], model_error.shape[3]
    blocks, band, half, order = covariance.shape
    tiles, sections = lax.axis_size("tile"), lax.axis_size("sub")
    slots = observed_cell.shape[2]
    level = lax.axis_index("lev")
    vmem, smem = pl.BlockSpec(memory_space=pltpu.VMEM), pl.BlockSpec(memory_space=pltpu.SMEM)
    hbm = pl.BlockSpec(memory_space=pltpu.HBM)

    control = model_error[0, :, 0].transpose(1, 0, 2)
    other = swap(control, "lev")
    chunks = slots // LANES
    sizes = (rows, members, chunks)
    offsets, edge, start, packed, meta, control_here = pl.pallas_call(
        stage_kernel,
        out_shape=[
            pltpu.SMEM(offsets.shape, jnp.int32),
            pltpu.VMEM((4, members, LANES), BF),
            pltpu.VMEM((members * rows, LANES), F32),
            pltpu.VMEM((chunks * members, LANES), jnp.int16),
            pltpu.VMEM((META, LANES), jnp.int32),
            pltpu.VMEM(control.shape, BF),
        ],
        in_specs=[hbm] * 8,
        out_specs=[smem] + [vmem] * 5,
        scratch_shapes=[
            pltpu.VMEM((rows, 1, LANES), F32),
            pltpu.VMEM((chunks, LANES), jnp.int32),
            pltpu.VMEM((chunks, LANES), F32),
            pltpu.VMEM((members, slots), F32),
            pltpu.SemaphoreType.DMA((7,)),
        ],
        compiler_params=pltpu.CompilerParams(vmem_limit_bytes=STAGE_ROOM),
        cost_estimate=pl.CostEstimate(flops=0, bytes_accessed=2 * 10**6, transcendentals=0),
        name="stage",
    )(
        offsets, control, start_state.reshape(members * rows, LANES),
        diffusion.reshape(rows, 1, LANES), observed_cell.reshape(chunks, LANES),
        observed_weight.reshape(chunks, LANES), observed_value[0, 0].T, covariance,
    )

    far_edge = lax.dynamic_slice_in_dim(other, jnp.where(level == 0, rows - 4, 0), 4)
    near = swap_facing(jnp.concatenate([edge, far_edge]))
    cov = covariance
    sums, meta = pl.pallas_call(
        functools.partial(own_kernel, chunks),
        out_shape=[
            pltpu.VMEM((rows, members, LANES), F32),
            pltpu.VMEM((META, LANES), jnp.int32),
        ],
        in_specs=[smem] * 2 + [vmem] * 5,
        out_specs=[vmem] * 2,
        scratch_shapes=[pltpu.VMEM((blocks, members, order), BF)],
        compiler_params=pltpu.CompilerParams(vmem_limit_bytes=OWN_ROOM),
        cost_estimate=pl.CostEstimate(flops=0, bytes_accessed=6 * 10**6, transcendentals=0),
        name="own",
    )(offsets, observed_count, start, meta, control_here, other, cov)

    near, sums = lax.optimization_barrier((near, sums))
    far = swap(near, "lev")
    message_rows = rows * members + chunks * members + META
    message = pl.pallas_call(
        forcing_kernel,
        out_shape=jax.ShapeDtypeStruct((message_rows, LANES), jnp.int16),
        in_specs=[smem] + [vmem] * 6,
        out_specs=vmem,
        scratch_shapes=[
            pltpu.VMEM((4, members, order), BF),
            pltpu.VMEM((rows, members, LANES), F32),
        ],
        compiler_params=pltpu.CompilerParams(vmem_limit_bytes=8 * MIB),
        name="forcing",
    )(offsets, near, far, sums, packed, meta, cov)

    pieces = [message] + [swap(message, "tile", d) for d in range(1, tiles)]
    early = [swap(piece, "sub", d) for d in range(1, sections) for piece in pieces[1::-1]]
    early, held = lax.optimization_barrier((early, pieces[:1:-1]))
    late = jnp.concatenate(
        [swap(jnp.concatenate(held[::-1]), "sub", d) for d in range(1, sections)]
    )

    all_rows = tiles * rows
    wide = (all_rows, members, LANES)
    flat = (all_rows, 8, LANES)
    room = 4 * all_rows * (members + 8) * LANES

    def prepare(arrays, masks, count):
        height = count * rows
        return pl.pallas_call(
            functools.partial(prepare_kernel, tiles, sizes, masks),
            out_shape=[
                jax.ShapeDtypeStruct((height, size, LANES), F32) for size in (members, 8) * 2
            ],
            in_specs=[vmem] * len(arrays),
            out_specs=[vmem] * 4,
            compiler_params=pltpu.CompilerParams(vmem_limit_bytes=6 * MIB + 2 * room),
            cost_estimate=pl.CostEstimate(
                flops=10**8 * count, bytes_accessed=10**6 * count, transcendentals=0
            ),
            name="prepare",
        )(*arrays)

    own_section = prepare(pieces, tuple(range(tiles)), tiles)
    others = [prepare(early[2 * d : 2 * d + 2], (1, 0), 2) for d in range(sections - 1)]
    early_section = [jnp.concatenate(group) for group in zip(*others)]

    result, keep, give = pl.pallas_call(
        functools.partial(chain_kernel, tiles, sections, sizes),
        out_shape=[jax.ShapeDtypeStruct((blocks, members, half), BF)]
        + [jax.ShapeDtypeStruct((4, members, half), F32)] * 2,
        in_specs=[smem] + [vmem] * 10,
        out_specs=[vmem] * 3,
        scratch_shapes=[
            pltpu.VMEM((all_rows + 2, members, LANES), F32),
            pltpu.VMEM((sections,) + wide, F32),
            pltpu.VMEM((sections,) + flat, F32),
            pltpu.VMEM((sections,) + wide, F32),
            pltpu.VMEM((sections,) + flat, F32),
        ],
        compiler_params=pltpu.CompilerParams(vmem_limit_bytes=6 * MIB + (3 * sections + 3) * room),
        name="chain",
    )(offsets, *early_section, *own_section, late, cov)

    ghost_got = swap(give, "lev")
    ghost = swap_facing((keep + ghost_got).astype(BF))
    kept, given = pl.pallas_call(
        core_kernel,
        out_shape=[jax.ShapeDtypeStruct((blocks, members, half), F32)] * 2,
        in_specs=[smem] + [vmem] * 2,
        out_specs=[vmem] * 2,
        compiler_params=pltpu.CompilerParams(vmem_limit_bytes=4 * MIB),
        cost_estimate=pl.CostEstimate(flops=10**9, bytes_accessed=8 * 10**6, transcendentals=0),
        name="core",
    )(offsets, result, cov)
    got = swap(given, "lev")
    ghost_far = swap(jnp.where(level == 0, ghost[2:], ghost[:2]), "lev")
    out = pl.pallas_call(
        final_kernel,
        out_shape=jax.ShapeDtypeStruct((members * rows, LANES), F32),
        in_specs=[vmem] * 5,
        out_specs=vmem,
        scratch_shapes=[pltpu.VMEM((blocks, members, half), F32)],
        compiler_params=pltpu.CompilerParams(vmem_limit_bytes=4 * MIB),
        name="final",
    )(control_here, kept, got, ghost, ghost_far)
    return out.reshape(1, members, 1, rows, LANES)


def solution(mesh):
    in_specs = (
        P("sub", "grp", "lev", "tile", None),
        P("grp", "lev", "tile", None),
        P("tile", None, "lev", None),
        P("tile", None),
        P("sub", "lev", "tile", None),
        P("sub", "tile", "grp"),
        P("sub", "tile", "grp"),
        P("sub", "tile", None, "grp"),
        P("sub", "tile", "grp"),
    )
    out_specs = P("sub", "grp", "lev", "tile", None)
    return jax.shard_map(body, mesh=mesh, in_specs=in_specs, out_specs=out_specs, check_vma=False)
```
